32 devices in a mesh: pair: 2 (over y), dp: 16 (over z, x, core).
Axes of the slice: x: 2, y: 2, z: 4, core: 2. Of those that a mesh axis runs over, the one named last changes fastest.
Arguments:
- big_images: float32 [64, 3, 1024], P('dp'), may hold values from -3 to 3
- big_noise: float32 [64, 3, 1024], P('dp'), may hold values from -6 to 6
- small_images: float32 [32, 3, 256], P('dp'), may hold values from -3 to 3
- small_noise: float32 [32, 3, 256], P('dp'), may hold values from -6 to 6
- big_level: int32 [64], P('dp'), may hold values from 0 to 9
- small_level: int32 [32], P('dp'), may hold values from 0 to 9
- small_mask: int32 [32, 256], P('dp'), may hold values from 0 to 1
- owner_map: int32 [176], replicated, may hold values from 0 to 191, as said below
- blocks: float32 [192, 128, 128], P(('pair', 'dp')), may hold values from -0.375 to 0.375
- moments: float32 [192, 128, 128], P(('pair', 'dp')), may hold values from -0.0034179688 to 0.0034179688
- left_stats: float32 [192, 128, 128], P(('pair', 'dp')), as said below
- right_stats: float32 [192, 128, 128], P(('pair', 'dp')), as said below
- left_roots: float32 [192, 128, 128], P(('pair', 'dp')), as said below
- right_roots: float32 [192, 128, 128], P(('pair', 'dp')), as said below
- vectors: float32 [74, 256], replicated
- vec_first: float32 [74, 256], replicated, may hold values from -0.0012207031 to 0.0012207031
- vec_second: float32 [74, 256], replicated, as said below
Outputs:
- loss_sum: float32 [], replicated
- grad_norm: float32 [], replicated
- new_blocks: float32 [192, 128, 128], P(('pair', 'dp'))
- new_moments: float32 [192, 128, 128], P(('pair', 'dp'))
- new_left: float32 [192, 128, 128], P(('pair', 'dp'))
- new_right: float32 [192, 128, 128], P(('pair', 'dp'))
- new_vectors: float32 [74, 256], replicated
- new_vec_first: float32 [74, 256], replicated
- new_vec_second: float32 [74, 256], replicated
The draws below stay inside these ranges and needn't reach their ends.
Inputs may be any that keep to these rules, and one draw needn't show every extreme that they name: `owner_map`: distinct slot numbers. `left_stats`: symmetric, positive diagonal. `right_stats`: symmetric, positive diagonal. `left_roots`: symmetric, positive diagonal. `right_roots`: symmetric, positive diagonal. `vec_second`: positive.
All inputs are finite; a program needn't handle non-finite values.
Results may differ from the reference program's by a relative error of at most 0.0053.
Values may be sent and summed in bfloat16 or wider, within the bound.
A program may use at most 320 MiB of HBM per device.

```python
import math
import jax
import jax.numpy as jnp
from jax import lax

CH = 256
GROUPS = 32
BLOCK = 128
SIDE = 32
SMALL_SIDE = 16
SMALL_DEV = 2
NSTEPS = 11
STEP = 10
NV = 74
BIGS = 64
SMALLS = 32
NB = 176
SLOTS = 192
PARAMS = 2902528
N_DP = 16


def symmetric_draw(key, diag_lo, diag_hi, off_scale):
    key_diag, key_off = jax.random.split(key)
    raw = jax.random.normal(key_off, (SLOTS, BLOCK, BLOCK), jnp.float32)
    sym = (raw + jnp.swapaxes(raw, 1, 2)) * (off_scale / 2 ** 0.5)
    diag = diag_lo * (diag_hi / diag_lo) ** jax.random.uniform(key_diag, (SLOTS, BLOCK), jnp.float32)
    eye = jnp.eye(BLOCK, dtype=jnp.float32)
    return sym * (1.0 - eye) + diag[:, :, None] * eye


def draw_small_mask(key, part):
    key = jax.random.fold_in(key, 1)
    device = jnp.arange(SMALLS, dtype=jnp.int32) // SMALL_DEV
    limit = 250 + 500 * device // max(N_DP - 1, 1)
    ticket = jax.random.randint(key, (SMALLS, SMALL_SIDE * SMALL_SIDE), 0, 1000)
    return (ticket < limit[:, None]).astype(jnp.int32)


def draw_owner_map(key, part):
    key = jax.random.fold_in(key, 2)
    return jax.random.permutation(key, SLOTS)[:NB].astype(jnp.int32)


def draw_left_stats(key, part):
    key = jax.random.fold_in(key, 3)
    stat = 0.002 * BLOCK / PARAMS
    return symmetric_draw(key, stat, 4.0 * stat, 0.6 * stat / BLOCK ** 0.5)


def draw_right_stats(key, part):
    key = jax.random.fold_in(key, 4)
    stat = 0.002 * BLOCK / PARAMS
    return symmetric_draw(key, stat, 4.0 * stat, 0.6 * stat / BLOCK ** 0.5)


def draw_left_roots(key, part):
    key = jax.random.fold_in(key, 5)
    return symmetric_draw(key, 0.5, 2.0, 0.6 / BLOCK ** 0.5)


def draw_right_roots(key, part):
    key = jax.random.fold_in(key, 6)
    return symmetric_draw(key, 0.5, 2.0, 0.6 / BLOCK ** 0.5)


def draw_vectors(key, part):
    key = jax.random.fold_in(key, 7)
    normals = jnp.clip(jax.random.normal(key, (NV, CH), jnp.float32), -4.0, 4.0)
    rows = jnp.arange(NV)[:, None]
    scale = jnp.where(rows < 27, 27.0 ** (-0.5), jnp.where(rows >= 47, (9.0 * CH) ** (-0.5), 0.1))
    gains = (rows == 28) | (rows == 34) | (rows == 40) | (rows == 45)
    return jnp.where(gains, 1.0 + 0.1 * normals, scale * normals)


def draw_vec_second(key, part):
    key = jax.random.fold_in(key, 8)
    factor = 4.0 ** jax.random.uniform(key, (NV, CH), jnp.float32)
    return factor * (0.009 / PARAMS)


def with_ends(result, own_key, smallest, largest):
    spot = [jax.random.randint(jax.random.fold_in(own_key, axis), (), 0, length) for axis, length in enumerate(result.shape)]
    main_axis = result.shape.index(max(result.shape))
    next_to = spot[:main_axis] + [(spot[main_axis] + 1) % result.shape[main_axis]] + spot[main_axis + 1:]
    return result.at[tuple(spot)].set(smallest).at[tuple(next_to)].set(largest)


def level_of(key, shape, cuts, smallest, high):
    def one(axis_at, blocks):
        heights = jax.random.uniform(jax.random.fold_in(jax.random.fold_in(key, 6), axis_at), (blocks,), jnp.float32, smallest / len(cuts), high / len(cuts))
        return jnp.repeat(jnp.exp(heights), shape[axis_at] // blocks).reshape((-1,) + (1,) * (len(shape) - axis_at - 1))

    gain = one(*cuts[0])
    for cut in cuts[1:]:
        gain = gain * one(*cut)
    return gain


def scatter_about(stream_key, extent, deviation, reach, cuts=(), kind=jnp.bfloat16):
    entries = jax.random.normal(stream_key, extent, jnp.float32) * deviation
    if len(cuts) > 0:
        entries = level_of(stream_key, extent, cuts, -0.22, 0.18) * entries
    return jnp.clip(entries, min=-reach, max=reach).astype(kind)


def setup_inputs(seed: int = 0) -> dict:
    keys = jax.random.split(jax.random.key(seed), 18)
    return {
        "big_images": scatter_about(keys[0], (BIGS, 3, SIDE * SIDE), 0.5, 3.0, ((0, 16),), jnp.float32),
        "big_noise": scatter_about(keys[1], (BIGS, 3, SIDE * SIDE), 1.0, 6.0, ((0, 16),), jnp.float32),
        "small_images": scatter_about(keys[2], (SMALLS, 3, SMALL_SIDE * SMALL_SIDE), 0.5, 3.0, ((0, 16),), jnp.float32),
        "small_noise": scatter_about(keys[3], (SMALLS, 3, SMALL_SIDE * SMALL_SIDE), 1.0, 6.0, ((0, 16),), jnp.float32),
        "big_level": with_ends(jax.random.randint(keys[4], (BIGS,), 0, NSTEPS - 1), jax.random.fold_in(keys[4], 1), 0, (NSTEPS - 1) - 1).astype(jnp.int32),
        "small_level": with_ends(jax.random.randint(keys[5], (SMALLS,), 0, NSTEPS - 1), jax.random.fold_in(keys[5], 1), 0, (NSTEPS - 1) - 1).astype(jnp.int32),
        "small_mask": draw_small_mask(jax.random.fold_in(keys[17], 71), 0),
        "owner_map": draw_owner_map(jax.random.fold_in(keys[17], 71), 0),
        "blocks": scatter_about(keys[8], (SLOTS, BLOCK, BLOCK), CH ** -0.5, 0.375, ((0, 32),), jnp.float32),
        "moments": scatter_about(keys[9], (SLOTS, BLOCK, BLOCK), PARAMS ** -0.5, 0.0034179688, ((0, 32),), jnp.float32),
        "left_stats": draw_left_stats(jax.random.fold_in(keys[17], 71), 0),
        "right_stats": draw_right_stats(jax.random.fold_in(keys[17], 71), 0),
        "left_roots": draw_left_roots(jax.random.fold_in(keys[17], 71), 0),
        "right_roots": draw_right_roots(jax.random.fold_in(keys[17], 71), 0),
        "vectors": draw_vectors(jax.random.fold_in(keys[17], 71), 0),
        "vec_first": scatter_about(keys[15], (NV, CH), (9 * PARAMS) ** -0.5, 0.0012207031, (), jnp.float32),
        "vec_second": draw_vec_second(jax.random.fold_in(keys[17], 71), 0),
    }


@jax.custom_vjp
def low(v):
    return lax.optimization_barrier(v.astype(jnp.bfloat16)).astype(jnp.float32)

@jax.custom_vjp
def low_back(v):
    return v

def low_keep(v):
    return (low(v), None)

def low_pass(kept, grad):
    return (grad,)

def back_keep(v):
    return (v, None)

def back_low(kept, grad):
    return (low(grad),)
low.defvjp(low_keep, low_pass)
low_back.defvjp(back_keep, back_low)
HIGH = lax.Precision.HIGHEST
SIGMA_DATA = 0.5
SIGMA_MIN = 0.002
SIGMA_MAX = 80.0
RHO = 7.0
HUBER = 0.00054
CLIP = 1.0
BETA_ONE = 0.9
BETA_TWO = 0.999
DECAY = 0.0001
RATE_MATRIX = 0.02
RATE_VECTOR = 0.02
ROOT_HALF = 1.0 / math.sqrt(2.0)

def product_low(left, right):
    return low_back(jnp.dot(low(left), low(right), precision=HIGH))

def sigma_of(levels):
    lowest = SIGMA_MIN ** (1.0 / RHO)
    highest = SIGMA_MAX ** (1.0 / RHO)
    return (lowest + levels.astype(jnp.float32) / (NSTEPS - 1) * (highest - lowest)) ** RHO

def patches(values, side):
    grid = values.reshape(side, side, values.shape[-1])
    padded = jnp.pad(grid, ((1, 1), (1, 1), (0, 0)))
    taps = [padded[offset_y:offset_y + side, offset_x:offset_x + side] for offset_y in range(3) for offset_x in range(3)]
    return jnp.concatenate(taps, axis=-1).reshape(side * side, -1)

def group_norm(values, groups):
    pixels, width = values.shape
    grouped = values.reshape(pixels, groups, width // groups)
    center = grouped - lax.optimization_barrier(jnp.mean(grouped, axis=(0, 2), keepdims=True))
    spread = lax.optimization_barrier(jnp.mean(center * center, axis=(0, 2), keepdims=True))
    return (center * lax.rsqrt(spread + 1e-06)).reshape(pixels, width)

def unpack_blocks(mats, width, block):

    def matrix(start, rows, cols):
        tall, broad = (rows // block, cols // block)
        part = mats[start:start + tall * broad]
        return (part.reshape(tall, broad, block, block).transpose(0, 2, 1, 3).reshape(rows, cols), start + tall * broad)
    offset = 0
    convs = []
    for number in range(4):
        weight, offset = matrix(offset, 9 * width, width)
        convs.append(weight)
    times = []
    for number in range(2):
        weight, offset = matrix(offset, width, 2 * width)
        times.append(weight)
    triple, offset = matrix(offset, width, 3 * width)
    project, offset = matrix(offset, width, width)
    return (convs, times, triple, project)

def network(weights, vectors, noisy, sigma, side):
    convs, times, triple_weight, proj_weight = weights
    width = vectors.shape[1]
    half = width // 2
    freqs = jnp.exp(jnp.arange(half, dtype=jnp.float32) * (math.log(100.0) / (half - 1)))
    phase = jnp.log(sigma) / 4.0 * freqs
    embed = jnp.concatenate([jnp.sin(phase), jnp.cos(phase)])[None, :]
    scale_in = lax.rsqrt(sigma * sigma + SIGMA_DATA ** 2)
    hidden = jnp.dot(patches(noisy * scale_in, side), vectors[0:27], precision=HIGH) + vectors[27]
    for number in range(2):
        base = 28 + 6 * number
        active = jax.nn.silu(group_norm(hidden, GROUPS) * vectors[base] + vectors[base + 1])
        first = product_low(patches(active, side), convs[2 * number]) + vectors[base + 2]
        shifts = product_low(embed, times[number])[0]
        active = jax.nn.silu(group_norm(first, GROUPS) * (1.0 + shifts[:width] + vectors[base + 3]) + shifts[width:] + vectors[base + 4])
        second = product_low(patches(active, side), convs[2 * number + 1]) + vectors[base + 5]
        hidden = (hidden + second) * ROOT_HALF
    normed = group_norm(hidden, GROUPS) * vectors[40] + vectors[41]
    triple = product_low(normed, triple_weight)
    query = triple[:, :width] + vectors[42]
    keyset = triple[:, width:2 * width]
    valueset = triple[:, 2 * width:] + vectors[43]
    scores = product_low(query, keyset.T) * (1.0 / math.sqrt(width))
    probs = jax.nn.softmax(scores, axis=-1)
    mixed = product_low(probs, valueset)
    hidden = (hidden + product_low(mixed, proj_weight) + vectors[44]) * ROOT_HALF
    active = jax.nn.silu(group_norm(hidden, GROUPS) * vectors[45] + vectors[46])
    head = vectors[47:74].reshape(9, 3, width).transpose(0, 2, 1).reshape(9 * width, 3)
    return jnp.dot(patches(active, side), head, precision=HIGH)

def consistency(weights, vectors, clean, noise, sigma, side):
    noisy = (clean + sigma * noise).T
    raw = network(weights, vectors, noisy, sigma, side)
    skip = SIGMA_DATA ** 2 / ((sigma - SIGMA_MIN) ** 2 + SIGMA_DATA ** 2)
    outer = (sigma - SIGMA_MIN) * SIGMA_DATA * lax.rsqrt(SIGMA_DATA ** 2 + sigma * sigma)
    return (skip * noisy + outer * raw).T

def pseudo_huber(student_out, target_out, mask_row, sigma_student, sigma_target):
    diff = student_out - target_out
    total = jnp.sum(mask_row[None, :] * diff * diff)
    bound = HUBER * math.sqrt(3 * diff.shape[1])
    return (jnp.sqrt(total + bound * bound) - bound) / (sigma_student - sigma_target)

def shampoo(grads, master, moments, left_stats, right_stats, left_roots, right_roots):
    first = BETA_ONE * moments + (1 - BETA_ONE) * grads
    left = BETA_TWO * left_stats + (1 - BETA_TWO) * jnp.einsum('sij,skj->sik', grads, grads, precision=HIGH)
    right = BETA_TWO * right_stats + (1 - BETA_TWO) * jnp.einsum('sji,sjk->sik', grads, grads, precision=HIGH)
    turned = jnp.einsum('sij,sjk->sik', left_roots, first, precision=HIGH)
    turned = jnp.einsum('sij,sjk->sik', turned, right_roots, precision=HIGH)
    norm_rms = jnp.sqrt(lax.optimization_barrier(jnp.mean(turned * turned, axis=(1, 2), keepdims=True)) + 1e-20)
    return (master - RATE_MATRIX * (turned / norm_rms + DECAY * master), first, left, right)

def adamw(grads, params, first, second):
    first = BETA_ONE * first + (1 - BETA_ONE) * grads
    second = BETA_TWO * second + (1 - BETA_TWO) * grads * grads
    fixed_first = first / (1 - BETA_ONE ** STEP)
    fixed_second = second / (1 - BETA_TWO ** STEP)
    return (params - RATE_VECTOR * (fixed_first / (jnp.sqrt(fixed_second) + 1e-08) + DECAY * params), first, second)

def reference(big_images, big_noise, small_images, small_noise, big_level, small_level, small_mask, owner_map, blocks, moments, left_stats, right_stats, left_roots, right_roots, vectors, vec_first, vec_second):
    width = vectors.shape[1]
    block = blocks.shape[1]
    rounded = low(blocks[owner_map])
    groups = ((big_images, big_noise, big_level, jnp.ones((big_images.shape[0], SIDE * SIDE), jnp.float32), SIDE), (small_images, small_noise, small_level, small_mask.astype(jnp.float32), SMALL_SIDE))
    fixed_weights = unpack_blocks(rounded, width, block)
    targets = []
    for clean, noise, level, mask, side in groups:

        def target_one(item, side=side):
            return consistency(fixed_weights, vectors, item[0], item[1], item[2], side)
        targets.append(lax.map(target_one, (clean, noise, sigma_of(level))))

    def objective(mats, params):
        weights = unpack_blocks(mats, width, block)
        total = jnp.zeros((), jnp.float32)
        for (clean, noise, level, mask, side), target in zip(groups, targets):

            def student_one(item, side=side):
                output = consistency(weights, params, item[0], item[1], item[2], side)
                return pseudo_huber(output, item[3], item[4], item[2], item[5])
            terms = lax.map(jax.checkpoint(student_one), (clean, noise, sigma_of(level + 1), target, mask, sigma_of(level)))
            total = total + jnp.sum(terms)
        return total
    loss_sum, pull = jax.vjp(objective, rounded, vectors)
    mat_grad, vec_grad = pull(jnp.ones((), jnp.float32))
    grad_norm = jnp.sqrt(jnp.sum(mat_grad * mat_grad) + jnp.sum(vec_grad * vec_grad))
    factor = jnp.minimum(1.0, CLIP / (grad_norm + 1e-06))
    slot_grad = jnp.zeros_like(blocks).at[owner_map].set(mat_grad * factor)
    new_blocks, new_moments, new_left, new_right = shampoo(slot_grad, blocks, moments, left_stats, right_stats, left_roots, right_roots)
    new_vectors, new_first, new_second = adamw(vec_grad * factor, vectors, vec_first, vec_second)
    return (loss_sum, grad_norm, new_blocks, new_moments, new_left, new_right, new_vectors, new_first, new_second)
```

```python
from functools import partial
import math

import jax
import jax.numpy as jnp
from jax import lax
from jax.experimental import pallas as pl
from jax.experimental.pallas import tpu as pltpu
from jax.sharding import PartitionSpec as P

GROUPS = 32
SIDE = 32
SMALL_SIDE = 16
NSTEPS = 11
STEP = 10
CH = 256
BLOCK = 128

HIGH = lax.Precision.HIGHEST
SIGMA_DATA = 0.5
SIGMA_MIN = 0.002
SIGMA_MAX = 80.0
RHO = 7.0
HUBER = 0.00054
CLIP = 1.0
BETA_ONE = 0.9
BETA_TWO = 0.999
DECAY = 0.0001
RATE_MATRIX = 0.02
RATE_VECTOR = 0.02
ROOT_HALF = 1.0 / math.sqrt(2.0)
ANY = pl.ANY
F32 = jnp.float32
BF16 = jnp.bfloat16

CONV_BLOCKS = 36
TIME_FIRST, TIME_COUNT = 144, 8
TRIPLE_FIRST, TRIPLE_COUNT = 160, 12
PROJ_FIRST, PROJ_COUNT = 172, 4

ROWS = 128
MM_ROWS = 256


def mm(left, right):
    return jnp.dot(left, right, preferred_element_type=F32)


def mm_nt(left, right):
    return lax.dot_general(left, right, (((1,), (1,)), ((), ())), preferred_element_type=F32)


def mm_tn(left, right):
    return lax.dot_general(left, right, (((0,), (0,)), ((), ())), preferred_element_type=F32)


def split(value):
    high = value.astype(BF16)
    return high, (value - high.astype(F32)).astype(BF16)


def fold(value):
    return jnp.sum(value.reshape(value.shape[0] // 8, 8, value.shape[1]), axis=0)


def over_rows(value):
    return jnp.sum(value, axis=0, keepdims=True)


def group_sum(value):
    value = jnp.broadcast_to(value, (8, CH))
    lane = lax.broadcasted_iota(jnp.int32, (8, CH), 1)
    for step in (1, 2, 4):
        other = jnp.where(
            (lane & step) != 0, pltpu.roll(value, step, 1), pltpu.roll(value, CH - step, 1)
        )
        value = value + other
    return value[0:1]


def sigmoid(value):
    return 1.0 / (1.0 + jnp.exp(-value))


def group_stats(ref, pixels):
    scale = 1.0 / (8 * pixels)
    total = jnp.zeros((8, CH), F32)
    for row in range(0, pixels, ROWS):
        total = total + fold(ref[row : row + ROWS, :])
    mean = group_sum(over_rows(total)) * scale
    total = jnp.zeros((8, CH), F32)
    for row in range(0, pixels, ROWS):
        center = ref[row : row + ROWS, :] - mean
        total = total + fold(center * center)
    return mean, lax.rsqrt(group_sum(over_rows(total)) * scale + 1e-06)


def write_shifted(ref, row, value, side):
    count = value.shape[0]
    column = lax.broadcasted_iota(jnp.int32, (count, CH), 0) & (side - 1)
    left = jnp.where(column == 0, 0.0, pltpu.roll(value, 1, 0))
    right = jnp.where(column == side - 1, 0.0, pltpu.roll(value, count - 1, 0))
    at = slice(side + row, side + row + count)
    ref[at, 0:CH] = left.astype(BF16)
    ref[at, CH : 2 * CH] = value.astype(BF16)
    ref[at, 2 * CH : 3 * CH] = right.astype(BF16)


def clear_ends(ref, side):
    pixels = side * side
    zeros = jnp.zeros((side, 3 * CH), BF16)
    ref[0:side, :] = zeros
    ref[side + pixels : 2 * side + pixels, :] = zeros


def tap_shifts(side):
    pixels = side * side
    place = lax.broadcasted_iota(jnp.int32, (8, pixels), 1)
    x = place & (side - 1)
    y = place >> (side.bit_length() - 1)
    taps = []
    for dy in (-1, 0, 1):
        for dx in (-1, 0, 1):
            inside = (x + dx >= 0) & (x + dx < side) & (y + dy >= 0) & (y + dy < side)
            taps.append((dy * side + dx, inside))
    return taps


def net_kernel(
    owner_ref,
    scal_ref,
    emb_ref,
    big_ref,
    big_noise_ref,
    small_ref,
    small_noise_ref,
    mask_ref,
    vec_ref,
    vin_ref,
    head_ref,
    whole_ref,
    grads_ref,
    gvec_ref,
    gin_ref,
    ghead_ref,
    loss_ref,
    conv_w,
    time_w,
    triple_w,
    proj_w,
    conv_g,
    time_g,
    triple_g,
    proj_g,
    stage,
    hid_t,
    hid_s,
    first_t,
    first_s,
    pat_t,
    pat_s,
    gpat,
    grad_t,
    probs,
    keep,
    keep_t,
    normed,
    mixed,
    act_hi,
    act_lo,
    dhid,
    dact,
    dtri,
    tsh,
    gtime,
    x80,
    sem,
):
    bigs = big_ref.shape[0]
    smalls = small_ref.shape[0]
    count = bigs + smalls

    def block_copy(index, target):
        return pltpu.make_async_copy(whole_ref.at[owner_ref[index]], target, sem)

    def conv_target(array, index):
        m = index // CONV_BLOCKS
        rest = index - m * CONV_BLOCKS
        i = rest // 2
        j = rest - i * 2
        return array.at[m, pl.ds(pl.multiple_of(i * BLOCK, BLOCK), BLOCK), pl.ds(pl.multiple_of(j * BLOCK, BLOCK), BLOCK)]

    def load_conv(index, _):
        block_copy(index, conv_target(conv_w, index)).start()
        return _

    lax.fori_loop(0, 4 * CONV_BLOCKS, load_conv, 0)
    others = []
    for number in range(2):
        for k in range(TIME_COUNT):
            i, j = k // 4, k % 4
            others.append((TIME_FIRST + TIME_COUNT * number + k, time_w.at[number, i * BLOCK : (i + 1) * BLOCK, j * BLOCK : (j + 1) * BLOCK]))
    for k in range(TRIPLE_COUNT):
        i, j = k // 6, k % 6
        others.append((TRIPLE_FIRST + k, triple_w.at[i * BLOCK : (i + 1) * BLOCK, j * BLOCK : (j + 1) * BLOCK]))
    for k in range(PROJ_COUNT):
        i, j = k // 2, k % 2
        others.append((PROJ_FIRST + k, proj_w.at[i * BLOCK : (i + 1) * BLOCK, j * BLOCK : (j + 1) * BLOCK]))
    for index, target in others:
        block_copy(index, target).start()

    conv_g[...] = jnp.zeros_like(conv_g)
    triple_g[...] = jnp.zeros_like(triple_g)
    proj_g[...] = jnp.zeros_like(proj_g)
    gvec_ref[...] = jnp.zeros_like(gvec_ref)
    gin_ref[...] = jnp.zeros_like(gin_ref)
    ghead_ref[...] = jnp.zeros_like(ghead_ref)
    loss_ref[...] = jnp.zeros_like(loss_ref)
    gtime[...] = jnp.zeros_like(gtime)

    vin_hi, vin_lo = split(vin_ref[...])
    vin3 = jnp.concatenate([vin_hi, vin_lo, vin_hi], axis=0)
    head_hi, head_lo = split(head_ref[...])
    head2 = jnp.concatenate([head_hi, head_lo], axis=0)
    head3 = jnp.concatenate([head_hi, head_lo, head_hi], axis=0)

    def wait_conv(index, _):
        block_copy(0, conv_target(conv_w, index)).wait()
        return _

    lax.fori_loop(0, 4 * CONV_BLOCKS, wait_conv, 0)
    for index, target in others:
        block_copy(index, target).wait()

    for number in range(2):
        tsh[number] = mm(emb_ref[...], time_w[number])

    def vec(row):
        return vec_ref[row : row + 1, :]

    def add_vec(row, value):
        gvec_ref[row : row + 1, :] += value

    def run(image, clean_ref, noise_ref, local, side, small):
        pixels = side * side
        taps = tap_shifts(side)

        def scal(which, item):
            return scal_ref[image * 16 + which * 4 + item]

        def chunks(step=ROWS):
            return range(0, pixels, min(step, pixels))

        rows = min(ROWS, pixels)
        mrows = min(MM_ROWS, pixels)

        clear_ends(pat_t, side)
        for k in range(4):
            clear_ends(pat_s.at[k], side)
        clear_ends(gpat, side)

        noisies = []
        for which in range(2):
            noisies.append(clean_ref[local] + scal(which, 0) * noise_ref[local])

        def shifted_input(which):
            scaled = noisies[which] * scal(which, 1)
            parts = []
            for shift, inside in taps:
                parts.append(jnp.where(inside, pltpu.roll(scaled, (-shift) % pixels, 1), 0.0))
            first = lax.broadcasted_iota(jnp.int32, (8, pixels), 0) == 0
            parts.append(jnp.where(first, 1.0, 0.0))
            return jnp.concatenate(parts, axis=0)

        def hid(which, level):
            return hid_t if which == 0 else hid_s.at[level]

        def pat(which, level):
            return pat_t if which == 0 else pat_s.at[level]

        def first(which, level):
            return first_t if which == 0 else first_s.at[level]

        for which in range(2):
            value = shifted_input(which)
            high, low = split(value)
            if which == 1:
                x80[0:80, 0:pixels] = high
                x80[80:160, 0:pixels] = low
            three = jnp.concatenate([high, high, low], axis=0)
            hid(which, 0)[0:pixels, :] = mm_tn(three, vin3)

        def shifts(which, number):
            row = tsh[number, pl.ds(2 * image + which, 1), :]
            return row[:, 0:CH], row[:, CH:]

        stats = {}

        def act(which, key, src, gain, bias, dst):
            mean, rstd = group_stats(src, pixels)
            if which == 1:
                stats[key] = (mean, rstd)
            scale = rstd * gain
            for row in chunks():
                z = (src[row : row + rows, :] - mean) * scale + bias
                write_shifted(dst, row, z * sigmoid(z), side)

        def conv(src, number, row):
            total = None
            for dy in range(3):
                part = mm(src[dy * side + row : dy * side + row + mrows, :], conv_w[number, dy * 768 : (dy + 1) * 768, :])
                total = part if total is None else total + part
            return total

        for number in range(2):
            base = 28 + 6 * number
            for which in range(2):
                act(which, ("a", number), hid(which, number), vec(base), vec(base + 1), pat(which, 2 * number))
            for which in range(2):
                for row in chunks(MM_ROWS):
                    first(which, number)[row : row + mrows, :] = conv(pat(which, 2 * number), 2 * number, row) + vec(base + 2)
            for which in range(2):
                gain_t, bias_t = shifts(which, number)
                act(
                    which,
                    ("b", number),
                    first(which, number),
                    1.0 + gain_t + vec(base + 3),
                    bias_t + vec(base + 4),
                    pat(which, 2 * number + 1),
                )
            for which in range(2):
                for row in chunks(MM_ROWS):
                    second = conv(pat(which, 2 * number + 1), 2 * number + 1, row) + vec(base + 5)
                    at = slice(row, row + mrows)
                    hid(which, number + 1)[at, :] = (hid(which, number)[at, :] + second) * ROOT_HALF

        results = []
        for which in range(2):
            src = hid(which, 2)
            mean, rstd = group_stats(src, pixels)
            if which == 1:
                stats["n"] = (mean, rstd)
            scale = rstd * vec(40)
            for row in chunks():
                value = (src[row : row + rows, :] - mean) * scale + vec(41)
                normed[row : row + rows, :] = value.astype(BF16)
            for row in chunks(MM_ROWS):
                at = slice(row, row + mrows)
                triple = mm(normed[at, :], triple_w[...])
                keep[0, at, :] = (triple[:, 0:CH] + vec(42)).astype(BF16)
                key = triple[:, CH : 2 * CH]
                value = triple[:, 2 * CH :] + vec(43)
                keep[1, at, :] = key.astype(BF16)
                keep[2, at, :] = value.astype(BF16)
                keep_t[0, :, at] = jnp.transpose(value).astype(BF16)
                if which == 1:
                    keep_t[1, :, at] = jnp.transpose(key).astype(BF16)
            for col in chunks(MM_ROWS):
                at = slice(col, col + mrows)
                scores = mm_nt(keep[1, 0:pixels, :], keep[0, at, :]) * (1.0 / math.sqrt(CH))
                top = jnp.max(scores, axis=0, keepdims=True)
                weight = jnp.exp(scores - top)
                weight = weight * (1.0 / jnp.sum(weight, axis=0, keepdims=True))
                if which == 1:
                    probs[0:pixels, at] = weight
                out_t = mm(keep_t[0, :, 0:pixels], weight.astype(BF16))
                mixed[at, :] = jnp.transpose(out_t).astype(BF16)
            for row in chunks(MM_ROWS):
                at = slice(row, row + mrows)
                value = mm(mixed[at, :], proj_w[...]) + vec(44)
                hid(which, 3)[at, :] = (hid(which, 2)[at, :] + value) * ROOT_HALF
            src = hid(which, 3)
            mean, rstd = group_stats(src, pixels)
            if which == 1:
                stats["h"] = (mean, rstd)
            scale = rstd * vec(45)
            for row in chunks():
                z = (src[row : row + rows, :] - mean) * scale + vec(46)
                high, low = split(z * sigmoid(z))
                act_hi[row : row + rows, :] = high
                act_lo[row : row + rows, :] = low
            wide = mm_nt(head2, act_hi[0:pixels, :])
            wide = wide[0:80] + wide[80:160] + mm_nt(head_hi, act_lo[0:pixels, :])
            out = jnp.zeros((8, pixels), F32)
            for k, (shift, inside) in enumerate(taps):
                out = out + jnp.where(inside, pltpu.roll(wide[8 * k : 8 * k + 8], (-shift) % pixels, 1), 0.0)
            results.append(scal(which, 2) * noisies[which] + scal(which, 3) * out)

        diff = results[1] - results[0]
        weighted = diff * mask_ref[local] if small else diff
        bound = HUBER * math.sqrt(3 * pixels)
        total = jnp.sum(jnp.sum(weighted * diff, axis=1, keepdims=True), axis=0, keepdims=True)
        root = jnp.sqrt(total + bound * bound)
        rate = scal(2, 0)
        loss_ref[...] += jnp.broadcast_to((root - bound) * rate, (8, 128))
        dout = weighted * ((rate * scal(1, 3)) / root)

        parts = []
        for shift, inside in taps:
            parts.append(pltpu.roll(jnp.where(inside, dout, 0.0), shift % pixels, 1))
        parts.append(jnp.zeros((8, pixels), F32))
        high, low = split(jnp.concatenate(parts, axis=0))
        two = jnp.concatenate([high, low], axis=0)
        three = jnp.concatenate([high, high, low], axis=0)
        wide = mm(two, act_hi[0:pixels, :])
        ghead_ref[...] += wide[0:80] + wide[80:160] + mm(high, act_lo[0:pixels, :])
        dact[0:pixels, :] = mm_tn(three, head3)

        scale8 = 1.0 / (8 * pixels)

        def act_back(key, src, gain, bias, active):
            mean, rstd = stats[key]
            sum_b = jnp.zeros((8, CH), F32)
            sum_g = jnp.zeros((8, CH), F32)
            for row in chunks():
                at = slice(row, row + rows)
                value = (src[at, :] - mean) * rstd
                grad = dact[at, :]
                if active:
                    z = value * gain + bias
                    sig = sigmoid(z)
                    grad = grad * (sig * (1.0 + z * (1.0 - sig)))
                    dact[at, :] = grad
                sum_b = sum_b + fold(grad)
                sum_g = sum_g + fold(grad * value)
            sum_b = over_rows(sum_b)
            sum_g = over_rows(sum_g)
            mean_b = group_sum(sum_b * gain) * scale8
            mean_g = group_sum(sum_g * gain) * scale8

            def final(row):
                at = slice(row, row + rows)
                value = (src[at, :] - mean) * rstd
                return rstd * (gain * dact[at, :] - mean_b - value * mean_g)

            return sum_b, sum_g, final

        sum_b, sum_g, final = act_back("h", hid_s.at[3], vec(45), vec(46), True)
        add_vec(45, sum_g)
        add_vec(46, sum_b)
        total = jnp.zeros((8, CH), F32)
        for row in chunks():
            at = slice(row, row + rows)
            grad = final(row) * ROOT_HALF
            dhid[at, :] = grad
            total = total + fold(grad)
            low = grad.astype(BF16)
            normed_g = low
            gpat[row : row + rows, 0:CH] = normed_g
            grad_t[0, :, at] = jnp.transpose(grad).astype(BF16)
        add_vec(44, over_rows(total))
        proj_g[...] += mm(grad_t[0, :, 0:pixels], mixed[0:pixels, :])
        for row in chunks(MM_ROWS):
            at = slice(row, row + mrows)
            gpat[at, CH : 2 * CH] = mm_nt(gpat[at, 0:CH], proj_w[...]).astype(BF16)
        total = jnp.zeros((8, CH), F32)
        for col in chunks(MM_ROWS):
            at = slice(col, col + mrows)
            grad = mm_nt(keep[2, 0:pixels, :], gpat[at, CH : 2 * CH])
            weight = probs[0:pixels, at]
            inner = jnp.sum(weight * grad, axis=0, keepdims=True)
            probs_g = (weight * (grad - inner) * (1.0 / math.sqrt(CH))).astype(BF16)
            stage[0:pixels, at] = probs_g
            stage[0:pixels, 1024 + col : 1024 + col + mrows] = weight.astype(BF16)
            dq_t = mm(keep_t[1, :, 0:pixels], probs_g)
            dtri[at, 0:CH] = jnp.transpose(dq_t).astype(BF16)
            grad_t[0, :, at] = dq_t.astype(BF16)
            total = total + fold(jnp.transpose(dq_t))
        add_vec(42, over_rows(total))
        total = jnp.zeros((8, CH), F32)
        for row in chunks(MM_ROWS):
            at = slice(row, row + mrows)
            dk = mm(stage[at, 0:pixels], keep[0, 0:pixels, :])
            dv = mm(stage[at, 1024 : 1024 + pixels], gpat[0:pixels, CH : 2 * CH])
            total = total + fold(dv)
            dtri[at, CH : 2 * CH] = dk.astype(BF16)
            dtri[at, 2 * CH :] = dv.astype(BF16)
            grad_t[1, :, at] = jnp.transpose(dk).astype(BF16)
            grad_t[2, :, at] = jnp.transpose(dv).astype(BF16)
        add_vec(43, over_rows(total))
        for part in range(3):
            triple_g[part * CH : (part + 1) * CH, :] += mm(grad_t[part, :, 0:pixels], normed[0:pixels, :])
        for row in chunks(MM_ROWS):
            at = slice(row, row + mrows)
            dact[at, :] = mm_nt(dtri[at, :], triple_w[...])
        clear_ends(gpat, side)
        sum_b, sum_g, final = act_back("n", hid_s.at[2], vec(40), vec(41), False)
        add_vec(40, sum_g)
        add_vec(41, sum_b)
        for row in chunks():
            at = slice(row, row + rows)
            dhid[at, :] += final(row)

        def conv_back(number):
            for dy in range(3):
                conv_g[number, :, dy * 768 : (dy + 1) * 768] += mm(
                    grad_t[0, :, 0:pixels], pat_s[number, dy * side : dy * side + pixels, :]
                )
            for row in chunks(MM_ROWS):
                total = None
                for dy in range(3):
                    for dx in range(3):
                        tap = dy * 3 + dx
                        start = (2 - dy) * side + row
                        part = mm_nt(
                            gpat[start : start + mrows, (2 - dx) * CH : (3 - dx) * CH],
                            conv_w[number, tap * CH : (tap + 1) * CH, :],
                        )
                        total = part if total is None else total + part
                dact[row : row + mrows, :] = total

        for number in (1, 0):
            base = 28 + 6 * number
            total = jnp.zeros((8, CH), F32)
            for row in chunks():
                at = slice(row, row + rows)
                grad = dhid[at, :] * ROOT_HALF
                dhid[at, :] = grad
                total = total + fold(grad)
                write_shifted(gpat, row, grad, side)
                grad_t[0, :, at] = jnp.transpose(grad).astype(BF16)
            add_vec(base + 5, over_rows(total))
            conv_back(2 * number + 1)
            gain_t, bias_t = shifts(1, number)
            sum_b, sum_g, final = act_back(
                ("b", number),
                first_s.at[number],
                1.0 + gain_t + vec(base + 3),
                bias_t + vec(base + 4),
                True,
            )
            add_vec(base + 3, sum_g)
            add_vec(base + 4, sum_b)
            gtime[number, pl.ds(image, 1), 0:CH] = sum_g
            gtime[number, pl.ds(image, 1), CH:] = sum_b
            total = jnp.zeros((8, CH), F32)
            for row in chunks():
                at = slice(row, row + rows)
                grad = final(row)
                total = total + fold(grad)
                write_shifted(gpat, row, grad, side)
                grad_t[0, :, at] = jnp.transpose(grad).astype(BF16)
            add_vec(base + 2, over_rows(total))
            conv_back(2 * number)
            sum_b, sum_g, final = act_back(("a", number), hid_s.at[number], vec(base), vec(base + 1), True)
            add_vec(base, sum_g)
            add_vec(base + 1, sum_b)
            for row in chunks():
                at = slice(row, row + rows)
                dhid[at, :] += final(row)

        high, low = split(dhid[0:pixels, :])
        wide = mm(x80[:, 0:pixels], high)
        gin_ref[...] += wide[0:80] + wide[80:160] + mm(x80[0:80, 0:pixels], low)

    def big_image(index, carry):
        run(index, big_ref, big_noise_ref, index, SIDE, False)
        return carry

    lax.fori_loop(0, bigs, big_image, 0)

    def small_image(index, carry):
        run(bigs + index, small_ref, small_noise_ref, index, SMALL_SIDE, True)
        return carry

    lax.fori_loop(0, smalls, small_image, 0)

    emb = emb_ref[...].astype(F32)
    mine = jnp.concatenate(
        [emb[2 * k + 1 : 2 * k + 2] for k in range(count)] + [jnp.zeros((gtime.shape[1] - count, CH), F32)], axis=0
    ).astype(BF16)
    for number in range(2):
        time_g[number] = mm_tn(gtime[number].astype(BF16), mine)

    def out_copy(source, index):
        return pltpu.make_async_copy(source, grads_ref.at[owner_ref[index]], sem)

    for m in range(4):
        for j in range(2):
            part = slice(j * BLOCK, (j + 1) * BLOCK)
            for i in range(18):
                conv_w[m, i * BLOCK : (i + 1) * BLOCK, part] = conv_g[m, part, i * BLOCK : (i + 1) * BLOCK].astype(BF16)
    for number in range(2):
        for k in range(TIME_COUNT):
            i, j = k // 4, k % 4
            time_w[number, i * BLOCK : (i + 1) * BLOCK, j * BLOCK : (j + 1) * BLOCK] = time_g[
                number, j * BLOCK : (j + 1) * BLOCK, i * BLOCK : (i + 1) * BLOCK
            ].astype(BF16)
    for k in range(TRIPLE_COUNT):
        i, j = k // 6, k % 6
        triple_w[i * BLOCK : (i + 1) * BLOCK, j * BLOCK : (j + 1) * BLOCK] = triple_g[
            j * BLOCK : (j + 1) * BLOCK, i * BLOCK : (i + 1) * BLOCK
        ].astype(BF16)
    for k in range(PROJ_COUNT):
        i, j = k // 2, k % 2
        proj_w[i * BLOCK : (i + 1) * BLOCK, j * BLOCK : (j + 1) * BLOCK] = proj_g[
            j * BLOCK : (j + 1) * BLOCK, i * BLOCK : (i + 1) * BLOCK
        ].astype(BF16)

    def store_conv(index, carry):
        out_copy(conv_target(conv_w, index), index).start()
        return carry

    lax.fori_loop(0, 4 * CONV_BLOCKS, store_conv, 0)
    for index, target in others:
        out_copy(target, index).start()

    def wait_store(index, carry):
        out_copy(conv_target(conv_w, index), 0).wait()
        return carry

    lax.fori_loop(0, 4 * CONV_BLOCKS, wait_store, 0)
    for index, target in others:
        out_copy(target, index).wait()


def network_grads(owner_map, scalars, embed, big, big_noise, small, small_noise, mask, vectors, vin, head, whole):
    nb = owner_map.shape[0]
    slots = whole.shape[0]
    vmem = pl.BlockSpec(memory_space=pltpu.VMEM)
    smem = pl.BlockSpec(memory_space=pltpu.SMEM)
    hbm = pl.BlockSpec(memory_space=ANY)
    big_px = SIDE * SIDE
    tall = (SIDE + 2) * SIDE
    return pl.pallas_call(
        net_kernel,
        out_shape=(
            jax.ShapeDtypeStruct((slots, BLOCK, BLOCK), BF16),
            jax.ShapeDtypeStruct((80, CH), F32),
            jax.ShapeDtypeStruct((80, CH), F32),
            jax.ShapeDtypeStruct((80, CH), F32),
            jax.ShapeDtypeStruct((8, 128), F32),
        ),
        in_specs=[smem, smem] + [vmem] * 9 + [hbm],
        out_specs=(hbm, vmem, vmem, vmem, vmem),
        scratch_shapes=[
            pltpu.VMEM((4, 9 * CH, CH), BF16),
            pltpu.VMEM((2, CH, 2 * CH), BF16),
            pltpu.VMEM((CH, 3 * CH), BF16),
            pltpu.VMEM((CH, CH), BF16),
            pltpu.VMEM((4, CH, 9 * CH), F32),
            pltpu.VMEM((2, 2 * CH, CH), F32),
            pltpu.VMEM((3 * CH, CH), F32),
            pltpu.VMEM((CH, CH), F32),
            pltpu.VMEM((big_px, 2 * big_px), BF16),
            pltpu.VMEM((big_px, CH), F32),
            pltpu.VMEM((4, big_px, CH), F32),
            pltpu.VMEM((big_px, CH), F32),
            pltpu.VMEM((2, big_px, CH), F32),
            pltpu.VMEM((tall, 3 * CH), BF16),
            pltpu.VMEM((4, tall, 3 * CH), BF16),
            pltpu.VMEM((tall, 3 * CH), BF16),
            pltpu.VMEM((3, CH, big_px), BF16),
            pltpu.VMEM((big_px, big_px), F32),
            pltpu.VMEM((3, big_px, CH), BF16),
            pltpu.VMEM((2, CH, big_px), BF16),
            pltpu.VMEM((big_px, CH), BF16),
            pltpu.VMEM((big_px, CH), BF16),
            pltpu.VMEM((big_px, CH), BF16),
            pltpu.VMEM((big_px, CH), BF16),
            pltpu.VMEM((big_px, CH), F32),
            pltpu.VMEM((big_px, CH), F32),
            pltpu.VMEM((big_px, 3 * CH), BF16),
            pltpu.VMEM((2, embed.shape[0], 2 * CH), F32),
            pltpu.VMEM((2, 16, 2 * CH), F32),
            pltpu.VMEM((160, big_px), BF16),
            pltpu.SemaphoreType.DMA,
        ],
        compiler_params=pltpu.CompilerParams(vmem_limit_bytes=60 * 1024 * 1024),
        cost_estimate=pl.CostEstimate(flops=57 * 10**9, bytes_accessed=20 * 10**6, transcendentals=10**7),
    )(owner_map, scalars, embed, big, big_noise, small, small_noise, mask, vectors, vin, head, whole)


def sigma_of(levels):
    lowest = SIGMA_MIN ** (1.0 / RHO)
    highest = SIGMA_MAX ** (1.0 / RHO)
    return (lowest + levels.astype(F32) / (NSTEPS - 1) * (highest - lowest)) ** RHO


def shampoo(grads, master, moments, left_stats, right_stats, left_roots, right_roots):
    first = BETA_ONE * moments + (1 - BETA_ONE) * jnp.swapaxes(grads, 1, 2)
    left = BETA_TWO * left_stats + (1 - BETA_TWO) * jnp.einsum(
        "sji,sjk->sik", grads, grads, precision=HIGH
    )
    right = BETA_TWO * right_stats + (1 - BETA_TWO) * jnp.einsum(
        "sij,skj->sik", grads, grads, precision=HIGH
    )
    turned = jnp.einsum("sij,sjk->sik", left_roots, first, precision=HIGH)
    turned = jnp.einsum("sij,sjk->sik", turned, right_roots, precision=HIGH)
    norm_rms = jnp.sqrt(jnp.mean(turned * turned, axis=(1, 2), keepdims=True) + 1e-20)
    return (master - RATE_MATRIX * (turned / norm_rms + DECAY * master), first, left, right)


def adamw(grads, params, first, second):
    first = BETA_ONE * first + (1 - BETA_ONE) * grads
    second = BETA_TWO * second + (1 - BETA_TWO) * grads * grads
    fixed_first = first / (1 - BETA_ONE**STEP)
    fixed_second = second / (1 - BETA_TWO**STEP)
    return (
        params - RATE_VECTOR * (fixed_first / (jnp.sqrt(fixed_second) + 1e-08) + DECAY * params),
        first,
        second,
    )


def prepare(big_images, big_noise, small_images, small_noise, big_level, small_level, small_mask, vectors, pair_index):
    def half(values):
        count = values.shape[0] // 2
        return lax.dynamic_slice_in_dim(values, pair_index * count, count, 0)

    def rows8(values):
        return jnp.pad(values, ((0, 0), (0, 5), (0, 0)))

    levels = jnp.concatenate([half(big_level), half(small_level)])
    count = levels.shape[0]
    sigma = sigma_of(levels[:, None] + jnp.arange(2)[None, :])
    scale_in = lax.rsqrt(sigma * sigma + SIGMA_DATA**2)
    skip = SIGMA_DATA**2 / ((sigma - SIGMA_MIN) ** 2 + SIGMA_DATA**2)
    outer = (sigma - SIGMA_MIN) * SIGMA_DATA * lax.rsqrt(SIGMA_DATA**2 + sigma * sigma)
    rate = 1.0 / (sigma[:, 1] - sigma[:, 0])
    per_pass = jnp.stack([sigma, scale_in, skip, outer], axis=-1).reshape(count, 8)
    scalars = jnp.concatenate([per_pass, jnp.pad(rate[:, None], ((0, 0), (0, 7)))], axis=1).reshape(-1)
    half_ch = CH // 2
    freqs = jnp.exp(jnp.arange(half_ch, dtype=F32) * (math.log(100.0) / (half_ch - 1)))
    phase = (jnp.log(sigma) / 4.0).reshape(-1, 1) * freqs
    embed = jnp.concatenate([jnp.sin(phase), jnp.cos(phase)], axis=-1)
    embed = jnp.pad(embed, ((0, -embed.shape[0] % 16), (0, 0))).astype(BF16)
    vin = jnp.pad(vectors[0:27].reshape(9, 3, CH), ((0, 0), (0, 5), (0, 0))).reshape(72, CH)
    vin = jnp.concatenate([vin, vectors[27:28], jnp.zeros((7, CH), F32)], axis=0)
    head = jnp.pad(vectors[47:74].reshape(9, 3, CH), ((0, 0), (0, 5), (0, 0))).reshape(72, CH)
    head = jnp.pad(head, ((0, 8), (0, 0)))
    mask = jnp.broadcast_to(half(small_mask).astype(F32)[:, None, :], (small_mask.shape[0] // 2, 8, small_mask.shape[1]))
    return (
        scalars,
        embed,
        rows8(half(big_images)),
        rows8(half(big_noise)),
        rows8(half(small_images)),
        rows8(half(small_noise)),
        mask,
        jnp.pad(vectors, ((0, 6), (0, 0))),
        vin,
        head,
    )


def local(
    big_images,
    big_noise,
    small_images,
    small_noise,
    big_level,
    small_level,
    small_mask,
    owner_map,
    blocks,
    moments,
    left_stats,
    right_stats,
    left_roots,
    right_roots,
    vectors,
    vec_first,
    vec_second,
):
    slot_count = blocks.shape[0]
    whole = lax.all_gather(blocks.astype(BF16), ("pair", "dp"), axis=0, tiled=True)
    ready = prepare(
        big_images, big_noise, small_images, small_noise, big_level, small_level, small_mask, vectors, lax.axis_index("pair")
    )
    grads, gvec, gin, ghead, loss = network_grads(owner_map, *ready, whole)
    summed = lax.psum_scatter(grads.reshape(grads.shape[0], -1), ("pair", "dp"), scatter_dimension=0, tiled=True)
    slot_ids = lax.axis_index(("pair", "dp")) * slot_count + jnp.arange(slot_count, dtype=jnp.int32)
    owned = jnp.any(slot_ids[:, None] == owner_map[None, :], axis=1)
    mine = jnp.where(owned[:, None], summed.astype(F32), 0.0)
    vec_part = jnp.concatenate(
        [
            gin[0:72].reshape(9, 8, CH)[:, 0:3].reshape(27, CH),
            gin[72:73],
            gvec[28:47],
            ghead[0:72].reshape(9, 8, CH)[:, 0:3].reshape(27, CH),
        ],
        axis=0,
    )
    vec_total, loss_total, square = lax.psum((vec_part, loss[0, 0], jnp.sum(mine * mine)), ("pair", "dp"))
    grad_norm = jnp.sqrt(square + jnp.sum(vec_total * vec_total))
    factor = jnp.minimum(1.0, CLIP / (grad_norm + 1e-06))
    slot_grad = mine.reshape(blocks.shape) * factor
    new_blocks, new_moments, new_left, new_right = shampoo(
        slot_grad, blocks, moments, left_stats, right_stats, left_roots, right_roots
    )
    new_vectors, new_first, new_second = adamw(vec_total * factor, vectors, vec_first, vec_second)
    return (
        loss_total,
        grad_norm,
        new_blocks,
        new_moments,
        new_left,
        new_right,
        new_vectors,
        new_first,
        new_second,
    )


def solution(mesh):
    by_slot = P(("pair", "dp"), None, None)
    by_image = P("dp", None, None)
    placed = (by_image,) * 4 + (P("dp"), P("dp"), P("dp", None), P()) + (by_slot,) * 6 + (P(),) * 3
    return jax.shard_map(
        local,
        mesh=mesh,
        in_specs=placed,
        out_specs=(P(), P()) + (by_slot,) * 4 + (P(),) * 3,
        check_vma=False,
    )
```

```python
from functools import partial
import math

import jax
import jax.numpy as jnp
from jax import lax
from jax.experimental import pallas as pl
from jax.experimental.pallas import tpu as pltpu
from jax.sharding import PartitionSpec as P

GROUPS = 32
SIDE = 32
SMALL_SIDE = 16
NSTEPS = 11
STEP = 10
CH = 256
BLOCK = 128

HIGH = lax.Precision.HIGHEST
SIGMA_DATA = 0.5
SIGMA_MIN = 0.002
SIGMA_MAX = 80.0
RHO = 7.0
HUBER = 0.00054
CLIP = 1.0
BETA_ONE = 0.9
BETA_TWO = 0.999
DECAY = 0.0001
RATE_MATRIX = 0.02
RATE_VECTOR = 0.02
ROOT_HALF = 1.0 / math.sqrt(2.0)
ANY = pl.ANY
F32 = jnp.float32
BF16 = jnp.bfloat16

CONV_BLOCKS = 36
TIME_FIRST, TIME_COUNT = 144, 8
TRIPLE_FIRST, TRIPLE_COUNT = 160, 12
PROJ_FIRST, PROJ_COUNT = 172, 4

ROWS = 128
MM_ROWS = 256


def mm(left, right):
    return jnp.dot(left, right, preferred_element_type=F32)


def mm_nt(left, right):
    return lax.dot_general(left, right, (((1,), (1,)), ((), ())), preferred_element_type=F32)


def mm_tn(left, right):
    return lax.dot_general(left, right, (((0,), (0,)), ((), ())), preferred_element_type=F32)


def split(value):
    high = value.astype(BF16)
    return high, (value - high.astype(F32)).astype(BF16)


def fold(value):
    return jnp.sum(value.reshape(value.shape[0] // 8, 8, value.shape[1]), axis=0)


def over_rows(value):
    return jnp.sum(value, axis=0, keepdims=True)


def group_sum(value):
    value = jnp.broadcast_to(value, (8, CH))
    lane = lax.broadcasted_iota(jnp.int32, (8, CH), 1)
    for step in (1, 2, 4):
        other = jnp.where(
            (lane & step) != 0, pltpu.roll(value, step, 1), pltpu.roll(value, CH - step, 1)
        )
        value = value + other
    return value[0:1]


def sigmoid(value):
    return 1.0 / (1.0 + jnp.exp(-value))


def group_stats(ref, pixels):
    scale = 1.0 / (8 * pixels)
    total = jnp.zeros((8, CH), F32)
    for row in range(0, pixels, ROWS):
        total = total + fold(ref[row : row + ROWS, :])
    mean = group_sum(over_rows(total)) * scale
    total = jnp.zeros((8, CH), F32)
    for row in range(0, pixels, ROWS):
        center = ref[row : row + ROWS, :] - mean
        total = total + fold(center * center)
    return mean, lax.rsqrt(group_sum(over_rows(total)) * scale + 1e-06)


def write_shifted(ref, row, value, side):
    count = value.shape[0]
    column = lax.broadcasted_iota(jnp.int32, (count, CH), 0) & (side - 1)
    left = jnp.where(column == 0, 0.0, pltpu.roll(value, 1, 0))
    right = jnp.where(column == side - 1, 0.0, pltpu.roll(value, count - 1, 0))
    at = slice(side + row, side + row + count)
    ref[at, 0:CH] = left.astype(BF16)
    ref[at, CH : 2 * CH] = value.astype(BF16)
    ref[at, 2 * CH : 3 * CH] = right.astype(BF16)


def clear_ends(ref, side):
    pixels = side * side
    zeros = jnp.zeros((side, 3 * CH), BF16)
    ref[0:side, :] = zeros
    ref[side + pixels : 2 * side + pixels, :] = zeros


def tap_shifts(side):
    pixels = side * side
    place = lax.broadcasted_iota(jnp.int32, (8, pixels), 1)
    x = place & (side - 1)
    y = place >> (side.bit_length() - 1)
    taps = []
    for dy in (-1, 0, 1):
        for dx in (-1, 0, 1):
            inside = (x + dx >= 0) & (x + dx < side) & (y + dy >= 0) & (y + dy < side)
            taps.append((dy * side + dx, inside))
    return taps


def net_kernel(
    owner_ref,
    scal_ref,
    emb_ref,
    big_ref,
    big_noise_ref,
    small_ref,
    small_noise_ref,
    mask_ref,
    vec_ref,
    vin_ref,
    head_ref,
    whole_ref,
    grads_ref,
    gvec_ref,
    conv_w,
    time_w,
    triple_w,
    proj_w,
    conv_g,
    time_g,
    triple_g,
    proj_g,
    stage,
    hid_t,
    hid_s,
    first_t,
    first_s,
    pat_t,
    pat_s,
    gpat,
    grad_t,
    probs,
    keep,
    keep_t,
    normed,
    mixed,
    act_hi,
    act_lo,
    dhid,
    dact,
    dtri,
    tsh,
    gtime,
    x80,
    gin_ref,
    ghead_ref,
    loss_ref,
    sem,
):
    bigs = big_ref.shape[0]
    smalls = small_ref.shape[0]
    count = bigs + smalls

    def block_copy(index, target):
        return pltpu.make_async_copy(whole_ref.at[owner_ref[index]], target, sem)

    def conv_target(array, index):
        m = index // CONV_BLOCKS
        rest = index - m * CONV_BLOCKS
        i = rest // 2
        j = rest - i * 2
        return array.at[m, pl.ds(pl.multiple_of(i * BLOCK, BLOCK), BLOCK), pl.ds(pl.multiple_of(j * BLOCK, BLOCK), BLOCK)]

    def load_conv(index, _):
        block_copy(index, conv_target(conv_w, index)).start()
        return _

    lax.fori_loop(0, 4 * CONV_BLOCKS, load_conv, 0)
    others = []
    for number in range(2):
        for k in range(TIME_COUNT):
            i, j = k // 4, k % 4
            others.append((TIME_FIRST + TIME_COUNT * number + k, time_w.at[number, i * BLOCK : (i + 1) * BLOCK, j * BLOCK : (j + 1) * BLOCK]))
    for k in range(TRIPLE_COUNT):
        i, j = k // 6, k % 6
        others.append((TRIPLE_FIRST + k, triple_w.at[i * BLOCK : (i + 1) * BLOCK, j * BLOCK : (j + 1) * BLOCK]))
    for k in range(PROJ_COUNT):
        i, j = k // 2, k % 2
        others.append((PROJ_FIRST + k, proj_w.at[i * BLOCK : (i + 1) * BLOCK, j * BLOCK : (j + 1) * BLOCK]))
    for index, target in others:
        block_copy(index, target).start()

    conv_g[...] = jnp.zeros_like(conv_g)
    triple_g[...] = jnp.zeros_like(triple_g)
    proj_g[...] = jnp.zeros_like(proj_g)
    gvec_ref[...] = jnp.zeros_like(gvec_ref)
    gin_ref[...] = jnp.zeros_like(gin_ref)
    ghead_ref[...] = jnp.zeros_like(ghead_ref)
    loss_ref[...] = jnp.zeros_like(loss_ref)
    gtime[...] = jnp.zeros_like(gtime)

    vin_hi, vin_lo = split(vin_ref[...])
    vin3 = jnp.concatenate([vin_hi, vin_lo, vin_hi], axis=0)
    head_hi, head_lo = split(head_ref[...])
    head2 = jnp.concatenate([head_hi, head_lo], axis=0)
    head3 = jnp.concatenate([head_hi, head_lo, head_hi], axis=0)

    def wait_conv(index, _):
        block_copy(0, conv_target(conv_w, index)).wait()
        return _

    lax.fori_loop(0, 4 * CONV_BLOCKS, wait_conv, 0)
    for index, target in others:
        block_copy(index, target).wait()

    for number in range(2):
        tsh[number] = mm(emb_ref[...], time_w[number])

    def vec(row):
        return vec_ref[row : row + 1, :]

    def add_vec(row, value):
        gvec_ref[row : row + 1, :] += value

    def run(image, clean_ref, noise_ref, local, side, small):
        pixels = side * side
        taps = tap_shifts(side)

        def scal(which, item):
            return scal_ref[image * 16 + which * 4 + item]

        def chunks(step=ROWS):
            return range(0, pixels, min(step, pixels))

        rows = min(ROWS, pixels)
        mrows = min(MM_ROWS, pixels)

        clear_ends(pat_t, side)
        for k in range(4):
            clear_ends(pat_s.at[k], side)
        clear_ends(gpat, side)

        noisies = []
        for which in range(2):
            noisies.append(clean_ref[local] + scal(which, 0) * noise_ref[local])

        def shifted_input(which):
            scaled = noisies[which] * scal(which, 1)
            parts = []
            for shift, inside in taps:
                parts.append(jnp.where(inside, pltpu.roll(scaled, (-shift) % pixels, 1), 0.0))
            first = lax.broadcasted_iota(jnp.int32, (8, pixels), 0) == 0
            parts.append(jnp.where(first, 1.0, 0.0))
            return jnp.concatenate(parts, axis=0)

        def hid(which, level):
            return hid_t if which == 0 else hid_s.at[level]

        def pat(which, level):
            return pat_t if which == 0 else pat_s.at[level]

        def first(which, level):
            return first_t if which == 0 else first_s.at[level]

        for which in range(2):
            value = shifted_input(which)
            high, low = split(value)
            if which == 1:
                x80[0:80, 0:pixels] = high
                x80[80:160, 0:pixels] = low
            three = jnp.concatenate([high, high, low], axis=0)
            hid(which, 0)[0:pixels, :] = mm_tn(three, vin3)

        def shifts(which, number):
            row = tsh[number, pl.ds(2 * image + which, 1), :]
            return row[:, 0:CH], row[:, CH:]

        stats = {}

        def act(which, key, src, gain, bias, dst):
            mean, rstd = group_stats(src, pixels)
            if which == 1:
                stats[key] = (mean, rstd)
            scale = rstd * gain
            for row in chunks():
                z = (src[row : row + rows, :] - mean) * scale + bias
                write_shifted(dst, row, z * sigmoid(z), side)

        def conv(src, number, row):
            total = None
            for dy in range(3):
                part = mm(src[dy * side + row : dy * side + row + mrows, :], conv_w[number, dy * 768 : (dy + 1) * 768, :])
                total = part if total is None else total + part
            return total

        for number in range(2):
            base = 28 + 6 * number
            for which in range(2):
                act(which, ("a", number), hid(which, number), vec(base), vec(base + 1), pat(which, 2 * number))
            for which in range(2):
                for row in chunks(MM_ROWS):
                    first(which, number)[row : row + mrows, :] = conv(pat(which, 2 * number), 2 * number, row) + vec(base + 2)
            for which in range(2):
                gain_t, bias_t = shifts(which, number)
                act(
                    which,
                    ("b", number),
                    first(which, number),
                    1.0 + gain_t + vec(base + 3),
                    bias_t + vec(base + 4),
                    pat(which, 2 * number + 1),
                )
            for which in range(2):
                for row in chunks(MM_ROWS):
                    second = conv(pat(which, 2 * number + 1), 2 * number + 1, row) + vec(base + 5)
                    at = slice(row, row + mrows)
                    hid(which, number + 1)[at, :] = (hid(which, number)[at, :] + second) * ROOT_HALF

        results = []
        for which in range(2):
            src = hid(which, 2)
            mean, rstd = group_stats(src, pixels)
            if which == 1:
                stats["n"] = (mean, rstd)
            scale = rstd * vec(40)
            for row in chunks():
                value = (src[row : row + rows, :] - mean) * scale + vec(41)
                normed[row : row + rows, :] = value.astype(BF16)
            for row in chunks(MM_ROWS):
                at = slice(row, row + mrows)
                triple = mm(normed[at, :], triple_w[...])
                keep[0, at, :] = (triple[:, 0:CH] + vec(42)).astype(BF16)
                key = triple[:, CH : 2 * CH]
                value = triple[:, 2 * CH :] + vec(43)
                keep[1, at, :] = key.astype(BF16)
                keep[2, at, :] = value.astype(BF16)
                keep_t[0, :, at] = jnp.transpose(value).astype(BF16)
                if which == 1:
                    keep_t[1, :, at] = jnp.transpose(key).astype(BF16)
            for col in chunks(MM_ROWS):
                at = slice(col, col + mrows)
                scores = mm_nt(keep[1, 0:pixels, :], keep[0, at, :]) * (1.0 / math.sqrt(CH))
                top = jnp.max(scores, axis=0, keepdims=True)
                weight = jnp.exp(scores - top)
                weight = weight * (1.0 / jnp.sum(weight, axis=0, keepdims=True))
                if which == 1:
                    probs[0:pixels, at] = weight
                out_t = mm(keep_t[0, :, 0:pixels], weight.astype(BF16))
                mixed[at, :] = jnp.transpose(out_t).astype(BF16)
            for row in chunks(MM_ROWS):
                at = slice(row, row + mrows)
                value = mm(mixed[at, :], proj_w[...]) + vec(44)
                hid(which, 3)[at, :] = (hid(which, 2)[at, :] + value) * ROOT_HALF
            src = hid(which, 3)
            mean, rstd = group_stats(src, pixels)
            if which == 1:
                stats["h"] = (mean, rstd)
            scale = rstd * vec(45)
            for row in chunks():
                z = (src[row : row + rows, :] - mean) * scale + vec(46)
                high, low = split(z * sigmoid(z))
                act_hi[row : row + rows, :] = high
                act_lo[row : row + rows, :] = low
            wide = mm_nt(head2, act_hi[0:pixels, :])
            wide = wide[0:80] + wide[80:160] + mm_nt(head_hi, act_lo[0:pixels, :])
            out = jnp.zeros((8, pixels), F32)
            for k, (shift, inside) in enumerate(taps):
                out = out + jnp.where(inside, pltpu.roll(wide[8 * k : 8 * k + 8], (-shift) % pixels, 1), 0.0)
            results.append(scal(which, 2) * noisies[which] + scal(which, 3) * out)

        diff = results[1] - results[0]
        weighted = diff * mask_ref[local] if small else diff
        bound = HUBER * math.sqrt(3 * pixels)
        total = jnp.sum(jnp.sum(weighted * diff, axis=1, keepdims=True), axis=0, keepdims=True)
        root = jnp.sqrt(total + bound * bound)
        rate = scal(2, 0)
        loss_ref[...] += jnp.broadcast_to((root - bound) * rate, (8, CH))
        dout = weighted * ((rate * scal(1, 3)) / root)

        parts = []
        for shift, inside in taps:
            parts.append(pltpu.roll(jnp.where(inside, dout, 0.0), shift % pixels, 1))
        parts.append(jnp.zeros((8, pixels), F32))
        high, low = split(jnp.concatenate(parts, axis=0))
        two = jnp.concatenate([high, low], axis=0)
        three = jnp.concatenate([high, high, low], axis=0)
        wide = mm(two, act_hi[0:pixels, :])
        ghead_ref[...] += wide[0:80] + wide[80:160] + mm(high, act_lo[0:pixels, :])
        dact[0:pixels, :] = mm_tn(three, head3)

        scale8 = 1.0 / (8 * pixels)

        def act_back(key, src, gain, bias, active):
            mean, rstd = stats[key]
            sum_b = jnp.zeros((8, CH), F32)
            sum_g = jnp.zeros((8, CH), F32)
            for row in chunks():
                at = slice(row, row + rows)
                value = (src[at, :] - mean) * rstd
                grad = dact[at, :]
                if active:
                    z = value * gain + bias
                    sig = sigmoid(z)
                    grad = grad * (sig * (1.0 + z * (1.0 - sig)))
                    dact[at, :] = grad
                sum_b = sum_b + fold(grad)
                sum_g = sum_g + fold(grad * value)
            sum_b = over_rows(sum_b)
            sum_g = over_rows(sum_g)
            mean_b = group_sum(sum_b * gain) * scale8
            mean_g = group_sum(sum_g * gain) * scale8

            def final(row):
                at = slice(row, row + rows)
                value = (src[at, :] - mean) * rstd
                return rstd * (gain * dact[at, :] - mean_b - value * mean_g)

            return sum_b, sum_g, final

        sum_b, sum_g, final = act_back("h", hid_s.at[3], vec(45), vec(46), True)
        add_vec(45, sum_g)
        add_vec(46, sum_b)
        total = jnp.zeros((8, CH), F32)
        for row in chunks():
            at = slice(row, row + rows)
            grad = final(row) * ROOT_HALF
            dhid[at, :] = grad
            total = total + fold(grad)
            low = grad.astype(BF16)
            normed_g = low
            gpat[row : row + rows, 0:CH] = normed_g
            grad_t[0, :, at] = jnp.transpose(grad).astype(BF16)
        add_vec(44, over_rows(total))
        proj_g[...] += mm(grad_t[0, :, 0:pixels], mixed[0:pixels, :])
        for row in chunks(MM_ROWS):
            at = slice(row, row + mrows)
            gpat[at, CH : 2 * CH] = mm_nt(gpat[at, 0:CH], proj_w[...]).astype(BF16)
        total = jnp.zeros((8, CH), F32)
        for col in chunks(MM_ROWS):
            at = slice(col, col + mrows)
            grad = mm_nt(keep[2, 0:pixels, :], gpat[at, CH : 2 * CH])
            weight = probs[0:pixels, at]
            inner = jnp.sum(weight * grad, axis=0, keepdims=True)
            probs_g = (weight * (grad - inner) * (1.0 / math.sqrt(CH))).astype(BF16)
            stage[0:pixels, at] = probs_g
            stage[0:pixels, 1024 + col : 1024 + col + mrows] = weight.astype(BF16)
            dq_t = mm(keep_t[1, :, 0:pixels], probs_g)
            dtri[at, 0:CH] = jnp.transpose(dq_t).astype(BF16)
            grad_t[0, :, at] = dq_t.astype(BF16)
            total = total + fold(jnp.transpose(dq_t))
        add_vec(42, over_rows(total))
        total = jnp.zeros((8, CH), F32)
        for row in chunks(MM_ROWS):
            at = slice(row, row + mrows)
            dk = mm(stage[at, 0:pixels], keep[0, 0:pixels, :])
            dv = mm(stage[at, 1024 : 1024 + pixels], gpat[0:pixels, CH : 2 * CH])
            total = total + fold(dv)
            dtri[at, CH : 2 * CH] = dk.astype(BF16)
            dtri[at, 2 * CH :] = dv.astype(BF16)
            grad_t[1, :, at] = jnp.transpose(dk).astype(BF16)
            grad_t[2, :, at] = jnp.transpose(dv).astype(BF16)
        add_vec(43, over_rows(total))
        for part in range(3):
            triple_g[part * CH : (part + 1) * CH, :] += mm(grad_t[part, :, 0:pixels], normed[0:pixels, :])
        for row in chunks(MM_ROWS):
            at = slice(row, row + mrows)
            dact[at, :] = mm_nt(dtri[at, :], triple_w[...])
        clear_ends(gpat, side)
        sum_b, sum_g, final = act_back("n", hid_s.at[2], vec(40), vec(41), False)
        add_vec(40, sum_g)
        add_vec(41, sum_b)
        for row in chunks():
            at = slice(row, row + rows)
            dhid[at, :] += final(row)

        def conv_back(number):
            for dy in range(3):
                conv_g[number, :, dy * 768 : (dy + 1) * 768] += mm(
                    grad_t[0, :, 0:pixels], pat_s[number, dy * side : dy * side + pixels, :]
                )
            for row in chunks(MM_ROWS):
                total = None
                for dy in range(3):
                    for dx in range(3):
                        tap = dy * 3 + dx
                        start = (2 - dy) * side + row
                        part = mm_nt(
                            gpat[start : start + mrows, (2 - dx) * CH : (3 - dx) * CH],
                            conv_w[number, tap * CH : (tap + 1) * CH, :],
                        )
                        total = part if total is None else total + part
                dact[row : row + mrows, :] = total

        for number in (1, 0):
            base = 28 + 6 * number
            total = jnp.zeros((8, CH), F32)
            for row in chunks():
                at = slice(row, row + rows)
                grad = dhid[at, :] * ROOT_HALF
                dhid[at, :] = grad
                total = total + fold(grad)
                write_shifted(gpat, row, grad, side)
                grad_t[0, :, at] = jnp.transpose(grad).astype(BF16)
            add_vec(base + 5, over_rows(total))
            conv_back(2 * number + 1)
            gain_t, bias_t = shifts(1, number)
            sum_b, sum_g, final = act_back(
                ("b", number),
                first_s.at[number],
                1.0 + gain_t + vec(base + 3),
                bias_t + vec(base + 4),
                True,
            )
            add_vec(base + 3, sum_g)
            add_vec(base + 4, sum_b)
            gtime[number, pl.ds(image, 1), 0:CH] = sum_g
            gtime[number, pl.ds(image, 1), CH:] = sum_b
            total = jnp.zeros((8, CH), F32)
            for row in chunks():
                at = slice(row, row + rows)
                grad = final(row)
                total = total + fold(grad)
                write_shifted(gpat, row, grad, side)
                grad_t[0, :, at] = jnp.transpose(grad).astype(BF16)
            add_vec(base + 2, over_rows(total))
            conv_back(2 * number)
            sum_b, sum_g, final = act_back(("a", number), hid_s.at[number], vec(base), vec(base + 1), True)
            add_vec(base, sum_g)
            add_vec(base + 1, sum_b)
            for row in chunks():
                at = slice(row, row + rows)
                dhid[at, :] += final(row)

        high, low = split(dhid[0:pixels, :])
        wide = mm(x80[:, 0:pixels], high)
        gin_ref[...] += wide[0:80] + wide[80:160] + mm(x80[0:80, 0:pixels], low)

    def big_image(index, carry):
        run(index, big_ref, big_noise_ref, index, SIDE, False)
        return carry

    lax.fori_loop(0, bigs, big_image, 0)

    def small_image(index, carry):
        run(bigs + index, small_ref, small_noise_ref, index, SMALL_SIDE, True)
        return carry

    lax.fori_loop(0, smalls, small_image, 0)

    emb = emb_ref[...].astype(F32)
    mine = jnp.concatenate(
        [emb[2 * k + 1 : 2 * k + 2] for k in range(count)] + [jnp.zeros((gtime.shape[1] - count, CH), F32)], axis=0
    ).astype(BF16)
    for number in range(2):
        time_g[number] = mm_tn(gtime[number].astype(BF16), mine)

    for tap in range(9):
        gvec_ref[3 * tap : 3 * tap + 3, :] = gin_ref[8 * tap : 8 * tap + 3, :]
        gvec_ref[47 + 3 * tap : 50 + 3 * tap, :] = ghead_ref[8 * tap : 8 * tap + 3, :]
    gvec_ref[27:28, :] = gin_ref[72:73, :]
    gvec_ref[74:75, :] = loss_ref[0:1, :]

    def out_copy(source, index):
        return pltpu.make_async_copy(source, grads_ref.at[owner_ref[index]], sem)

    for m in range(4):
        for j in range(2):
            part = slice(j * BLOCK, (j + 1) * BLOCK)
            for i in range(18):
                conv_w[m, i * BLOCK : (i + 1) * BLOCK, part] = conv_g[m, part, i * BLOCK : (i + 1) * BLOCK].astype(BF16)
    for number in range(2):
        for k in range(TIME_COUNT):
            i, j = k // 4, k % 4
            time_w[number, i * BLOCK : (i + 1) * BLOCK, j * BLOCK : (j + 1) * BLOCK] = time_g[
                number, j * BLOCK : (j + 1) * BLOCK, i * BLOCK : (i + 1) * BLOCK
            ].astype(BF16)
    for k in range(TRIPLE_COUNT):
        i, j = k // 6, k % 6
        triple_w[i * BLOCK : (i + 1) * BLOCK, j * BLOCK : (j + 1) * BLOCK] = triple_g[
            j * BLOCK : (j + 1) * BLOCK, i * BLOCK : (i + 1) * BLOCK
        ].astype(BF16)
    for k in range(PROJ_COUNT):
        i, j = k // 2, k % 2
        proj_w[i * BLOCK : (i + 1) * BLOCK, j * BLOCK : (j + 1) * BLOCK] = proj_g[
            j * BLOCK : (j + 1) * BLOCK, i * BLOCK : (i + 1) * BLOCK
        ].astype(BF16)

    def store_conv(index, carry):
        out_copy(conv_target(conv_w, index), index).start()
        return carry

    lax.fori_loop(0, 4 * CONV_BLOCKS, store_conv, 0)
    for index, target in others:
        out_copy(target, index).start()

    def wait_store(index, carry):
        out_copy(conv_target(conv_w, index), 0).wait()
        return carry

    lax.fori_loop(0, 4 * CONV_BLOCKS, wait_store, 0)
    for index, target in others:
        out_copy(target, index).wait()


def network_grads(owner_map, scalars, embed, big, big_noise, small, small_noise, mask, vectors, vin, head, whole):
    nb = owner_map.shape[0]
    slots = whole.shape[0]
    vmem = pl.BlockSpec(memory_space=pltpu.VMEM)
    smem = pl.BlockSpec(memory_space=pltpu.SMEM)
    hbm = pl.BlockSpec(memory_space=ANY)
    big_px = SIDE * SIDE
    tall = (SIDE + 2) * SIDE
    return pl.pallas_call(
        net_kernel,
        out_shape=(
            jax.ShapeDtypeStruct((slots, BLOCK, BLOCK), BF16),
            jax.ShapeDtypeStruct((80, CH), F32),
        ),
        in_specs=[smem, smem] + [vmem] * 9 + [hbm],
        out_specs=(hbm, vmem),
        scratch_shapes=[
            pltpu.VMEM((4, 9 * CH, CH), BF16),
            pltpu.VMEM((2, CH, 2 * CH), BF16),
            pltpu.VMEM((CH, 3 * CH), BF16),
            pltpu.VMEM((CH, CH), BF16),
            pltpu.VMEM((4, CH, 9 * CH), F32),
            pltpu.VMEM((2, 2 * CH, CH), F32),
            pltpu.VMEM((3 * CH, CH), F32),
            pltpu.VMEM((CH, CH), F32),
            pltpu.VMEM((big_px, 2 * big_px), BF16),
            pltpu.VMEM((big_px, CH), F32),
            pltpu.VMEM((4, big_px, CH), F32),
            pltpu.VMEM((big_px, CH), F32),
            pltpu.VMEM((2, big_px, CH), F32),
            pltpu.VMEM((tall, 3 * CH), BF16),
            pltpu.VMEM((4, tall, 3 * CH), BF16),
            pltpu.VMEM((tall, 3 * CH), BF16),
            pltpu.VMEM((3, CH, big_px), BF16),
            pltpu.VMEM((big_px, big_px), F32),
            pltpu.VMEM((3, big_px, CH), BF16),
            pltpu.VMEM((2, CH, big_px), BF16),
            pltpu.VMEM((big_px, CH), BF16),
            pltpu.VMEM((big_px, CH), BF16),
            pltpu.VMEM((big_px, CH), BF16),
            pltpu.VMEM((big_px, CH), BF16),
            pltpu.VMEM((big_px, CH), F32),
            pltpu.VMEM((big_px, CH), F32),
            pltpu.VMEM((big_px, 3 * CH), BF16),
            pltpu.VMEM((2, embed.shape[0], 2 * CH), F32),
            pltpu.VMEM((2, 16, 2 * CH), F32),
            pltpu.VMEM((160, big_px), BF16),
            pltpu.VMEM((80, CH), F32),
            pltpu.VMEM((80, CH), F32),
            pltpu.VMEM((8, CH), F32),
            pltpu.SemaphoreType.DMA,
        ],
        compiler_params=pltpu.CompilerParams(vmem_limit_bytes=60 * 1024 * 1024),
        cost_estimate=pl.CostEstimate(flops=57 * 10**9, bytes_accessed=20 * 10**6, transcendentals=10**7),
    )(owner_map, scalars, embed, big, big_noise, small, small_noise, mask, vectors, vin, head, whole)


MESH_ID = pl.DeviceIdType.MESH


def where_am_i():
    dp = lax.axis_index("dp")
    return lax.axis_index("pair"), dp // 4, (dp // 2) % 2, dp % 2


def device(pair, line, mid, core):
    return (pair, (line * 2 + mid) * 2 + core)


def neighbours():
    pair, line, mid, core = where_am_i()
    flip_pair, flip_mid = 1 - 2 * pair, 1 - 2 * mid
    second = device(pair + (1 - core) * flip_pair, line, mid + core * flip_mid, core)
    third = device(pair + core * flip_pair, line, mid + (1 - core) * flip_mid, core)
    sibling = device(pair, line, mid, 1 - core)
    at_second = (1 - core) * pair + core * mid
    at_third = core * pair + (1 - core) * mid
    return pair, line, mid, core, at_second, at_third, second, third, sibling


def greet(lines, devices, lower, upper, line):
    barrier = pltpu.get_barrier_semaphore()
    for other in devices:
        pl.semaphore_signal(barrier, inc=1, device_id=other, device_id_type=MESH_ID)
    for there, other in ((lower >= 0, lower), (upper < lines, upper)):

        @pl.when(there)
        def _(other=other):
            pl.semaphore_signal(barrier, inc=1, device_id=line(other), device_id_type=MESH_ID)

    beside = jnp.where(lower >= 0, 1, 0) + jnp.where(upper < lines, 1, 0)
    pl.semaphore_wait(barrier, len(devices) + beside)


def gather_kernel(
    lines, blocks_ref, whole_ref, own, up_send, down_send, second_send, third_send, sib_send, line_recv, second_recv, third_recv, sib_recv, own_sem
):
    pair, line, mid, core, at_second, at_third, second, third, sibling = neighbours()
    count = blocks_ref.shape[0]
    group = 4 * lines
    upper = device(pair, line + 1, mid, core)
    lower = device(pair, line - 1, mid, core)

    def place(l, s, t, c):
        p = (1 - c) * s + c * t
        m = c * s + (1 - c) * t
        return whole_ref.at[pl.ds((p * group + (l * 2 + m) * 2 + c) * count, count)]

    def copy(source, target, send, recv, to):
        return pltpu.make_async_remote_copy(
            src_ref=source, dst_ref=target, send_sem=send, recv_sem=recv, device_id=to, device_id_type=MESH_ID
        )

    def to_sibling(l, s, t, source=None):
        where = place(l, s, t, core)
        p = (1 - core) * s + core * t
        m = core * s + (1 - core) * t
        index = l * 4 + p * 2 + m
        return copy(where if source is None else source, where, sib_send.at[index], sib_recv.at[index], sibling)

    def to_second(l, source=None):
        where = place(l, at_second, at_third, core)
        return copy(where if source is None else source, where, second_send.at[l], second_recv.at[l], second)

    def to_third(l, s, source=None):
        where = place(l, s, at_third, core)
        index = l * 2 + s
        return copy(where if source is None else source, where, third_send.at[index], third_recv.at[index], third)

    def to_upper(l, source=None):
        where = place(l, at_second, at_third, core)
        return copy(where if source is None else source, where, up_send.at[l], line_recv.at[l], upper)

    def to_lower(l, source=None):
        where = place(l, at_second, at_third, core)
        return copy(where if source is None else source, where, down_send.at[l], line_recv.at[l], lower)

    own[...] = blocks_ref[...].astype(BF16)
    greet(lines, (second, third, sibling), line - 1, line + 1, lambda l: device(pair, l, mid, core))

    @pl.when(line < lines - 1)
    def _():
        to_upper(line, own).start()

    @pl.when(line > 0)
    def _():
        to_lower(line, own).start()

    to_third(line, at_second, own).start()
    to_second(line, own).start()
    to_sibling(line, at_second, at_third, own).start()
    keep = pltpu.make_async_copy(own, place(line, at_second, at_third, core), own_sem)
    keep.start()

    def from_second(l):
        to_second(l).wait_recv()
        to_third(l, 1 - at_second).start()
        to_sibling(l, 1 - at_second, at_third).start()

    def from_line(l):
        to_upper(l).wait_recv()

        @pl.when((l < line) & (line < lines - 1))
        def _():
            to_upper(l).start()

        @pl.when((l > line) & (line > 0))
        def _():
            to_lower(l).start()

        to_second(l).start()
        to_third(l, at_second).start()
        to_sibling(l, at_second, at_third).start()

    def both(distance, carry):
        @pl.when(line - distance >= 0)
        def _():
            from_line(line - distance)

        @pl.when(line + distance < lines)
        def _():
            from_line(line + distance)

        @pl.when(line - distance + 1 >= 0)
        def _():
            from_second(line - distance + 1)

        @pl.when((line + distance - 1 < lines) & (distance > 1))
        def _():
            from_second(line + distance - 1)

        return carry

    lax.fori_loop(1, lines + 1, both, 0)

    def from_third(l, carry):
        for s in range(2):
            to_third(l, s).wait_recv()
            to_sibling(l, s, 1 - at_third).start()
        return carry

    lax.fori_loop(0, lines, from_third, 0)

    def finish(l, carry):
        @pl.when((l <= line) & (line < lines - 1))
        def _():
            to_upper(l).wait_send()

        @pl.when((l >= line) & (line > 0))
        def _():
            to_lower(l).wait_send()

        to_second(l).wait_send()
        for s in range(2):
            to_third(l, s).wait_send()
            for t in range(2):
                done = to_sibling(l, s, t)
                done.wait_send()
                done.wait_recv()
        return carry

    lax.fori_loop(0, lines, finish, 0)
    keep.wait()


def gather_blocks(blocks):
    lines = lax.axis_size("dp") // 4
    count = blocks.shape[0]
    total = count * lines * 8
    dma = pltpu.SemaphoreType.DMA
    return pl.pallas_call(
        partial(gather_kernel, lines),
        out_shape=jax.ShapeDtypeStruct((total, BLOCK, BLOCK), BF16),
        in_specs=[pl.BlockSpec(memory_space=pltpu.VMEM)],
        out_specs=pl.BlockSpec(memory_space=ANY),
        scratch_shapes=[
            pltpu.VMEM((count, BLOCK, BLOCK), BF16),
            dma((lines,)),
            dma((lines,)),
            dma((lines,)),
            dma((2 * lines,)),
            dma((4 * lines,)),
            dma((lines,)),
            dma((lines,)),
            dma((2 * lines,)),
            dma((4 * lines,)),
            dma,
        ],
        compiler_params=pltpu.CompilerParams(collective_id=0, has_side_effects=True),
        cost_estimate=pl.CostEstimate(flops=0, bytes_accessed=2 * total * BLOCK * BLOCK * 2, transcendentals=0),
    )(blocks)


def sum_kernel(
    lines,
    grads_ref,
    vec_in,
    owned_ref,
    sum_ref,
    vec_ref,
    square_ref,
    mine,
    from_sib,
    from_third,
    from_second,
    from_lower,
    from_upper,
    vec_own,
    vec_got,
    sq_own,
    sq_got,
    load_sem,
    sib_send,
    third_send,
    second_send,
    up_send,
    down_send,
    sib_recv,
    third_recv,
    second_recv,
    up_recv,
    down_recv,
    vec_send,
    vec_recv,
    sq_send,
    sq_recv,
):
    pair, line, mid, core, at_second, at_third, second, third, sibling = neighbours()
    count = sum_ref.shape[0]
    group = 4 * lines
    upper = device(pair, line + 1, mid, core)
    lower = device(pair, line - 1, mid, core)
    steps = lines.bit_length() - 1
    hops = [sibling, third, second]
    far = []
    for bit in range(steps):
        flipped = line + (1 - 2 * ((line // 2**bit) % 2)) * 2**bit
        far.append(device(pair, flipped, mid, core))

    def copy(source, target, send, recv, to):
        return pltpu.make_async_remote_copy(
            src_ref=source, dst_ref=target, send_sem=send, recv_sem=recv, device_id=to, device_id_type=MESH_ID
        )

    def spot(l, s, t):
        return l * 4 + s * 2 + t

    def slots(l, s, t, c):
        p = (1 - c) * s + c * t
        m = c * s + (1 - c) * t
        return pl.ds((p * group + (l * 2 + m) * 2 + c) * count, count)

    def to_sibling(l, s, t):
        index = spot(l, s, t)
        return copy(grads_ref.at[slots(l, s, t, 1 - core)], from_sib.at[index], sib_send.at[index], sib_recv.at[index], sibling)

    def load(l, s, t):
        index = spot(l, s, t)
        return pltpu.make_async_copy(grads_ref.at[slots(l, s, t, core)], mine.at[index], load_sem.at[index])

    def to_third(l, s):
        index = l * 2 + s
        return copy(mine.at[spot(l, s, 1 - at_third)], from_third.at[index], third_send.at[index], third_recv.at[index], third)

    def to_second(l):
        return copy(mine.at[spot(l, 1 - at_second, at_third)], from_second.at[l], second_send.at[l], second_recv.at[l], second)

    def to_upper(l):
        return copy(mine.at[spot(l, at_second, at_third)], from_lower.at[l], up_send.at[l], up_recv.at[l], upper)

    def to_lower(l):
        return copy(mine.at[spot(l, at_second, at_third)], from_upper.at[l], down_send.at[l], down_recv.at[l], lower)

    def vec_step(k):
        to = (hops + far)[k]
        return copy(vec_own.at[k], vec_got.at[k], vec_send.at[k], vec_recv.at[k], to)

    def vec_next(k):
        vec_step(k).wait_recv()
        if k < 2 + steps:
            vec_own[k + 1] = vec_own[k] + vec_got[k]
            vec_step(k + 1).start()
        else:
            vec_ref[...] = vec_own[k] + vec_got[k]

    beside = line + 2 * (line % 2) - 1
    lowest = jnp.where(line % 2 == 0, beside, -1)
    highest = jnp.where(line % 2 == 1, beside, lines)
    greet(lines, hops + far, lowest, highest, lambda l: device(pair, l, mid, core))

    def far_first(function):
        def step(k, carry):
            distance = lines - 1 - k

            @pl.when(line + distance < lines)
            def _():
                function(line + distance)

            @pl.when((line - distance >= 0) & (distance > 0))
            def _():
                function(line - distance)

            return carry

        lax.fori_loop(0, lines, step, 0)

    def start_sibling(l, s, t):
        to_sibling(l, s, t).start()

    sib_second, sib_third = at_third, at_second
    for s, t in ((1, 1), (0, 1), (1, 0), (0, 0)):
        s_at = sib_second + s * (1 - 2 * sib_second)
        t_at = sib_third + t * (1 - 2 * sib_third)
        far_first(lambda l, s_at=s_at, t_at=t_at: start_sibling(l, s_at, t_at))
        s_own = at_second + s * (1 - 2 * at_second)
        t_own = at_third + t * (1 - 2 * at_third)
        far_first(lambda l, s_own=s_own, t_own=t_own: load(l, s_own, t_own).start())
    vec_own[0] = vec_in[...]
    vec_step(0).start()

    def both_cores(l, s, t):
        load(l, s, t).wait()
        to_sibling(l, s, t).wait_recv()
        index = spot(l, s, t)
        return mine[index].astype(F32) + from_sib[index].astype(F32)

    def send_third(l, s):
        mine[spot(l, s, 1 - at_third)] = both_cores(l, s, 1 - at_third).astype(BF16)
        to_third(l, s).start()

    far_first(lambda l: send_third(l, 1 - at_second))
    far_first(lambda l: send_third(l, at_second))
    vec_next(0)

    def with_third(l, s):
        total = both_cores(l, s, at_third)
        to_third(l, s).wait_recv()
        return total + from_third[l * 2 + s].astype(F32)

    def send_second(l):
        mine[spot(l, 1 - at_second, at_third)] = with_third(l, 1 - at_second).astype(BF16)
        to_second(l).start()

    far_first(send_second)
    vec_next(1)

    def with_second(l):
        total = with_third(l, at_second)
        to_second(l).wait_recv()
        return total + from_second[l].astype(F32)

    def send_line(k, carry):
        distance = lines - 1 - k
        above = line + distance
        below = line - distance

        @pl.when(above < lines)
        def _():
            total = with_second(above)
            index = spot(above, at_second, at_third)
            mine[index] = total.astype(BF16)

            @pl.when(line > 0)
            def _():
                to_upper(above).wait_recv()
                mine[index] = (total + from_lower[above].astype(F32)).astype(BF16)

            to_upper(above).start()

        @pl.when(below >= 0)
        def _():
            total = with_second(below)
            index = spot(below, at_second, at_third)
            mine[index] = total.astype(BF16)

            @pl.when(line < lines - 1)
            def _():
                to_lower(below).wait_recv()
                mine[index] = (total + from_upper[below].astype(F32)).astype(BF16)

            to_lower(below).start()

        return carry

    lax.fori_loop(0, lines - 1, send_line, 0)
    vec_next(2)
    sum_ref[...] = with_second(line)

    @pl.when(line > 0)
    def _():
        to_upper(line).wait_recv()
        sum_ref[...] += from_lower[line].astype(F32)

    @pl.when(line < lines - 1)
    def _():
        to_lower(line).wait_recv()
        sum_ref[...] += from_upper[line].astype(F32)

    total = jnp.where(owned_ref[...] > 0, sum_ref[...], 0.0)
    sum_ref[...] = total
    square = jnp.sum((total * total).reshape(count * BLOCK // 8, 8, BLOCK), axis=0)
    sq_own[0] = square

    def sq_step(k):
        to = (hops + far)[k]
        return copy(sq_own.at[k], sq_got.at[k], sq_send.at[k], sq_recv.at[k], to)

    sq_step(0).start()
    for k in range(3 + steps):
        if k > 2:
            vec_next(k)
        sq_step(k).wait_recv()
        if k < 2 + steps:
            sq_own[k + 1] = sq_own[k] + sq_got[k]
            sq_step(k + 1).start()
        else:
            square_ref[...] = sq_own[k] + sq_got[k]

    def finish(l, carry):
        for s in range(2):
            for t in range(2):
                to_sibling(l, s, t).wait_send()
            to_third(l, s).wait_send()
        to_second(l).wait_send()

        @pl.when((l > line) & (line < lines - 1))
        def _():
            to_upper(l).wait_send()

        @pl.when((l < line) & (line > 0))
        def _():
            to_lower(l).wait_send()

        return carry

    lax.fori_loop(0, lines, finish, 0)
    for k in range(3 + steps):
        vec_step(k).wait_send()
        sq_step(k).wait_send()


def sum_by_slot(grads, vec, owned):
    lines = lax.axis_size("dp") // 4
    count = grads.shape[0] // (8 * lines)
    steps = 3 + lines.bit_length() - 1
    dma = pltpu.SemaphoreType.DMA
    vmem = pl.BlockSpec(memory_space=pltpu.VMEM)
    shard = (count, BLOCK, BLOCK)
    owned = jnp.broadcast_to(owned.astype(F32)[:, None, None], (count, 1, BLOCK))
    return pl.pallas_call(
        partial(sum_kernel, lines),
        out_shape=(
            jax.ShapeDtypeStruct(shard, F32),
            jax.ShapeDtypeStruct(vec.shape, F32),
            jax.ShapeDtypeStruct((8, BLOCK), F32),
        ),
        in_specs=[pl.BlockSpec(memory_space=ANY), vmem, vmem],
        out_specs=(vmem, vmem, vmem),
        scratch_shapes=[
            pltpu.VMEM((4 * lines,) + shard, BF16),
            pltpu.VMEM((4 * lines,) + shard, BF16),
            pltpu.VMEM((2 * lines,) + shard, BF16),
            pltpu.VMEM((lines,) + shard, BF16),
            pltpu.VMEM((lines,) + shard, BF16),
            pltpu.VMEM((lines,) + shard, BF16),
            pltpu.VMEM((steps,) + vec.shape, F32),
            pltpu.VMEM((steps,) + vec.shape, F32),
            pltpu.VMEM((steps, 8, BLOCK), F32),
            pltpu.VMEM((steps, 8, BLOCK), F32),
            dma((4 * lines,)),
            dma((4 * lines,)),
            dma((2 * lines,)),
            dma((lines,)),
            dma((lines,)),
            dma((lines,)),
            dma((4 * lines,)),
            dma((2 * lines,)),
            dma((lines,)),
            dma((lines,)),
            dma((lines,)),
            dma((steps,)),
            dma((steps,)),
            dma((steps,)),
            dma((steps,)),
        ],
        compiler_params=pltpu.CompilerParams(collective_id=1, has_side_effects=True, vmem_limit_bytes=48 * 1024 * 1024),
        cost_estimate=pl.CostEstimate(flops=0, bytes_accessed=2 * grads.size * 2, transcendentals=0),
    )(grads, vec, owned)


def sigma_of(levels):
    lowest = SIGMA_MIN ** (1.0 / RHO)
    highest = SIGMA_MAX ** (1.0 / RHO)
    return (lowest + levels.astype(F32) / (NSTEPS - 1) * (highest - lowest)) ** RHO


def shampoo(grads, master, moments, left_stats, right_stats, left_roots, right_roots):
    first = BETA_ONE * moments + (1 - BETA_ONE) * jnp.swapaxes(grads, 1, 2)
    left = BETA_TWO * left_stats + (1 - BETA_TWO) * jnp.einsum(
        "sji,sjk->sik", grads, grads, precision=HIGH
    )
    right = BETA_TWO * right_stats + (1 - BETA_TWO) * jnp.einsum(
        "sij,skj->sik", grads, grads, precision=HIGH
    )
    turned = jnp.einsum("sij,sjk->sik", left_roots, first, precision=HIGH)
    turned = jnp.einsum("sij,sjk->sik", turned, right_roots, precision=HIGH)
    norm_rms = jnp.sqrt(jnp.mean(turned * turned, axis=(1, 2), keepdims=True) + 1e-20)
    return (master - RATE_MATRIX * (turned / norm_rms + DECAY * master), first, left, right)


def adamw(grads, params, first, second):
    first = BETA_ONE * first + (1 - BETA_ONE) * grads
    second = BETA_TWO * second + (1 - BETA_TWO) * grads * grads
    fixed_first = first / (1 - BETA_ONE**STEP)
    fixed_second = second / (1 - BETA_TWO**STEP)
    return (
        params - RATE_VECTOR * (fixed_first / (jnp.sqrt(fixed_second) + 1e-08) + DECAY * params),
        first,
        second,
    )


def prepare(big_images, big_noise, small_images, small_noise, big_level, small_level, small_mask, vectors, pair_index):
    def half(values):
        count = values.shape[0] // 2
        return lax.dynamic_slice_in_dim(values, pair_index * count, count, 0)

    def rows8(values):
        return jnp.pad(values, ((0, 0), (0, 5), (0, 0)))

    levels = jnp.concatenate([half(big_level), half(small_level)])
    count = levels.shape[0]
    sigma = sigma_of(levels[:, None] + jnp.arange(2)[None, :])
    scale_in = lax.rsqrt(sigma * sigma + SIGMA_DATA**2)
    skip = SIGMA_DATA**2 / ((sigma - SIGMA_MIN) ** 2 + SIGMA_DATA**2)
    outer = (sigma - SIGMA_MIN) * SIGMA_DATA * lax.rsqrt(SIGMA_DATA**2 + sigma * sigma)
    rate = 1.0 / (sigma[:, 1] - sigma[:, 0])
    per_pass = jnp.stack([sigma, scale_in, skip, outer], axis=-1).reshape(count, 8)
    scalars = jnp.concatenate([per_pass, jnp.pad(rate[:, None], ((0, 0), (0, 7)))], axis=1).reshape(-1)
    half_ch = CH // 2
    freqs = jnp.exp(jnp.arange(half_ch, dtype=F32) * (math.log(100.0) / (half_ch - 1)))
    phase = (jnp.log(sigma) / 4.0).reshape(-1, 1) * freqs
    embed = jnp.concatenate([jnp.sin(phase), jnp.cos(phase)], axis=-1)
    embed = jnp.pad(embed, ((0, -embed.shape[0] % 16), (0, 0))).astype(BF16)
    vin = jnp.pad(vectors[0:27].reshape(9, 3, CH), ((0, 0), (0, 5), (0, 0))).reshape(72, CH)
    vin = jnp.concatenate([vin, vectors[27:28], jnp.zeros((7, CH), F32)], axis=0)
    head = jnp.pad(vectors[47:74].reshape(9, 3, CH), ((0, 0), (0, 5), (0, 0))).reshape(72, CH)
    head = jnp.pad(head, ((0, 8), (0, 0)))
    mask = jnp.broadcast_to(half(small_mask).astype(F32)[:, None, :], (small_mask.shape[0] // 2, 8, small_mask.shape[1]))
    return (
        scalars,
        embed,
        rows8(half(big_images)),
        rows8(half(big_noise)),
        rows8(half(small_images)),
        rows8(half(small_noise)),
        mask,
        jnp.pad(vectors, ((0, 6), (0, 0))),
        vin,
        head,
    )


def local(
    big_images,
    big_noise,
    small_images,
    small_noise,
    big_level,
    small_level,
    small_mask,
    owner_map,
    blocks,
    moments,
    left_stats,
    right_stats,
    left_roots,
    right_roots,
    vectors,
    vec_first,
    vec_second,
):
    slot_count = blocks.shape[0]
    whole = gather_blocks(blocks)
    ready = prepare(
        big_images, big_noise, small_images, small_noise, big_level, small_level, small_mask, vectors, lax.axis_index("pair")
    )
    grads, vec_part = network_grads(owner_map, *ready, whole)
    slot_ids = lax.axis_index(("pair", "dp")) * slot_count + jnp.arange(slot_count, dtype=jnp.int32)
    owned = jnp.any(slot_ids[:, None] == owner_map[None, :], axis=1)
    mine, vec_sum, square = sum_by_slot(grads, vec_part, owned)
    count = vectors.shape[0]
    vec_total = vec_sum[:count]
    loss_total = vec_sum[count, 0]
    grad_norm = jnp.sqrt(jnp.sum(square) + jnp.sum(vec_total * vec_total))
    factor = jnp.minimum(1.0, CLIP / (grad_norm + 1e-06))
    slot_grad = mine * factor
    new_blocks, new_moments, new_left, new_right = shampoo(
        slot_grad, blocks, moments, left_stats, right_stats, left_roots, right_roots
    )
    new_vectors, new_first, new_second = adamw(vec_total * factor, vectors, vec_first, vec_second)
    return (
        loss_total,
        grad_norm,
        new_blocks,
        new_moments,
        new_left,
        new_right,
        new_vectors,
        new_first,
        new_second,
    )


def solution(mesh):
    by_slot = P(("pair", "dp"), None, None)
    by_image = P("dp", None, None)
    placed = (by_image,) * 4 + (P("dp"), P("dp"), P("dp", None), P()) + (by_slot,) * 6 + (P(),) * 3
    return jax.shard_map(
        local,
        mesh=mesh,
        in_specs=placed,
        out_specs=(P(), P()) + (by_slot,) * 4 + (P(),) * 3,
        check_vma=False,
    )
```

```python
from functools import partial
import math

import jax
import jax.numpy as jnp
from jax import lax
from jax.experimental import pallas as pl
from jax.experimental.pallas import tpu as pltpu
from jax.sharding import PartitionSpec as P
import numpy as np

GROUPS = 32
SIDE = 32
SMALL_SIDE = 16
NSTEPS = 11
STEP = 10
CH = 256
BLOCK = 128

HIGH = lax.Precision.HIGHEST
SIGMA_DATA = 0.5
SIGMA_MIN = 0.002
SIGMA_MAX = 80.0
RHO = 7.0
HUBER = 0.00054
CLIP = 1.0
BETA_ONE = 0.9
BETA_TWO = 0.999
DECAY = 0.0001
RATE_MATRIX = 0.02
RATE_VECTOR = 0.02
ROOT_HALF = 1.0 / math.sqrt(2.0)
ANY = pl.ANY
F32 = jnp.float32
BF16 = jnp.bfloat16

CONV_BLOCKS = 36
TIME_FIRST, TIME_COUNT = 144, 8
TRIPLE_FIRST, TRIPLE_COUNT = 160, 12
PROJ_FIRST, PROJ_COUNT = 172, 4

ROWS = 128
MM_ROWS = 256


def mm(left, right):
    return jnp.dot(left, right, preferred_element_type=F32)


def mm_nt(left, right):
    return lax.dot_general(left, right, (((1,), (1,)), ((), ())), preferred_element_type=F32)


def mm_tn(left, right):
    return lax.dot_general(left, right, (((0,), (0,)), ((), ())), preferred_element_type=F32)


def split(value):
    high = value.astype(BF16)
    return high, (value - high.astype(F32)).astype(BF16)


def fold(value):
    return jnp.sum(value.reshape(value.shape[0] // 8, 8, value.shape[1]), axis=0)


def over_rows(value):
    return jnp.sum(value, axis=0, keepdims=True)


def group_mean(value, ones):
    high = value.astype(BF16).astype(F32)
    rest = value - high
    middle = rest.astype(BF16).astype(F32)
    parts = jnp.concatenate([high, middle, rest - middle, jnp.zeros_like(value)], axis=0).astype(BF16)
    sums = mm(parts, ones)
    return (sums[0:8] + sums[8:16] + sums[16:24]) * 0.125


def sigmoid(value):
    return 0.5 + 0.5 * jnp.tanh(0.5 * value)


def group_stats(ref, pixels, ones):
    total = jnp.zeros((8, CH), F32)
    for row in range(0, pixels, ROWS):
        total = total + fold(ref[row : row + ROWS, :])
    own = jnp.broadcast_to(over_rows(total) * (1.0 / pixels), (8, CH))
    mean = group_mean(own, ones)
    total = jnp.zeros((8, CH), F32)
    for row in range(0, pixels, ROWS):
        center = ref[row : row + ROWS, :] - own[0:1]
        total = total + fold(center * center)
    within = jnp.broadcast_to(over_rows(total) * (1.0 / pixels), (8, CH))
    between = own - mean
    spread = group_mean(within + between * between, ones)
    return mean[0:1], lax.rsqrt(spread[0:1] + 1e-06)


def write_shifted(ref, row, value, side):
    count = value.shape[0]
    column = lax.broadcasted_iota(jnp.int32, (count, CH), 0) & (side - 1)
    left = jnp.where(column == 0, 0.0, pltpu.roll(value, 1, 0))
    right = jnp.where(column == side - 1, 0.0, pltpu.roll(value, count - 1, 0))
    at = slice(side + row, side + row + count)
    ref[at, 0:CH] = left.astype(BF16)
    ref[at, CH : 2 * CH] = value.astype(BF16)
    ref[at, 2 * CH : 3 * CH] = right.astype(BF16)


def clear_ends(ref, side):
    pixels = side * side
    zeros = jnp.zeros((side, 3 * CH), BF16)
    ref[0:side, :] = zeros
    ref[side + pixels : 2 * side + pixels, :] = zeros


def tap_shifts(side):
    pixels = side * side
    place = lax.broadcasted_iota(jnp.int32, (8, pixels), 1)
    x = place & (side - 1)
    y = place >> (side.bit_length() - 1)
    taps = []
    for dy in (-1, 0, 1):
        for dx in (-1, 0, 1):
            inside = (x + dx >= 0) & (x + dx < side) & (y + dy >= 0) & (y + dy < side)
            taps.append((dy * side + dx, inside))
    return taps


class Shared:
    pass


class Job:
    def __init__(self, image, local, clean, noise, mask, side, refs):
        self.image, self.local, self.clean, self.noise, self.mask, self.side = image, local, clean, noise, mask, side
        self.pixels = side * side
        self.rows = min(ROWS, self.pixels)
        self.mrows = min(MM_ROWS, self.pixels)
        (
            self.hid,
            self.first,
            self.pat,
            self.gpat,
            self.grad_t,
            self.expo,
            self.dscore,
            self.keep,
            self.value_t,
            self.key_t,
            self.normed,
            self.mixed,
            self.mixed_t,
            self.rinv,
            self.act_hi,
            self.act_lo,
            self.dhid,
            self.dact,
            self.dtri,
            self.x80,
            self.scaled,
        ) = refs
        self.stats = {}
        self.outs = [None, None]
        self.noisy = [None, None]

    def chunks(self):
        return [slice(row, row + self.rows) for row in range(0, self.pixels, self.rows)]

    def blocks(self):
        return [slice(row, row + self.mrows) for row in range(0, self.pixels, self.mrows)]

    def hid_of(self, which, level):
        return self.hid.at[level] if which else self.dhid

    def first_of(self, which, number):
        return self.first.at[number] if which else self.dact

    def pat_of(self, which, number):
        return self.pat.at[number] if which else self.gpat

    def keep_of(self, which, part):
        return self.keep.at[part] if which else self.dtri.at[part]

    def expo_of(self, which):
        return self.expo if which else self.dscore

    def value_t_of(self, which):
        return self.value_t if which else self.grad_t.at[0]


def job_scratch(side):
    pixels = side * side
    tall = pixels + 2 * side
    return [
        pltpu.VMEM((4, pixels, CH), F32),
        pltpu.VMEM((2, pixels, CH), F32),
        pltpu.VMEM((4, tall, 3 * CH), BF16),
        pltpu.VMEM((tall, 3 * CH), BF16),
        pltpu.VMEM((3, CH, pixels), BF16),
        pltpu.VMEM((pixels, pixels), BF16),
        pltpu.VMEM((pixels, pixels), BF16),
        pltpu.VMEM((3, pixels, CH), BF16),
        pltpu.VMEM((CH, pixels), BF16),
        pltpu.VMEM((CH, pixels), BF16),
        pltpu.VMEM((pixels, CH), BF16),
        pltpu.VMEM((pixels, CH), BF16),
        pltpu.VMEM((CH, pixels), F32),
        pltpu.VMEM((8, pixels), F32),
        pltpu.VMEM((pixels, CH), BF16),
        pltpu.VMEM((pixels, CH), BF16),
        pltpu.VMEM((pixels, CH), F32),
        pltpu.VMEM((pixels, CH), F32),
        pltpu.VMEM((3, pixels, CH), BF16),
        pltpu.VMEM((160, pixels), BF16),
        pltpu.VMEM((pixels, CH), BF16),
    ]


JOB_REFS = 21


def forward_pass(job, which, net):
    vec, side, pixels = net.vec, job.side, job.pixels
    taps = tap_shifts(side)

    def scal(item):
        return net.scal(job, which, item)

    noisy = job.clean[job.local] + scal(0) * job.noise[job.local]
    noisy = jnp.concatenate([noisy, jnp.zeros((5, pixels), F32)], axis=0)
    job.noisy[which] = noisy
    scaled = noisy * scal(1)
    parts = [jnp.where(inside, pltpu.roll(scaled, (-shift) % pixels, 1), 0.0) for shift, inside in taps]
    parts.append(jnp.where(lax.broadcasted_iota(jnp.int32, (8, pixels), 0) == 0, 1.0, 0.0))
    high, low = split(jnp.concatenate(parts, axis=0))
    if which:
        job.x80[0:80, :] = high
        job.x80[80:160, :] = low
        for k in range(4):
            clear_ends(job.pat.at[k], side)
    else:
        clear_ends(job.gpat, side)
    job.hid_of(which, 0)[...] = mm_tn(jnp.concatenate([high, high, low], axis=0), net.vin3)
    yield

    def act(key, src, gain, bias, dst):
        mean, rstd = group_stats(src, pixels, net.ones)
        job.stats[which, key] = (mean, rstd)
        scale = rstd * gain
        for at in job.chunks():
            z = (src[at, :] - mean) * scale + bias
            write_shifted(dst, at.start, z * sigmoid(z), side)

    def conv(src, number, row):
        total = None
        for dy in range(3):
            start = dy * side + row
            part = mm(src[start : start + job.mrows, :], net.conv_w[number, dy * 768 : (dy + 1) * 768, :])
            total = part if total is None else total + part
        return total

    for number in range(2):
        base = 28 + 6 * number
        hid = job.hid_of(which, number)
        after = job.hid_of(which, number + 1)
        act(("a", number), hid, vec(base), vec(base + 1), job.pat_of(which, 2 * number))
        yield
        net.ready(2 * number)
        first = job.first_of(which, number)
        for at in job.blocks():
            first[at, :] = conv(job.pat_of(which, 2 * number), 2 * number, at.start) + vec(base + 2)
        yield
        gain_t, bias_t = net.shifts(job, which, number)
        act(("b", number), first, 1.0 + gain_t + vec(base + 3), bias_t + vec(base + 4), job.pat_of(which, 2 * number + 1))
        yield
        net.ready(2 * number + 1)
        for at in job.blocks():
            second = conv(job.pat_of(which, 2 * number + 1), 2 * number + 1, at.start) + vec(base + 5)
            after[at, :] = (hid[at, :] + second) * ROOT_HALF
        yield

    net.ready("attention")
    src = job.hid_of(which, 2)
    mean, rstd = group_stats(src, pixels, net.ones)
    job.stats[which, "n"] = (mean, rstd)
    scale = rstd * vec(40)
    query, key, value_of = (job.keep_of(which, part) for part in range(3))
    value_t = job.value_t_of(which)
    for at in job.blocks():
        normed = ((src[at, :] - mean) * scale + vec(41)).astype(BF16)
        if which:
            job.normed[at, :] = normed
        triple = mm(normed, net.triple_w[...])
        query[at, :] = ((triple[:, 0:CH] + vec(42)) * (1.0 / math.sqrt(CH))).astype(BF16)
        key[at, :] = triple[:, CH : 2 * CH].astype(BF16)
        value = triple[:, 2 * CH :] + vec(43)
        value_of[at, :] = value.astype(BF16)
        value_t[:, at] = jnp.transpose(value).astype(BF16)
        if which:
            job.key_t[:, at] = (jnp.transpose(triple[:, CH : 2 * CH]) * (1.0 / math.sqrt(CH))).astype(BF16)
    yield
    expo = job.expo_of(which)
    after = job.hid_of(which, 3)
    for at in job.blocks():
        scores = mm_nt(key[...], query[at, :])
        weight = jnp.exp(scores - jnp.max(scores, axis=0, keepdims=True))
        total = jnp.sum(weight, axis=0, keepdims=True)
        expo[:, at] = weight.astype(BF16)
        rinv = 1.0 / total
        mixed_t = mm(value_t[...], expo[:, at]) * rinv
        mixed = jnp.transpose(mixed_t).astype(BF16)
        if which:
            job.rinv[:, at] = jnp.broadcast_to(rinv, (8, job.mrows))
            job.mixed_t[:, at] = mixed_t
            job.mixed[at, :] = mixed
        after[at, :] = (src[at, :] + (mm(mixed, net.proj_w[...]) + vec(44))) * ROOT_HALF
        yield
    mean, rstd = group_stats(after, pixels, net.ones)
    job.stats[which, "h"] = (mean, rstd)
    scale = rstd * vec(45)
    wide = []
    for at in job.blocks():
        z = (after[at, :] - mean) * scale + vec(46)
        high, low = split(z * sigmoid(z))
        if which:
            job.act_hi[at, :] = high
            job.act_lo[at, :] = low
        part = mm_nt(net.head2, high)
        wide.append(part[0:80] + part[80:160] + mm_nt(net.head_hi, low))
    wide = jnp.concatenate(wide, axis=1)
    out = jnp.zeros((8, pixels), F32)
    for k, (shift, inside) in enumerate(taps):
        out = out + jnp.where(inside, pltpu.roll(wide[8 * k : 8 * k + 8], (-shift) % pixels, 1), 0.0)
    job.outs[which] = scal(2) * noisy + scal(3) * out
    yield


def backward_pass(job, net, finish):
    vec, side, pixels = net.vec, job.side, job.pixels
    taps = tap_shifts(side)
    dact, dhid, gpat, grad_t = job.dact, job.dhid, job.gpat, job.grad_t

    def add_vec(row, value):
        net.gvec[row : row + 1, :] += value

    diff = job.outs[1] - job.outs[0]
    weighted = diff if job.mask is None else diff * job.mask[pl.ds(job.local, 1), :].astype(F32)
    bound = HUBER * math.sqrt(3 * pixels)
    total = jnp.sum(jnp.sum(weighted * diff, axis=1, keepdims=True), axis=0, keepdims=True)
    root = jnp.sqrt(total + bound * bound)
    rate = net.scal(job, 0, 4)
    net.loss[...] += jnp.broadcast_to((root - bound) * rate, (8, CH))
    dout = weighted * ((rate * net.scal(job, 1, 3)) / root)

    parts = [pltpu.roll(jnp.where(inside, dout, 0.0), shift % pixels, 1) for shift, inside in taps]
    parts.append(jnp.zeros((8, pixels), F32))
    high, low = split(jnp.concatenate(parts, axis=0))
    three = jnp.concatenate([high, high, low], axis=0)
    dact[...] = mm_tn(three, net.head3)
    wide = mm(jnp.concatenate([high, low], axis=0), job.act_hi[...])
    net.ghead[...] += wide[0:80] + wide[80:160] + mm(high, job.act_lo[...])
    yield

    def act_sums(key, src, gain, bias, active):
        mean, rstd = job.stats[1, key]
        sum_b = jnp.zeros((8, CH), F32)
        sum_g = jnp.zeros((8, CH), F32)
        for at in job.chunks():
            value = (src[at, :] - mean) * rstd
            grad = dact[at, :]
            if active:
                z = value * gain + bias
                sig = sigmoid(z)
                grad = grad * (sig * (1.0 + z * (1.0 - sig)))
                dact[at, :] = grad
            sum_b = sum_b + fold(grad)
            sum_g = sum_g + fold(grad * value)
        sum_b = over_rows(sum_b)
        sum_g = over_rows(sum_g)
        both = jnp.concatenate([sum_b * gain, sum_g * gain, jnp.zeros((6, CH), F32)], axis=0)
        means = group_mean(both, net.ones) * (1.0 / pixels)
        of_grad = rstd * gain
        of_value = rstd * rstd * means[1:2]
        constant = rstd * means[0:1]

        def final(at):
            return of_grad * dact[at, :] - (src[at, :] - mean) * of_value - constant

        return sum_b, sum_g, final

    sum_b, sum_g, final = act_sums("h", job.hid.at[3], vec(45), vec(46), True)
    add_vec(45, sum_g)
    add_vec(46, sum_b)
    yield
    total = jnp.zeros((8, CH), F32)
    for at in job.chunks():
        grad = final(at) * ROOT_HALF
        dhid[at, :] = grad
        total = total + fold(grad)
        gpat[at, 0:CH] = grad.astype(BF16)
        grad_t[0, :, at] = jnp.transpose(grad).astype(BF16)
    add_vec(44, over_rows(total))
    yield

    def wgrad(key, acc, at, value, last):
        if key in net.begun:
            value = value + acc[at]
        net.begun.add(key)
        if finish:
            last(value)
        else:
            acc[at] = value

    wgrad("proj", net.proj_g, (slice(None), slice(None)), mm(grad_t[0], job.mixed[...]), net.put_proj)
    total = jnp.zeros((8, CH), F32)
    query, key, value_of = (job.keep.at[part] for part in range(3))
    for at in job.blocks():
        out_t = mm_nt(net.proj_w[...], gpat[at, 0:CH])
        low_t = out_t.astype(BF16)
        inner = jnp.sum(low_t.astype(F32) * job.mixed_t[:, at], axis=0, keepdims=True)
        rinv = job.rinv[0:1, at]
        job.scaled[at, :] = jnp.transpose(out_t * rinv).astype(BF16)
        grad = mm(value_of[...], low_t)
        job.dscore[:, at] = (job.expo[:, at].astype(F32) * ((grad - inner) * rinv)).astype(BF16)
        dq_t = mm(job.key_t[...], job.dscore[:, at])
        dq = jnp.transpose(dq_t)
        total = total + fold(dq)
        job.dtri[0, at, :] = dq.astype(BF16)
        grad_t[0, :, at] = dq_t.astype(BF16)
        yield
    if finish:
        net.send("proj")
    add_vec(42, over_rows(total))
    total = jnp.zeros((8, CH), F32)
    for at in job.blocks():
        dk = mm(job.dscore[at, :], query[...])
        dv = mm(job.expo[at, :], job.scaled[...])
        total = total + fold(dv)
        job.dtri[1, at, :] = dk.astype(BF16)
        job.dtri[2, at, :] = dv.astype(BF16)
        grad_t[1, :, at] = jnp.transpose(dk).astype(BF16)
        grad_t[2, :, at] = jnp.transpose(dv).astype(BF16)
    add_vec(43, over_rows(total))
    yield
    for at in job.blocks():
        grad = None
        for part in range(3):
            more = mm_nt(job.dtri[part, at, :], net.triple_w[:, part * CH : (part + 1) * CH])
            grad = more if grad is None else grad + more
        dact[at, :] = grad
    for part in range(3):
        wgrad(
            ("triple", part),
            net.triple_g,
            (slice(part * CH, (part + 1) * CH), slice(None)),
            mm(grad_t[part], job.normed[...]),
            partial(net.put_triple, part),
        )
    if finish:
        net.send("triple")
    yield
    clear_ends(gpat, side)
    sum_b, sum_g, final = act_sums("n", job.hid.at[2], vec(40), vec(41), False)
    add_vec(40, sum_g)
    add_vec(41, sum_b)
    yield

    def conv_in(number):
        for at in job.blocks():
            total = None
            for dy in range(3):
                for dx in range(3):
                    tap = dy * 3 + dx
                    start = (2 - dy) * side + at.start
                    part = mm_nt(
                        gpat[start : start + job.mrows, (2 - dx) * CH : (3 - dx) * CH],
                        net.conv_w[number, tap * CH : (tap + 1) * CH, :],
                    )
                    total = part if total is None else total + part
            dact[at, :] = total

    def conv_matrix(number, slot):
        for dy in range(3):
            wgrad(
                (number, dy),
                net.conv_g,
                (number, slice(None), slice(dy * 768, (dy + 1) * 768)),
                mm(grad_t[slot], job.pat[number, dy * side : dy * side + pixels, :]),
                partial(net.put_conv, number, dy),
            )
        if finish:
            net.send(number)

    def turn(row, grad, slot):
        write_shifted(gpat, row, grad, side)
        grad_t[slot, :, row : row + job.rows] = jnp.transpose(grad).astype(BF16)

    for number in (1, 0):
        base = 28 + 6 * number
        total = jnp.zeros((8, CH), F32)
        for at in job.chunks():
            grad = (dhid[at, :] + final(at)) * ROOT_HALF
            dhid[at, :] = grad
            total = total + fold(grad)
            turn(at.start, grad, 0)
        add_vec(base + 5, over_rows(total))
        yield
        conv_in(2 * number + 1)
        yield
        gain_t, bias_t = net.shifts(job, 1, number)
        sum_b, sum_g, final = act_sums(
            ("b", number), job.first.at[number], 1.0 + gain_t + vec(base + 3), bias_t + vec(base + 4), True
        )
        conv_matrix(2 * number + 1, 0)
        add_vec(base + 3, sum_g)
        add_vec(base + 4, sum_b)
        net.gtime[number, job.image : job.image + 1, 0:CH] = sum_g
        net.gtime[number, job.image : job.image + 1, CH:] = sum_b
        yield
        total = jnp.zeros((8, CH), F32)
        for at in job.chunks():
            grad = final(at)
            total = total + fold(grad)
            turn(at.start, grad, 1)
        add_vec(base + 2, over_rows(total))
        yield
        conv_in(2 * number)
        yield
        sum_b, sum_g, final = act_sums(("a", number), job.hid.at[number], vec(base), vec(base + 1), True)
        conv_matrix(2 * number, 1)
        add_vec(base, sum_g)
        add_vec(base + 1, sum_b)
        yield

    total = jnp.zeros((80, CH), F32)
    for at in job.blocks():
        high, low = split(dhid[at, :] + final(at))
        wide = mm(job.x80[:, at], high)
        total = total + wide[0:80] + wide[80:160] + mm(job.x80[0:80, at], low)
    net.gin[...] += total
    yield


def together(passes):
    passes = list(passes)
    while passes:
        for one in list(passes):
            try:
                next(one)
            except StopIteration:
                passes.remove(one)


def later(one, steps):
    for _ in range(steps):
        yield
    yield from one


def net_kernel(
    owner_ref,
    number_ref,
    big_level_ref,
    small_level_ref,
    table_ref,
    big_ref,
    big_noise_ref,
    small_ref,
    small_noise_ref,
    mask_ref,
    vec_ref,
    whole_ref,
    grads_ref,
    conv_w,
    time_w,
    triple_w,
    proj_w,
    conv_g,
    triple_g,
    proj_g,
    tsh,
    gtime,
    gin_ref,
    ghead_ref,
    loss_ref,
    emb_ref,
    vin_ref,
    head_ref,
    gvec_ref,
    piece_ref,
    tile_ref,
    piece_low,
    load_sem,
    store_sem,
    piece_sem,
    *job_refs,
):
    bigs = big_ref.shape[0] // 2
    smalls = small_ref.shape[0] // 2
    count = bigs + smalls
    pair = lax.axis_index("pair")
    devices, shard_rows = grads_ref.shape[0], grads_ref.shape[1]
    per_device = shard_rows // BLOCK

    parts = {}
    for number in range(2):
        parts["time", number] = [
            (TIME_FIRST + TIME_COUNT * number + k, time_w.at[number], k // 4, k % 4) for k in range(TIME_COUNT)
        ]
    for m in range(4):
        parts[m] = [(m * CONV_BLOCKS + k, conv_w.at[m], k // 2, k % 2) for k in range(CONV_BLOCKS)]
    parts["triple"] = [(TRIPLE_FIRST + k, triple_w, k // 6, k % 6) for k in range(TRIPLE_COUNT)]
    parts["proj"] = [(PROJ_FIRST + k, proj_w, k // 2, k % 2) for k in range(PROJ_COUNT)]
    sem_of = {key: k for k, key in enumerate(parts)}

    def block(ref, i, j):
        return ref.at[i * BLOCK : (i + 1) * BLOCK, j * BLOCK : (j + 1) * BLOCK]

    def load(key):
        for index, ref, i, j in parts[key]:
            pltpu.make_async_copy(whole_ref.at[owner_ref[index]], block(ref, i, j), load_sem.at[sem_of[key]]).start()

    def wait_load(key):
        ref = parts[key][0][1]
        pltpu.make_async_copy(ref, ref, load_sem.at[sem_of[key]]).wait()

    def store(key):
        for index, ref, i, j in parts[key]:
            slot = owner_ref[index]
            home = slot // per_device
            row = pl.multiple_of((slot - home * per_device) * BLOCK, BLOCK)
            target = grads_ref.at[home, pl.ds(row, BLOCK), :]
            pltpu.make_async_copy(block(ref, i, j), target, store_sem.at[sem_of[key]]).start()

    def wait_store(key):
        ref = parts[key][0][1]
        pltpu.make_async_copy(ref, ref, store_sem.at[sem_of[key]]).wait()

    for key in parts:
        load(key)

    gvec_ref[...] = jnp.zeros_like(gvec_ref)
    gin_ref[...] = jnp.zeros_like(gin_ref)
    ghead_ref[...] = jnp.zeros_like(ghead_ref)
    loss_ref[...] = jnp.zeros_like(loss_ref)
    gtime[...] = jnp.zeros_like(gtime)

    vin_ref[...] = jnp.zeros_like(vin_ref)
    head_ref[...] = jnp.zeros_like(head_ref)
    for tap in range(9):
        vin_ref[8 * tap : 8 * tap + 3, :] = vec_ref[3 * tap : 3 * tap + 3, :]
        head_ref[8 * tap : 8 * tap + 3, :] = vec_ref[47 + 3 * tap : 50 + 3 * tap, :]
    vin_ref[72:73, :] = vec_ref[27:28, :]

    levels = [big_level_ref[pair * bigs + k] for k in range(bigs)]
    levels += [small_level_ref[pair * smalls + k] for k in range(smalls)]
    emb_ref[...] = jnp.zeros_like(emb_ref)
    for k in range(count):
        for which in range(2):
            emb_ref[2 * k + which : 2 * k + which + 1, :] = table_ref[pl.ds(levels[k] + which, 1), :]

    net = Shared()
    vin_hi, vin_lo = split(vin_ref[...])
    net.vin3 = jnp.concatenate([vin_hi, vin_lo, vin_hi], axis=0)
    head_hi, head_lo = split(head_ref[...])
    net.head_hi = head_hi
    net.head2 = jnp.concatenate([head_hi, head_lo], axis=0)
    net.head3 = jnp.concatenate([head_hi, head_lo, head_hi], axis=0)
    group_row = lax.broadcasted_iota(jnp.int32, (CH, CH), 0) >> 3
    group_col = lax.broadcasted_iota(jnp.int32, (CH, CH), 1) >> 3
    net.ones = jnp.where(group_row == group_col, 1.0, 0.0).astype(BF16)
    net.conv_w, net.triple_w, net.proj_w = conv_w, triple_w, proj_w
    net.conv_g, net.triple_g, net.proj_g = conv_g, triple_g, proj_g
    net.gvec, net.gin, net.ghead, net.loss, net.gtime = gvec_ref, gin_ref, ghead_ref, loss_ref, gtime
    net.vec = lambda row: vec_ref[row : row + 1, :]
    net.scal = lambda job, which, item: number_ref[(levels[job.image] + which) * 8 + item]

    def shifts(job, which, number):
        row = tsh[number, 2 * job.image + which : 2 * job.image + which + 1, :]
        return row[:, 0:CH], row[:, CH:]

    net.shifts = shifts
    loaded = set()

    def ready(what):
        if what == 0:
            keys = (("time", 0), ("time", 1), 0)
        else:
            keys = ("triple", "proj") if what == "attention" else (what,)
        for key in keys:
            if key not in loaded:
                loaded.add(key)
                wait_load(key)
                if isinstance(key, tuple):
                    tsh[key[1]] = mm(emb_ref[...].astype(BF16), time_w[key[1]])

    net.ready = ready

    def put_conv(number, dy, value):
        for i in range(6):
            row = (dy * 6 + i) * BLOCK
            for j in range(2):
                conv_w[number, row : row + BLOCK, j * BLOCK : (j + 1) * BLOCK] = value[
                    j * BLOCK : (j + 1) * BLOCK, i * BLOCK : (i + 1) * BLOCK
                ].astype(BF16)

    def put_triple(part, value):
        for j in range(2):
            for i in range(2):
                column = part * CH + j * BLOCK
                triple_w[i * BLOCK : (i + 1) * BLOCK, column : column + BLOCK] = value[
                    j * BLOCK : (j + 1) * BLOCK, i * BLOCK : (i + 1) * BLOCK
                ].astype(BF16)

    def put_proj(value):
        net.proj_value = value

    def send(key):
        if key == "proj":
            for i in range(2):
                for j in range(2):
                    proj_w[i * BLOCK : (i + 1) * BLOCK, j * BLOCK : (j + 1) * BLOCK] = net.proj_value[
                        j * BLOCK : (j + 1) * BLOCK, i * BLOCK : (i + 1) * BLOCK
                    ].astype(BF16)
        store(key)

    net.put_conv, net.put_triple, net.put_proj, net.send = put_conv, put_triple, put_proj, send

    big_jobs = [Job(k, pair * bigs + k, big_ref, big_noise_ref, None, SIDE, job_refs[:JOB_REFS]) for k in range(bigs)]
    small_jobs = [
        Job(bigs + k, pair * smalls + k, small_ref, small_noise_ref, mask_ref, SMALL_SIDE, job_refs[JOB_REFS:]) for k in range(smalls)
    ]
    net.begun = set()
    turns = [big_jobs[k : k + 1] + small_jobs[k : k + 1] for k in range(max(bigs, smalls))]
    if len(turns[-1]) > 1:
        turns[-1:] = [turns[-1][1:], turns[-1][:1]]
    for k, jobs in enumerate(turns):
        together(later(forward_pass(job, which, net), which) for job in jobs for which in range(2))
        together(backward_pass(job, net, k == len(turns) - 1) for job in jobs)

    emb = emb_ref[...]
    mine = jnp.concatenate(
        [emb[2 * k + 1 : 2 * k + 2] for k in range(count)] + [jnp.zeros((gtime.shape[1] - count, CH), F32)], axis=0
    ).astype(BF16)
    for number in range(2):
        value = mm_tn(gtime[number].astype(BF16), mine)
        for k in range(TIME_COUNT):
            i, j = k // 4, k % 4
            time_w[number, i * BLOCK : (i + 1) * BLOCK, j * BLOCK : (j + 1) * BLOCK] = value[
                j * BLOCK : (j + 1) * BLOCK, i * BLOCK : (i + 1) * BLOCK
            ].astype(BF16)
        store(("time", number))

    for tap in range(9):
        gvec_ref[3 * tap : 3 * tap + 3, :] = gin_ref[8 * tap : 8 * tap + 3, :]
        gvec_ref[47 + 3 * tap : 50 + 3 * tap, :] = ghead_ref[8 * tap : 8 * tap + 3, :]
    gvec_ref[27:28, :] = gin_ref[72:73, :]
    gvec_ref[74:75, :] = loss_ref[0:1, :]
    piece_ref[...] = jnp.zeros_like(piece_ref)
    tile_ref[0:80, :] = gvec_ref[:, 0:BLOCK]
    tile_ref[80:160, :] = gvec_ref[:, BLOCK:]
    rows = piece_rows(devices)
    for k in range(-(-160 // rows)):
        end = min(160, (k + 1) * rows)
        piece_ref[k, 0 : end - k * rows, :] = tile_ref[k * rows : end, :]
    value = piece_ref[...]
    high = value.astype(BF16).astype(F32)
    piece_low[...] = jnp.concatenate([high, value - high], axis=1).astype(BF16)
    keep = pltpu.make_async_copy(piece_low, grads_ref.at[:, pl.ds(per_device * BLOCK, 16), :], piece_sem)
    keep.start()
    keep.wait()
    for key in parts:
        wait_store(key)


def network_grads(owner_map, numbers, table, big_level, small_level, big, big_noise, small, small_noise, mask, vectors, whole, devices):
    per_device = whole.shape[0] // devices
    images = -(-(big.shape[0] + small.shape[0]) // 16) * 16
    vmem = pl.BlockSpec(memory_space=pltpu.VMEM)
    smem = pl.BlockSpec(memory_space=pltpu.SMEM)
    hbm = pl.BlockSpec(memory_space=ANY)
    return pl.pallas_call(
        net_kernel,
        out_shape=jax.ShapeDtypeStruct((devices, per_device * BLOCK + 16, BLOCK), BF16),
        in_specs=[smem] * 4 + [vmem] * 7 + [hbm],
        out_specs=hbm,
        scratch_shapes=[
            pltpu.VMEM((4, 9 * CH, CH), BF16),
            pltpu.VMEM((2, CH, 2 * CH), BF16),
            pltpu.VMEM((CH, 3 * CH), BF16),
            pltpu.VMEM((CH, CH), BF16),
            pltpu.VMEM((4, CH, 9 * CH), F32),
            pltpu.VMEM((3 * CH, CH), F32),
            pltpu.VMEM((CH, CH), F32),
            pltpu.VMEM((2, images, 2 * CH), F32),
            pltpu.VMEM((2, images, 2 * CH), F32),
            pltpu.VMEM((80, CH), F32),
            pltpu.VMEM((80, CH), F32),
            pltpu.VMEM((8, CH), F32),
            pltpu.VMEM((images, CH), F32),
            pltpu.VMEM((80, CH), F32),
            pltpu.VMEM((80, CH), F32),
            pltpu.VMEM((80, CH), F32),
            pltpu.VMEM((devices, 8, BLOCK), F32),
            pltpu.VMEM((160, BLOCK), F32),
            pltpu.VMEM((devices, 16, BLOCK), BF16),
            pltpu.SemaphoreType.DMA((8,)),
            pltpu.SemaphoreType.DMA((8,)),
            pltpu.SemaphoreType.DMA,
        ]
        + job_scratch(SIDE)
        + job_scratch(SMALL_SIDE),
        compiler_params=pltpu.CompilerParams(vmem_limit_bytes=62 * 1024 * 1024),
        cost_estimate=pl.CostEstimate(flops=57 * 10**9, bytes_accessed=20 * 10**6, transcendentals=10**7),
    )(owner_map, numbers, big_level, small_level, table, big, big_noise, small, small_noise, mask, vectors, whole)


MESH_ID = pl.DeviceIdType.MESH


def where_am_i():
    dp = lax.axis_index("dp")
    return lax.axis_index("pair"), dp // 4, (dp // 2) % 2, dp % 2


def device(pair, line, mid, core):
    return (pair, (line * 2 + mid) * 2 + core)


def neighbours():
    pair, line, mid, core = where_am_i()
    flip_pair, flip_mid = 1 - 2 * pair, 1 - 2 * mid
    second = device(pair + (1 - core) * flip_pair, line, mid + core * flip_mid, core)
    third = device(pair + core * flip_pair, line, mid + (1 - core) * flip_mid, core)
    sibling = device(pair, line, mid, 1 - core)
    at_second = (1 - core) * pair + core * mid
    at_third = core * pair + (1 - core) * mid
    return pair, line, mid, core, at_second, at_third, second, third, sibling


def greet(lines, devices, lower, upper, line):
    barrier = pltpu.get_barrier_semaphore()
    for other in devices:
        pl.semaphore_signal(barrier, inc=1, device_id=other, device_id_type=MESH_ID)
    for there, other in ((lower >= 0, lower), (upper < lines, upper)):

        @pl.when(there)
        def _(other=other):
            pl.semaphore_signal(barrier, inc=1, device_id=line(other), device_id_type=MESH_ID)

    beside = jnp.where(lower >= 0, 1, 0) + jnp.where(upper < lines, 1, 0)
    pl.semaphore_wait(barrier, len(devices) + beside)


def gather_kernel(
    lines, blocks_ref, whole_ref, own, up_send, down_send, second_send, third_send, sib_send, line_recv, second_recv, third_recv, sib_recv, own_sem
):
    pair, line, mid, core, at_second, at_third, second, third, sibling = neighbours()
    count = blocks_ref.shape[0]
    group = 4 * lines
    upper = device(pair, line + 1, mid, core)
    lower = device(pair, line - 1, mid, core)

    def place(l, s, t, c):
        p = (1 - c) * s + c * t
        m = c * s + (1 - c) * t
        return whole_ref.at[pl.ds((p * group + (l * 2 + m) * 2 + c) * count, count)]

    def copy(source, target, send, recv, to):
        return pltpu.make_async_remote_copy(
            src_ref=source, dst_ref=target, send_sem=send, recv_sem=recv, device_id=to, device_id_type=MESH_ID
        )

    def to_sibling(l, s, t, source=None):
        where = place(l, s, t, core)
        p = (1 - core) * s + core * t
        m = core * s + (1 - core) * t
        index = l * 4 + p * 2 + m
        return copy(where if source is None else source, where, sib_send.at[index], sib_recv.at[index], sibling)

    def to_second(l, source=None):
        where = place(l, at_second, at_third, core)
        return copy(where if source is None else source, where, second_send.at[l], second_recv.at[l], second)

    def to_third(l, s, source=None):
        where = place(l, s, at_third, core)
        index = l * 2 + s
        return copy(where if source is None else source, where, third_send.at[index], third_recv.at[index], third)

    def to_upper(l, source=None):
        where = place(l, at_second, at_third, core)
        return copy(where if source is None else source, where, up_send.at[l], line_recv.at[l], upper)

    def to_lower(l, source=None):
        where = place(l, at_second, at_third, core)
        return copy(where if source is None else source, where, down_send.at[l], line_recv.at[l], lower)

    own[...] = blocks_ref[...].astype(BF16)
    greet(lines, (second, third, sibling), line - 1, line + 1, lambda l: device(pair, l, mid, core))

    @pl.when(line < lines - 1)
    def _():
        to_upper(line, own).start()

    @pl.when(line > 0)
    def _():
        to_lower(line, own).start()

    to_third(line, at_second, own).start()
    to_second(line, own).start()
    to_sibling(line, at_second, at_third, own).start()
    keep = pltpu.make_async_copy(own, place(line, at_second, at_third, core), own_sem)
    keep.start()

    def from_second(l):
        to_second(l).wait_recv()
        to_third(l, 1 - at_second).start()
        to_sibling(l, 1 - at_second, at_third).start()

    def from_line(l):
        to_upper(l).wait_recv()

        @pl.when((l < line) & (line < lines - 1))
        def _():
            to_upper(l).start()

        @pl.when((l > line) & (line > 0))
        def _():
            to_lower(l).start()

        to_second(l).start()
        to_third(l, at_second).start()
        to_sibling(l, at_second, at_third).start()

    def both(distance, carry):
        @pl.when(line - distance >= 0)
        def _():
            from_line(line - distance)

        @pl.when(line + distance < lines)
        def _():
            from_line(line + distance)

        @pl.when(line - distance + 1 >= 0)
        def _():
            from_second(line - distance + 1)

        @pl.when((line + distance - 1 < lines) & (distance > 1))
        def _():
            from_second(line + distance - 1)

        return carry

    lax.fori_loop(1, lines + 1, both, 0)

    def from_third(l, carry):
        for s in range(2):
            to_third(l, s).wait_recv()
            to_sibling(l, s, 1 - at_third).start()
        return carry

    lax.fori_loop(0, lines, from_third, 0)

    def finish(l, carry):
        @pl.when((l <= line) & (line < lines - 1))
        def _():
            to_upper(l).wait_send()

        @pl.when((l >= line) & (line > 0))
        def _():
            to_lower(l).wait_send()

        to_second(l).wait_send()
        for s in range(2):
            to_third(l, s).wait_send()
            for t in range(2):
                done = to_sibling(l, s, t)
                done.wait_send()
                done.wait_recv()
        return carry

    lax.fori_loop(0, lines, finish, 0)
    keep.wait()


def gather_blocks(blocks):
    lines = lax.axis_size("dp") // 4
    count = blocks.shape[0]
    total = count * lines * 8
    dma = pltpu.SemaphoreType.DMA
    return pl.pallas_call(
        partial(gather_kernel, lines),
        out_shape=jax.ShapeDtypeStruct((total, BLOCK, BLOCK), BF16),
        in_specs=[pl.BlockSpec(memory_space=pltpu.VMEM)],
        out_specs=pl.BlockSpec(memory_space=ANY),
        scratch_shapes=[
            pltpu.VMEM((count, BLOCK, BLOCK), BF16),
            dma((lines,)),
            dma((lines,)),
            dma((lines,)),
            dma((2 * lines,)),
            dma((4 * lines,)),
            dma((lines,)),
            dma((lines,)),
            dma((2 * lines,)),
            dma((4 * lines,)),
            dma,
        ],
        compiler_params=pltpu.CompilerParams(collective_id=0, has_side_effects=True),
        cost_estimate=pl.CostEstimate(flops=0, bytes_accessed=2 * total * BLOCK * BLOCK * 2, transcendentals=0),
    )(blocks)


def sum_kernel(
    lines,
    grads_ref,
    owner_ref,
    sum_ref,
    tiles_ref,
    mine,
    from_sib,
    from_third,
    from_second,
    from_lower,
    from_upper,
    tiles,
    load_sem,
    sib_send,
    third_send,
    second_send,
    up_send,
    down_send,
    sib_recv,
    third_recv,
    second_recv,
    up_recv,
    down_recv,
    near_send,
    near_recv,
    far_send,
    far_recv,
):
    pair, line, mid, core, at_second, at_third, second, third, sibling = neighbours()
    count = sum_ref.shape[0]
    main = count * BLOCK
    group = 4 * lines
    upper = device(pair, line + 1, mid, core)
    lower = device(pair, line - 1, mid, core)
    here = pair * 4 + mid * 2 + core

    def peer(k):
        return device(k // 4, line, (k // 2) % 2, k % 2)

    def on_line(l):
        return device(pair, l, mid, core)

    def copy(source, target, send, recv, to):
        return pltpu.make_async_remote_copy(
            src_ref=source, dst_ref=target, send_sem=send, recv_sem=recv, device_id=to, device_id_type=MESH_ID
        )

    def spot(l, s, t):
        return l * 4 + s * 2 + t

    def shard(l, s, t, c):
        p = (1 - c) * s + c * t
        m = c * s + (1 - c) * t
        return p * group + (l * 2 + m) * 2 + c

    def to_sibling(l, s, t):
        index = spot(l, s, t)
        return copy(grads_ref.at[shard(l, s, t, 1 - core)], from_sib.at[index], sib_send.at[index], sib_recv.at[index], sibling)

    def load(l, s, t):
        index = spot(l, s, t)
        return pltpu.make_async_copy(grads_ref.at[shard(l, s, t, core)], mine.at[index], load_sem.at[index])

    def to_third(l, s):
        index = l * 2 + s
        return copy(mine.at[spot(l, s, 1 - at_third)], from_third.at[index], third_send.at[index], third_recv.at[index], third)

    def to_second(l):
        return copy(mine.at[spot(l, 1 - at_second, at_third)], from_second.at[l], second_send.at[l], second_recv.at[l], second)

    def to_upper(l):
        return copy(mine.at[spot(l, at_second, at_third)], from_lower.at[l], up_send.at[l], up_recv.at[l], upper)

    def to_lower(l):
        return copy(mine.at[spot(l, at_second, at_third)], from_upper.at[l], down_send.at[l], down_recv.at[l], lower)

    barrier = pltpu.get_barrier_semaphore()
    for k in range(8):

        @pl.when(here != k)
        def _(k=k):
            pl.semaphore_signal(barrier, inc=1, device_id=peer(k), device_id_type=MESH_ID)

    def greet_line(l, carry):
        @pl.when(l != line)
        def _():
            pl.semaphore_signal(barrier, inc=1, device_id=on_line(l), device_id_type=MESH_ID)

        return carry

    lax.fori_loop(0, lines, greet_line, 0)
    pl.semaphore_wait(barrier, 7 + lines - 1)

    def far_first(function):
        def step(k, carry):
            distance = lines - 1 - k

            @pl.when(line + distance < lines)
            def _():
                function(line + distance)

            @pl.when((line - distance >= 0) & (distance > 0))
            def _():
                function(line - distance)

            return carry

        lax.fori_loop(0, lines, step, 0)

    def start_both(l, places):
        s_at, t_at, s_own, t_own = places
        to_sibling(l, s_at, t_at).start()
        load(l, s_own, t_own).start()

    sib_second, sib_third = at_third, at_second
    for s, t in ((1, 1), (0, 1), (1, 0), (0, 0)):
        places = (
            sib_second + s * (1 - 2 * sib_second),
            sib_third + t * (1 - 2 * sib_third),
            at_second + s * (1 - 2 * at_second),
            at_third + t * (1 - 2 * at_third),
        )
        far_first(partial(start_both, places=places))

    def read(ref, index):
        tile = ref[index, main:, :].astype(F32)
        return ref[index, 0:main, :].astype(F32), tile[0:8] + tile[8:16]

    def add(value, ref, index):
        other = read(ref, index)
        return value[0] + other[0], value[1] + other[1]

    def write(index, value):
        high = value[1].astype(BF16).astype(F32)
        mine[index, 0:main, :] = value[0].astype(BF16)
        mine[index, main:, :] = jnp.concatenate([high, value[1] - high], axis=0).astype(BF16)

    def both_cores(l, s, t):
        load(l, s, t).wait()
        to_sibling(l, s, t).wait_recv()
        index = spot(l, s, t)
        return add(read(mine, index), from_sib, index)

    def send_third(l, s):
        write(spot(l, s, 1 - at_third), both_cores(l, s, 1 - at_third))
        to_third(l, s).start()

    far_first(lambda l: send_third(l, 1 - at_second))
    far_first(lambda l: send_third(l, at_second))

    def with_third(l, s):
        total = both_cores(l, s, at_third)
        to_third(l, s).wait_recv()
        return add(total, from_third, l * 2 + s)

    def send_second(l):
        write(spot(l, 1 - at_second, at_third), with_third(l, 1 - at_second))
        to_second(l).start()

    far_first(send_second)

    def with_second(l):
        total = with_third(l, at_second)
        to_second(l).wait_recv()
        return add(total, from_second, l)

    def send_line(k, carry):
        distance = lines - 1 - k
        above = line + distance
        below = line - distance

        @pl.when(above < lines)
        def _():
            index = spot(above, at_second, at_third)
            write(index, with_second(above))

            @pl.when(line > 0)
            def _():
                to_upper(above).wait_recv()
                write(index, add(read(mine, index), from_lower, above))

            to_upper(above).start()

        @pl.when(below >= 0)
        def _():
            index = spot(below, at_second, at_third)
            write(index, with_second(below))

            @pl.when(line < lines - 1)
            def _():
                to_lower(below).wait_recv()
                write(index, add(read(mine, index), from_upper, below))

            to_lower(below).start()

        return carry

    lax.fori_loop(0, lines - 1, send_line, 0)
    blocks, piece = with_second(line)
    sum_ref[...] = blocks.reshape(count, BLOCK, BLOCK)
    tiles[line, here] = piece

    def last(ref):
        more, piece = read(ref, line)
        sum_ref[...] += more.reshape(count, BLOCK, BLOCK)
        tiles[line, here] += piece

    @pl.when(line > 0)
    def _():
        to_upper(line).wait_recv()
        last(from_lower)

    @pl.when(line < lines - 1)
    def _():
        to_lower(line).wait_recv()
        last(from_upper)

    square = jnp.zeros((8, BLOCK), F32)
    for k in range(count):
        slot = (pair * group + (line * 2 + mid) * 2 + core) * count + k
        held = jnp.max(jnp.where(owner_ref[...] == slot, 1.0, 0.0), axis=1, keepdims=True)
        value = jnp.where(held > 0.0, sum_ref[k], 0.0)
        sum_ref[k] = value
        square = square + fold(value * value)
    at_last = lax.broadcasted_iota(jnp.int32, (8, BLOCK), 0) == 7
    tiles[line, here] = jnp.where(at_last, over_rows(square), tiles[line, here])

    def near(k):
        tile = tiles.at[line, here]
        return copy(tile, tile, near_send.at[k], near_recv.at[here], peer(k))

    def near_from(k):
        tile = tiles.at[line, k]
        return copy(tile, tile, near_send.at[k], near_recv.at[k], peer(k))

    def far(l):
        return copy(tiles.at[line], tiles.at[line], far_send.at[l], far_recv.at[line], on_line(l))

    def far_from(l):
        return copy(tiles.at[l], tiles.at[l], far_send.at[l], far_recv.at[l], on_line(l))

    def others(function):
        for k in range(8):

            @pl.when(here != k)
            def _(k=k):
                function(k)

    def other_lines(function):
        def step(l, carry):
            @pl.when(l != line)
            def _():
                function(l)

            return carry

        lax.fori_loop(0, lines, step, 0)

    others(lambda k: near(k).start())
    others(lambda k: near_from(k).wait_recv())
    other_lines(lambda l: far(l).start())

    def finish(l, carry):
        for s in range(2):
            for t in range(2):
                to_sibling(l, s, t).wait_send()
            to_third(l, s).wait_send()
        to_second(l).wait_send()

        @pl.when((l > line) & (line < lines - 1))
        def _():
            to_upper(l).wait_send()

        @pl.when((l < line) & (line > 0))
        def _():
            to_lower(l).wait_send()

        return carry

    lax.fori_loop(0, lines, finish, 0)
    others(lambda k: near(k).wait_send())
    other_lines(lambda l: far_from(l).wait_recv())
    other_lines(lambda l: far(l).wait_send())
    tiles_ref[...] = tiles[...]


def sum_by_slot(grads, owner_map):
    lines = lax.axis_size("dp") // 4
    rows = grads.shape[1]
    count = rows // BLOCK
    dma = pltpu.SemaphoreType.DMA
    vmem = pl.BlockSpec(memory_space=pltpu.VMEM)
    shard = (rows, BLOCK)
    return pl.pallas_call(
        partial(sum_kernel, lines),
        out_shape=(
            jax.ShapeDtypeStruct((count, BLOCK, BLOCK), F32),
            jax.ShapeDtypeStruct((lines, 8, 8, BLOCK), F32),
        ),
        in_specs=[pl.BlockSpec(memory_space=ANY), vmem],
        out_specs=(vmem, vmem),
        scratch_shapes=[
            pltpu.VMEM((4 * lines,) + shard, BF16),
            pltpu.VMEM((4 * lines,) + shard, BF16),
            pltpu.VMEM((2 * lines,) + shard, BF16),
            pltpu.VMEM((lines,) + shard, BF16),
            pltpu.VMEM((lines,) + shard, BF16),
            pltpu.VMEM((lines,) + shard, BF16),
            pltpu.VMEM((lines, 8, 8, BLOCK), F32),
            dma((4 * lines,)),
            dma((4 * lines,)),
            dma((2 * lines,)),
            dma((lines,)),
            dma((lines,)),
            dma((lines,)),
            dma((4 * lines,)),
            dma((2 * lines,)),
            dma((lines,)),
            dma((lines,)),
            dma((lines,)),
            dma((8,)),
            dma((8,)),
            dma((lines,)),
            dma((lines,)),
        ],
        compiler_params=pltpu.CompilerParams(collective_id=1, has_side_effects=True, vmem_limit_bytes=48 * 1024 * 1024),
        cost_estimate=pl.CostEstimate(flops=0, bytes_accessed=2 * grads.size * 2, transcendentals=0),
    )(grads, owner_map.reshape(1, -1))


def mm_exact(left, right, over):
    return lax.dot_general(left, right, (over, ((), ())), precision=HIGH, preferred_element_type=F32)


def update_kernel(
    sum_ref,
    tiles_ref,
    blocks_ref,
    moments_ref,
    left_ref,
    right_ref,
    left_root_ref,
    right_root_ref,
    vec_ref,
    vec_first_ref,
    vec_second_ref,
    loss_ref,
    norm_ref,
    new_blocks_ref,
    new_moments_ref,
    new_left_ref,
    new_right_ref,
    new_vec_ref,
    new_first_ref,
    new_second_ref,
    rows_ref,
):
    lines = tiles_ref.shape[0]
    piece = piece_rows(8 * lines)
    for line in range(lines):
        for k in range(8):
            shard = (k // 4) * 4 * lines + (line * 2 + (k // 2) % 2) * 2 + k % 2
            rows_ref[shard * piece : (shard + 1) * piece, :] = tiles_ref[line, k, 0:piece, :]
    count = vec_ref.shape[0]
    grads = jnp.concatenate([rows_ref[0:80, :], rows_ref[80:160, :]], axis=1)
    loss_ref[0, 0] = jnp.max(grads[74:75, :])
    vec_grad = grads[0:count]
    square = jnp.sum(tiles_ref[...].reshape(64 * lines, BLOCK).reshape(8 * lines, 8, BLOCK)[:, 7, :])
    total = jnp.full((1, 1), square + jnp.sum(vec_grad * vec_grad), F32)
    norm = jnp.sqrt(total)
    norm_ref[0, 0] = jnp.max(norm)
    factor = jnp.minimum(1.0, CLIP / (norm + 1e-06))

    for k in range(sum_ref.shape[0]):
        turned_grad = sum_ref[k] * factor
        first = BETA_ONE * moments_ref[k] + (1 - BETA_ONE) * jnp.transpose(turned_grad)
        new_moments_ref[k] = first
        new_left_ref[k] = BETA_TWO * left_ref[k] + (1 - BETA_TWO) * mm_exact(turned_grad, turned_grad, ((0,), (0,)))
        new_right_ref[k] = BETA_TWO * right_ref[k] + (1 - BETA_TWO) * mm_exact(turned_grad, turned_grad, ((1,), (1,)))
        turned = mm_exact(left_root_ref[k], first, ((1,), (0,)))
        turned = mm_exact(turned, right_root_ref[k], ((1,), (0,)))
        mean = jnp.sum(over_rows(fold(turned * turned)), axis=1, keepdims=True) * (1.0 / BLOCK**2)
        master = blocks_ref[k]
        new_blocks_ref[k] = master - RATE_MATRIX * (turned * (1.0 / jnp.sqrt(mean + 1e-20)) + DECAY * master)

    grad = vec_grad * factor
    params = vec_ref[...]
    first = BETA_ONE * vec_first_ref[...] + (1 - BETA_ONE) * grad
    second = BETA_TWO * vec_second_ref[...] + (1 - BETA_TWO) * grad * grad
    fixed_first = first * (1.0 / (1 - BETA_ONE**STEP))
    fixed_second = second * (1.0 / (1 - BETA_TWO**STEP))
    new_vec_ref[...] = params - RATE_VECTOR * (fixed_first / (jnp.sqrt(fixed_second) + 1e-08) + DECAY * params)
    new_first_ref[...] = first
    new_second_ref[...] = second


def piece_rows(devices):
    return -(-160 // devices)


def update(summed, tiles, blocks, moments, left_stats, right_stats, left_roots, right_roots, vectors, vec_first, vec_second):
    vmem = pl.BlockSpec(memory_space=pltpu.VMEM)
    smem = pl.BlockSpec(memory_space=pltpu.SMEM)
    devices = 8 * tiles.shape[0]
    like = lambda value: jax.ShapeDtypeStruct(value.shape, F32)
    scalar = jax.ShapeDtypeStruct((1, 1), F32)
    return pl.pallas_call(
        update_kernel,
        out_shape=(scalar, scalar) + (like(blocks),) * 4 + (like(vectors),) * 3,
        in_specs=[vmem] * 11,
        out_specs=(smem, smem) + (vmem,) * 7,
        scratch_shapes=[pltpu.VMEM((max(160, devices * piece_rows(devices)), BLOCK), F32)],
        compiler_params=pltpu.CompilerParams(vmem_limit_bytes=48 * 1024 * 1024),
        cost_estimate=pl.CostEstimate(flops=10**9, bytes_accessed=6 * 10**6, transcendentals=10**5),
    )(summed, tiles, blocks, moments, left_stats, right_stats, left_roots, right_roots, vectors, vec_first, vec_second)


def sigma_of(level):
    lowest = SIGMA_MIN ** (1.0 / RHO)
    highest = SIGMA_MAX ** (1.0 / RHO)
    return (lowest + level / (NSTEPS - 1) * (highest - lowest)) ** RHO


def level_tables():
    level = np.arange(NSTEPS, dtype=np.float64)
    sigma = sigma_of(level)
    inner = 1.0 / np.sqrt(sigma**2 + SIGMA_DATA**2)
    skip = SIGMA_DATA**2 / ((sigma - SIGMA_MIN) ** 2 + SIGMA_DATA**2)
    outer = (sigma - SIGMA_MIN) * SIGMA_DATA * inner
    rate = 1.0 / (sigma_of(level + 1) - sigma)
    numbers = np.stack([sigma, inner, skip, outer, rate] + [np.zeros_like(sigma)] * 3, axis=1).reshape(-1)
    half = CH // 2
    phase = np.log(sigma)[:, None] / 4.0 * np.exp(np.arange(half) * (math.log(100.0) / (half - 1)))
    embed = np.zeros((16, CH))
    embed[:NSTEPS] = np.concatenate([np.sin(phase), np.cos(phase)], axis=1)
    return numbers.astype(np.float32), embed.astype(np.float32)


def local(
    big_images,
    big_noise,
    small_images,
    small_noise,
    big_level,
    small_level,
    small_mask,
    owner_map,
    blocks,
    moments,
    left_stats,
    right_stats,
    left_roots,
    right_roots,
    vectors,
    vec_first,
    vec_second,
):
    whole = gather_blocks(blocks)
    numbers, table = level_tables()
    grads = network_grads(
        owner_map,
        jnp.asarray(numbers),
        jnp.asarray(table),
        big_level,
        small_level,
        big_images,
        big_noise,
        small_images,
        small_noise,
        small_mask,
        vectors,
        whole,
        lax.axis_size("pair") * lax.axis_size("dp"),
    )
    summed, tiles = sum_by_slot(grads, owner_map)
    loss, norm, *rest = update(
        summed, tiles, blocks, moments, left_stats, right_stats, left_roots, right_roots, vectors, vec_first, vec_second
    )
    return (loss.reshape(()), norm.reshape(()), *rest)


def solution(mesh):
    by_slot = P(("pair", "dp"), None, None)
    by_image = P("dp", None, None)
    placed = (by_image,) * 4 + (P("dp"), P("dp"), P("dp", None), P()) + (by_slot,) * 6 + (P(),) * 3
    return jax.shard_map(
        local,
        mesh=mesh,
        in_specs=placed,
        out_specs=(P(), P()) + (by_slot,) * 4 + (P(),) * 3,
        check_vma=False,
    )
```

```python
from functools import partial
import math

import jax
import jax.numpy as jnp
from jax import lax
from jax.experimental import pallas as pl
from jax.experimental.pallas import tpu as pltpu
from jax.sharding import PartitionSpec as P
import numpy as np

GROUPS = 32
SIDE = 32
SMALL_SIDE = 16
NSTEPS = 11
STEP = 10
CH = 256
BLOCK = 128

HIGH = lax.Precision.HIGHEST
SIGMA_DATA = 0.5
SIGMA_MIN = 0.002
SIGMA_MAX = 80.0
RHO = 7.0
HUBER = 0.00054
CLIP = 1.0
BETA_ONE = 0.9
BETA_TWO = 0.999
DECAY = 0.0001
RATE_MATRIX = 0.02
RATE_VECTOR = 0.02
ROOT_HALF = 1.0 / math.sqrt(2.0)
ANY = pl.ANY
F32 = jnp.float32
BF16 = jnp.bfloat16

CONV_BLOCKS = 36
TIME_FIRST, TIME_COUNT = 144, 8
TRIPLE_FIRST, TRIPLE_COUNT = 160, 12
PROJ_FIRST, PROJ_COUNT = 172, 4

ROWS = 128
MM_ROWS = 256
SKEW = 2


def mm(left, right):
    return jnp.dot(left, right, preferred_element_type=F32)


def mm_nt(left, right):
    return lax.dot_general(left, right, (((1,), (1,)), ((), ())), preferred_element_type=F32)


def mm_tn(left, right):
    return lax.dot_general(left, right, (((0,), (0,)), ((), ())), preferred_element_type=F32)


def split(value):
    high = value.astype(BF16)
    return high, (value - high.astype(F32)).astype(BF16)


def fold(value):
    return jnp.sum(value.reshape(value.shape[0] // 8, 8, value.shape[1]), axis=0)


def over_rows(value):
    return jnp.sum(value, axis=0, keepdims=True)


def group_mean(value, ones):
    high = value.astype(BF16).astype(F32)
    rest = value - high
    middle = rest.astype(BF16).astype(F32)
    parts = jnp.concatenate([high, middle, rest - middle, jnp.zeros_like(value)], axis=0).astype(BF16)
    sums = mm(parts, ones)
    return (sums[0:8] + sums[8:16] + sums[16:24]) * 0.125


def sigmoid(value):
    return 0.5 + 0.5 * jnp.tanh(0.5 * value)


def group_stats(ref, pixels, ones):
    total = jnp.zeros((8, CH), F32)
    for row in range(0, pixels, ROWS):
        total = total + fold(ref[row : row + ROWS, :])
    own = jnp.broadcast_to(over_rows(total) * (1.0 / pixels), (8, CH))
    mean = group_mean(own, ones)
    total = jnp.zeros((8, CH), F32)
    for row in range(0, pixels, ROWS):
        center = ref[row : row + ROWS, :] - own[0:1]
        total = total + fold(center * center)
    within = jnp.broadcast_to(over_rows(total) * (1.0 / pixels), (8, CH))
    between = own - mean
    spread = group_mean(within + between * between, ones)
    return mean[0:1], lax.rsqrt(spread[0:1] + 1e-06)


def write_shifted(ref, row, value, side):
    count = value.shape[0]
    column = lax.broadcasted_iota(jnp.int32, (count, CH), 0) & (side - 1)
    left = jnp.where(column == 0, 0.0, pltpu.roll(value, 1, 0))
    right = jnp.where(column == side - 1, 0.0, pltpu.roll(value, count - 1, 0))
    at = slice(side + row, side + row + count)
    ref[at, 0:CH] = left.astype(BF16)
    ref[at, CH : 2 * CH] = value.astype(BF16)
    ref[at, 2 * CH : 3 * CH] = right.astype(BF16)


def clear_ends(ref, side):
    pixels = side * side
    zeros = jnp.zeros((side, 3 * CH), BF16)
    ref[0:side, :] = zeros
    ref[side + pixels : 2 * side + pixels, :] = zeros


def tap_shifts(side):
    pixels = side * side
    place = lax.broadcasted_iota(jnp.int32, (8, pixels), 1)
    x = place & (side - 1)
    y = place >> (side.bit_length() - 1)
    taps = []
    for dy in (-1, 0, 1):
        for dx in (-1, 0, 1):
            inside = (x + dx >= 0) & (x + dx < side) & (y + dy >= 0) & (y + dy < side)
            taps.append((dy * side + dx, inside))
    return taps


class Shared:
    pass


class Job:
    def __init__(self, image, local, clean, noise, mask, side, refs):
        self.image, self.local, self.clean, self.noise, self.mask, self.side = image, local, clean, noise, mask, side
        self.pixels = side * side
        self.rows = min(ROWS, self.pixels)
        self.mrows = min(MM_ROWS, self.pixels)
        (
            self.hid,
            self.first,
            self.pat,
            self.gpat,
            self.grad_t,
            self.expo,
            self.dscore,
            self.keep,
            self.value_t,
            self.key_t,
            self.normed,
            self.mixed,
            self.mixed_t,
            self.rinv,
            self.act_hi,
            self.act_lo,
            self.dhid,
            self.dact,
            self.dtri,
            self.x80,
            self.scaled,
            self.dnext,
        ) = refs
        self.stats = {}
        self.outs = [None, None]
        self.noisy = [None, None]

    def chunks(self):
        return [slice(row, row + self.rows) for row in range(0, self.pixels, self.rows)]

    def blocks(self):
        return [slice(row, row + self.mrows) for row in range(0, self.pixels, self.mrows)]

    def hid_of(self, which, level):
        return self.hid.at[level] if which else self.dhid

    def first_of(self, which, number):
        return self.first.at[number] if which else self.dact

    def pat_of(self, which, number):
        return self.pat.at[number] if which else self.gpat

    def keep_of(self, which, part):
        return self.keep.at[part] if which else self.dtri.at[part]

    def expo_of(self, which):
        return self.expo if which else self.dscore

    def value_t_of(self, which):
        return self.value_t if which else self.grad_t.at[0]


def job_scratch(side):
    pixels = side * side
    tall = pixels + 2 * side
    return [
        pltpu.VMEM((4, pixels, CH), F32),
        pltpu.VMEM((2, pixels, CH), F32),
        pltpu.VMEM((4, tall, 3 * CH), BF16),
        pltpu.VMEM((tall, 3 * CH), BF16),
        pltpu.VMEM((3, CH, pixels), BF16),
        pltpu.VMEM((pixels, pixels), BF16),
        pltpu.VMEM((pixels, pixels), BF16),
        pltpu.VMEM((3, pixels, CH), BF16),
        pltpu.VMEM((CH, pixels), BF16),
        pltpu.VMEM((CH, pixels), BF16),
        pltpu.VMEM((pixels, CH), BF16),
        pltpu.VMEM((pixels, CH), BF16),
        pltpu.VMEM((CH, pixels), F32),
        pltpu.VMEM((8, pixels), F32),
        pltpu.VMEM((pixels, CH), BF16),
        pltpu.VMEM((pixels, CH), BF16),
        pltpu.VMEM((pixels, CH), F32),
        pltpu.VMEM((pixels, CH), F32),
        pltpu.VMEM((3, pixels, CH), BF16),
        pltpu.VMEM((160, pixels), BF16),
        pltpu.VMEM((pixels, CH), BF16),
        pltpu.VMEM((pixels, CH), F32),
    ]


JOB_REFS = 22


def forward_pass(job, which, net):
    vec, side, pixels = net.vec, job.side, job.pixels
    taps = tap_shifts(side)

    def scal(item):
        return net.scal(job, which, item)

    at = pl.ds(job.local, 1)
    noisy = [job.clean[channel, at, :] + scal(0) * job.noise[channel, at, :] for channel in range(3)]
    noisy = jnp.concatenate(noisy + [jnp.zeros((5, pixels), F32)], axis=0)
    job.noisy[which] = noisy
    scaled = noisy * scal(1)
    parts = [jnp.where(inside, pltpu.roll(scaled, (-shift) % pixels, 1), 0.0) for shift, inside in taps]
    parts.append(jnp.where(lax.broadcasted_iota(jnp.int32, (8, pixels), 0) == 0, 1.0, 0.0))
    high, low = split(jnp.concatenate(parts, axis=0))
    if which:
        job.x80[0:80, :] = high
        job.x80[80:160, :] = low
        for k in range(4):
            clear_ends(job.pat.at[k], side)
    else:
        clear_ends(job.gpat, side)
    job.hid_of(which, 0)[...] = mm_tn(jnp.concatenate([high, high, low], axis=0), net.vin3)
    yield

    def act_conv(key, src, gain, bias, dst, number, use):
        mean, rstd = group_stats(src, pixels, net.ones)
        job.stats[which, key] = (mean, rstd)
        scale = rstd * gain
        yield
        chunks = job.chunks()

        def put(until):
            while chunks and chunks[0].start < until:
                at = chunks.pop(0)
                z = (src[at, :] - mean) * scale + bias
                write_shifted(dst, at.start, z * sigmoid(z), side)

        put(job.mrows + side)
        net.ready(number)
        for at in job.blocks():
            put(at.stop + side)
            use(at, conv(dst, number, at.start))
            yield

    def conv(src, number, row):
        total = None
        for dy in range(3):
            start = dy * side + row
            part = mm(src[start : start + job.mrows, :], net.conv_w[number, dy * 768 : (dy + 1) * 768, :])
            total = part if total is None else total + part
        return total

    for number in range(2):
        base = 28 + 6 * number
        hid = job.hid_of(which, number)
        after = job.hid_of(which, number + 1)
        first = job.first_of(which, number)

        def use_first(at, value):
            first[at, :] = value + vec(base + 2)

        def use_second(at, value):
            after[at, :] = (hid[at, :] + (value + vec(base + 5))) * ROOT_HALF

        yield from act_conv(
            ("a", number), hid, vec(base), vec(base + 1), job.pat_of(which, 2 * number), 2 * number, use_first
        )
        gain_t, bias_t = net.shifts(job, which, number)
        yield from act_conv(
            ("b", number),
            first,
            1.0 + gain_t + vec(base + 3),
            bias_t + vec(base + 4),
            job.pat_of(which, 2 * number + 1),
            2 * number + 1,
            use_second,
        )

    net.ready("attention")
    src = job.hid_of(which, 2)
    mean, rstd = group_stats(src, pixels, net.ones)
    job.stats[which, "n"] = (mean, rstd)
    scale = rstd * vec(40)
    query, key, value_of = (job.keep_of(which, part) for part in range(3))
    value_t = job.value_t_of(which)
    for at in job.blocks():
        normed = ((src[at, :] - mean) * scale + vec(41)).astype(BF16)
        if which:
            job.normed[at, :] = normed
        triple = mm(normed, net.triple_w[...])
        query[at, :] = ((triple[:, 0:CH] + vec(42)) * (1.0 / math.sqrt(CH))).astype(BF16)
        key[at, :] = triple[:, CH : 2 * CH].astype(BF16)
        value = triple[:, 2 * CH :] + vec(43)
        value_of[at, :] = value.astype(BF16)
        value_t[:, at] = jnp.transpose(value).astype(BF16)
        if which:
            job.key_t[:, at] = (jnp.transpose(triple[:, CH : 2 * CH]) * (1.0 / math.sqrt(CH))).astype(BF16)
        yield
    expo = job.expo_of(which)
    scores = job.dnext if which else job.dact
    after = job.hid_of(which, 3)

    def mix(at, rinv):
        mixed_t = mm(value_t[...], expo[:, at]) * rinv
        mixed = jnp.transpose(mixed_t).astype(BF16)
        if which:
            job.rinv[:, at] = jnp.broadcast_to(rinv, (8, job.mrows))
            job.mixed_t[:, at] = mixed_t
            job.mixed[at, :] = mixed
        after[at, :] = (src[at, :] + (mm(mixed, net.proj_w[...]) + vec(44))) * ROOT_HALF

    before = None
    for at in job.blocks():
        scores[...] = mm_nt(key[...], query[at, :])
        if before is not None:
            mix(*before)
        yield
        top = jnp.max(scores[...], axis=0, keepdims=True)
        total = jnp.zeros((8, job.mrows), F32)
        for keys in job.chunks():
            weight = jnp.exp(scores[keys, :] - top)
            total = total + fold(weight)
            expo[keys, at] = weight.astype(BF16)
        before = (at, 1.0 / over_rows(total))
        yield
    mix(*before)
    yield
    mean, rstd = group_stats(after, pixels, net.ones)
    job.stats[which, "h"] = (mean, rstd)
    scale = rstd * vec(45)
    yield
    wide = []
    for at in job.blocks():
        z = (after[at, :] - mean) * scale + vec(46)
        high, low = split(z * sigmoid(z))
        if which:
            job.act_hi[at, :] = high
            job.act_lo[at, :] = low
        part = mm_nt(net.head2, high)
        wide.append(part[0:80] + part[80:160] + mm_nt(net.head_hi, low))
    wide = jnp.concatenate(wide, axis=1)
    out = jnp.zeros((8, pixels), F32)
    for k, (shift, inside) in enumerate(taps):
        out = out + jnp.where(inside, pltpu.roll(wide[8 * k : 8 * k + 8], (-shift) % pixels, 1), 0.0)
    job.outs[which] = scal(2) * noisy + scal(3) * out
    yield


def backward_pass(job, net, finish):
    vec, side, pixels = net.vec, job.side, job.pixels
    taps = tap_shifts(side)
    dact, dhid, gpat, grad_t = job.dact, job.dhid, job.gpat, job.grad_t

    def add_vec(row, value):
        net.gvec[row : row + 1, :] += value

    diff = job.outs[1] - job.outs[0]
    weighted = diff if job.mask is None else diff * job.mask[pl.ds(job.local, 1), :].astype(F32)
    bound = HUBER * math.sqrt(3 * pixels)
    total = jnp.sum(jnp.sum(weighted * diff, axis=1, keepdims=True), axis=0, keepdims=True)
    root = jnp.sqrt(total + bound * bound)
    rate = net.scal(job, 0, 4)
    net.loss[...] += jnp.broadcast_to((root - bound) * rate, (8, CH))
    dout = weighted * ((rate * net.scal(job, 1, 3)) / root)

    parts = [pltpu.roll(jnp.where(inside, dout, 0.0), shift % pixels, 1) for shift, inside in taps]
    parts.append(jnp.zeros((8, pixels), F32))
    high, low = split(jnp.concatenate(parts, axis=0))
    three = jnp.concatenate([high, high, low], axis=0)
    dact[...] = mm_tn(three, net.head3)
    wide = mm(jnp.concatenate([high, low], axis=0), job.act_hi[...])
    net.ghead[...] += wide[0:80] + wide[80:160] + mm(high, job.act_lo[...])
    yield

    def act_sums(key, src, gain, bias, active, beside=()):
        mean, rstd = job.stats[1, key]
        beside = list(beside)
        sum_b = jnp.zeros((8, CH), F32)
        sum_g = jnp.zeros((8, CH), F32)
        for index, at in enumerate(job.chunks()):
            value = (src[at, :] - mean) * rstd
            grad = dact[at, :]
            if active:
                z = value * gain + bias
                sig = sigmoid(z)
                grad = grad * (sig * (1.0 + z * (1.0 - sig)))
                dact[at, :] = grad
            sum_b = sum_b + fold(grad)
            sum_g = sum_g + fold(grad * value)
            if index % 3 == 2 and beside:
                beside.pop(0)()
        for more in beside:
            more()
        sum_b = over_rows(sum_b)
        sum_g = over_rows(sum_g)
        both = jnp.concatenate([sum_b * gain, sum_g * gain, jnp.zeros((6, CH), F32)], axis=0)
        means = group_mean(both, net.ones) * (1.0 / pixels)
        of_grad = rstd * gain
        of_value = rstd * rstd * means[1:2]
        constant = rstd * means[0:1]

        def final(at):
            return of_grad * dact[at, :] - (src[at, :] - mean) * of_value - constant

        return sum_b, sum_g, final

    sum_b, sum_g, final = act_sums("h", job.hid.at[3], vec(45), vec(46), True)
    add_vec(45, sum_g)
    add_vec(46, sum_b)
    yield
    total = jnp.zeros((8, CH), F32)
    for at in job.chunks():
        grad = final(at) * ROOT_HALF
        dhid[at, :] = grad
        total = total + fold(grad)
        gpat[at, 0:CH] = grad.astype(BF16)
        grad_t[0, :, at] = jnp.transpose(grad).astype(BF16)
    add_vec(44, over_rows(total))
    yield

    def wgrad(key, acc, at, value, last):
        if key in net.begun:
            value = value + acc[at]
        net.begun.add(key)
        if finish:
            last(value)
        else:
            acc[at] = value

    wgrad("proj", net.proj_g, (slice(None), slice(None)), mm(grad_t[0], job.mixed[...]), net.put_proj)
    total = jnp.zeros((8, CH), F32)
    query, key, value_of = (job.keep.at[part] for part in range(3))
    for at in job.blocks():
        out_t = mm_nt(net.proj_w[...], gpat[at, 0:CH])
        low_t = out_t.astype(BF16)
        inner = jnp.sum(low_t.astype(F32) * job.mixed_t[:, at], axis=0, keepdims=True)
        rinv = job.rinv[0:1, at]
        job.scaled[at, :] = jnp.transpose(out_t * rinv).astype(BF16)
        grad = mm(value_of[...], low_t)
        job.dscore[:, at] = (job.expo[:, at].astype(F32) * ((grad - inner) * rinv)).astype(BF16)
        dq_t = mm(job.key_t[...], job.dscore[:, at])
        dq = jnp.transpose(dq_t)
        total = total + fold(dq)
        job.dtri[0, at, :] = dq.astype(BF16)
        grad_t[0, :, at] = dq_t.astype(BF16)
        yield
    if finish:
        net.send("proj")
    add_vec(42, over_rows(total))
    total = jnp.zeros((8, CH), F32)
    for at in job.blocks():
        dk = mm(job.dscore[at, :], query[...])
        dv = mm(job.expo[at, :], job.scaled[...])
        total = total + fold(dv)
        job.dtri[1, at, :] = dk.astype(BF16)
        job.dtri[2, at, :] = dv.astype(BF16)
        grad_t[1, :, at] = jnp.transpose(dk).astype(BF16)
        grad_t[2, :, at] = jnp.transpose(dv).astype(BF16)
    add_vec(43, over_rows(total))
    yield
    for at in job.blocks():
        grad = None
        for part in range(3):
            more = mm_nt(job.dtri[part, at, :], net.triple_w[:, part * CH : (part + 1) * CH])
            grad = more if grad is None else grad + more
        dact[at, :] = grad
    for part in range(3):
        wgrad(
            ("triple", part),
            net.triple_g,
            (slice(part * CH, (part + 1) * CH), slice(None)),
            mm(grad_t[part], job.normed[...]),
            partial(net.put_triple, part),
        )
    if finish:
        net.send("triple")
    yield
    clear_ends(gpat, side)
    sum_b, sum_g, final = act_sums("n", job.hid.at[2], vec(40), vec(41), False)
    add_vec(40, sum_g)
    add_vec(41, sum_b)
    yield

    def conv_in(number, chunk_grad, slot):
        chunks = job.chunks()
        sums = [jnp.zeros((8, CH), F32)]

        def put(until):
            while chunks and chunks[0].start < until:
                at = chunks.pop(0)
                grad = chunk_grad(at)
                sums[0] = sums[0] + fold(grad)
                write_shifted(gpat, at.start, grad, side)
                grad_t[slot, :, at] = jnp.transpose(grad).astype(BF16)

        results = []
        for at in job.blocks():
            put(at.stop + side + job.rows)
            total = None
            for dy in range(3):
                for dx in range(3):
                    tap = dy * 3 + dx
                    start = (2 - dy) * side + at.start
                    part = mm_nt(
                        gpat[start : start + job.mrows, (2 - dx) * CH : (3 - dx) * CH],
                        net.conv_w[number, tap * CH : (tap + 1) * CH, :],
                    )
                    total = part if total is None else total + part
            job.dnext[at, :] = total
            yield
        sums_of[0] = over_rows(sums[0])

    sums_of = [None]

    def conv_matrix(number, slot):
        def one(dy):
            wgrad(
                (number, dy),
                net.conv_g,
                (number, slice(None), slice(dy * 768, (dy + 1) * 768)),
                mm(grad_t[slot], job.pat[number, dy * side : dy * side + pixels, :]),
                partial(net.put_conv, number, dy),
            )

        return [partial(one, dy) for dy in range(3)]

    for number in (1, 0):
        base = 28 + 6 * number

        def grad_second(at, final=final):
            grad = (dhid[at, :] + final(at)) * ROOT_HALF
            dhid[at, :] = grad
            return grad

        yield from conv_in(2 * number + 1, grad_second, 0)
        add_vec(base + 5, sums_of[0])
        dact, job.dnext = job.dnext, dact
        gain_t, bias_t = net.shifts(job, 1, number)
        sum_b, sum_g, final = act_sums(
            ("b", number),
            job.first.at[number],
            1.0 + gain_t + vec(base + 3),
            bias_t + vec(base + 4),
            True,
            conv_matrix(2 * number + 1, 0),
        )
        if finish:
            net.send(2 * number + 1)
        add_vec(base + 3, sum_g)
        add_vec(base + 4, sum_b)
        net.gtime[number, job.image : job.image + 1, 0:CH] = sum_g
        net.gtime[number, job.image : job.image + 1, CH:] = sum_b
        yield
        yield from conv_in(2 * number, final, 1)
        add_vec(base + 2, sums_of[0])
        dact, job.dnext = job.dnext, dact
        sum_b, sum_g, final = act_sums(
            ("a", number), job.hid.at[number], vec(base), vec(base + 1), True, conv_matrix(2 * number, 1)
        )
        if finish:
            net.send(2 * number)
        add_vec(base, sum_g)
        add_vec(base + 1, sum_b)
        yield

    total = jnp.zeros((80, CH), F32)
    for at in job.blocks():
        high, low = split(dhid[at, :] + final(at))
        wide = mm(job.x80[:, at], high)
        total = total + wide[0:80] + wide[80:160] + mm(job.x80[0:80, at], low)
    net.gin[...] += total
    yield


def together(passes):
    passes = list(passes)
    while passes:
        for one in list(passes):
            try:
                next(one)
            except StopIteration:
                passes.remove(one)


def later(one, steps):
    for _ in range(steps):
        yield
    yield from one


def net_kernel(
    owner_ref,
    number_ref,
    big_level_ref,
    small_level_ref,
    table_ref,
    big_ref,
    big_noise_ref,
    small_ref,
    small_noise_ref,
    mask_ref,
    vec_ref,
    whole_ref,
    grads_ref,
    conv_w,
    time_w,
    triple_w,
    proj_w,
    conv_g,
    triple_g,
    proj_g,
    tsh,
    gtime,
    gin_ref,
    ghead_ref,
    loss_ref,
    emb_ref,
    vin_ref,
    head_ref,
    gvec_ref,
    piece_ref,
    tile_ref,
    piece_low,
    load_sem,
    store_sem,
    piece_sem,
    *job_refs,
):
    bigs = big_ref.shape[1] // 2
    smalls = small_ref.shape[1] // 2
    count = bigs + smalls
    pair = lax.axis_index("pair")
    devices, shard_rows = grads_ref.shape[0], grads_ref.shape[1]
    per_device = shard_rows // BLOCK

    parts = {}
    for number in range(2):
        parts["time", number] = [
            (TIME_FIRST + TIME_COUNT * number + k, time_w.at[number], k // 4, k % 4) for k in range(TIME_COUNT)
        ]
    for m in range(4):
        parts[m] = [(m * CONV_BLOCKS + k, conv_w.at[m], k // 2, k % 2) for k in range(CONV_BLOCKS)]
    parts["triple"] = [(TRIPLE_FIRST + k, triple_w, k // 6, k % 6) for k in range(TRIPLE_COUNT)]
    parts["proj"] = [(PROJ_FIRST + k, proj_w, k // 2, k % 2) for k in range(PROJ_COUNT)]
    sem_of = {key: k for k, key in enumerate(parts)}

    def block(ref, i, j):
        return ref.at[i * BLOCK : (i + 1) * BLOCK, j * BLOCK : (j + 1) * BLOCK]

    def load(key):
        for index, ref, i, j in parts[key]:
            pltpu.make_async_copy(whole_ref.at[owner_ref[index]], block(ref, i, j), load_sem.at[sem_of[key]]).start()

    def wait_load(key):
        ref = parts[key][0][1]
        pltpu.make_async_copy(ref, ref, load_sem.at[sem_of[key]]).wait()

    def store(key):
        for index, ref, i, j in parts[key]:
            slot = owner_ref[index]
            home = slot // per_device
            row = pl.multiple_of((slot - home * per_device) * BLOCK, BLOCK)
            target = grads_ref.at[home, pl.ds(row, BLOCK), :]
            pltpu.make_async_copy(block(ref, i, j), target, store_sem.at[sem_of[key]]).start()

    def wait_store(key):
        ref = parts[key][0][1]
        pltpu.make_async_copy(ref, ref, store_sem.at[sem_of[key]]).wait()

    for key in parts:
        load(key)

    gvec_ref[...] = jnp.zeros_like(gvec_ref)
    gin_ref[...] = jnp.zeros_like(gin_ref)
    ghead_ref[...] = jnp.zeros_like(ghead_ref)
    loss_ref[...] = jnp.zeros_like(loss_ref)
    gtime[...] = jnp.zeros_like(gtime)

    vin_ref[...] = jnp.zeros_like(vin_ref)
    head_ref[...] = jnp.zeros_like(head_ref)
    for tap in range(9):
        vin_ref[8 * tap : 8 * tap + 3, :] = vec_ref[3 * tap : 3 * tap + 3, :]
        head_ref[8 * tap : 8 * tap + 3, :] = vec_ref[47 + 3 * tap : 50 + 3 * tap, :]
    vin_ref[72:73, :] = vec_ref[27:28, :]

    levels = [big_level_ref[pair * bigs + k] for k in range(bigs)]
    levels += [small_level_ref[pair * smalls + k] for k in range(smalls)]
    emb_ref[...] = jnp.zeros_like(emb_ref)
    for k in range(count):
        for which in range(2):
            emb_ref[2 * k + which : 2 * k + which + 1, :] = table_ref[pl.ds(levels[k] + which, 1), :]

    net = Shared()
    vin_hi, vin_lo = split(vin_ref[...])
    net.vin3 = jnp.concatenate([vin_hi, vin_lo, vin_hi], axis=0)
    head_hi, head_lo = split(head_ref[...])
    net.head_hi = head_hi
    net.head2 = jnp.concatenate([head_hi, head_lo], axis=0)
    net.head3 = jnp.concatenate([head_hi, head_lo, head_hi], axis=0)
    group_row = lax.broadcasted_iota(jnp.int32, (CH, CH), 0) >> 3
    group_col = lax.broadcasted_iota(jnp.int32, (CH, CH), 1) >> 3
    net.ones = jnp.where(group_row == group_col, 1.0, 0.0).astype(BF16)
    net.conv_w, net.triple_w, net.proj_w = conv_w, triple_w, proj_w
    net.conv_g, net.triple_g, net.proj_g = conv_g, triple_g, proj_g
    net.gvec, net.gin, net.ghead, net.loss, net.gtime = gvec_ref, gin_ref, ghead_ref, loss_ref, gtime
    net.vec = lambda row: vec_ref[row : row + 1, :]
    net.scal = lambda job, which, item: number_ref[(levels[job.image] + which) * 8 + item]

    def shifts(job, which, number):
        row = tsh[number, 2 * job.image + which : 2 * job.image + which + 1, :]
        return row[:, 0:CH], row[:, CH:]

    net.shifts = shifts
    loaded = set()

    def ready(what):
        if what == 0:
            keys = (("time", 0), ("time", 1), 0)
        else:
            keys = ("triple", "proj") if what == "attention" else (what,)
        for key in keys:
            if key not in loaded:
                loaded.add(key)
                wait_load(key)
                if isinstance(key, tuple):
                    tsh[key[1]] = mm(emb_ref[...].astype(BF16), time_w[key[1]])

    net.ready = ready

    def put_conv(number, dy, value):
        for i in range(6):
            row = (dy * 6 + i) * BLOCK
            for j in range(2):
                conv_w[number, row : row + BLOCK, j * BLOCK : (j + 1) * BLOCK] = value[
                    j * BLOCK : (j + 1) * BLOCK, i * BLOCK : (i + 1) * BLOCK
                ].astype(BF16)

    def put_triple(part, value):
        for j in range(2):
            for i in range(2):
                column = part * CH + j * BLOCK
                triple_w[i * BLOCK : (i + 1) * BLOCK, column : column + BLOCK] = value[
                    j * BLOCK : (j + 1) * BLOCK, i * BLOCK : (i + 1) * BLOCK
                ].astype(BF16)

    def put_proj(value):
        net.proj_value = value

    def send(key):
        if key == "proj":
            for i in range(2):
                for j in range(2):
                    proj_w[i * BLOCK : (i + 1) * BLOCK, j * BLOCK : (j + 1) * BLOCK] = net.proj_value[
                        j * BLOCK : (j + 1) * BLOCK, i * BLOCK : (i + 1) * BLOCK
                    ].astype(BF16)
        store(key)

    net.put_conv, net.put_triple, net.put_proj, net.send = put_conv, put_triple, put_proj, send

    big_jobs = [Job(k, pair * bigs + k, big_ref, big_noise_ref, None, SIDE, job_refs[:JOB_REFS]) for k in range(bigs)]
    small_jobs = [
        Job(bigs + k, pair * smalls + k, small_ref, small_noise_ref, mask_ref, SMALL_SIDE, job_refs[JOB_REFS:]) for k in range(smalls)
    ]
    net.begun = set()
    turns = [big_jobs[k : k + 1] + small_jobs[k : k + 1] for k in range(max(bigs, smalls))]
    if len(turns[-1]) > 1:
        turns[-1:] = [turns[-1][1:], turns[-1][:1]]
    for k, jobs in enumerate(turns):
        together(later(forward_pass(job, which, net), SKEW * which + k) for k, job in enumerate(jobs) for which in range(2))
        together(backward_pass(job, net, k == len(turns) - 1) for job in jobs)

    emb = emb_ref[...]
    mine = jnp.concatenate(
        [emb[2 * k + 1 : 2 * k + 2] for k in range(count)] + [jnp.zeros((gtime.shape[1] - count, CH), F32)], axis=0
    ).astype(BF16)
    for number in range(2):
        value = mm_tn(gtime[number].astype(BF16), mine)
        for k in range(TIME_COUNT):
            i, j = k // 4, k % 4
            time_w[number, i * BLOCK : (i + 1) * BLOCK, j * BLOCK : (j + 1) * BLOCK] = value[
                j * BLOCK : (j + 1) * BLOCK, i * BLOCK : (i + 1) * BLOCK
            ].astype(BF16)
        store(("time", number))

    for tap in range(9):
        gvec_ref[3 * tap : 3 * tap + 3, :] = gin_ref[8 * tap : 8 * tap + 3, :]
        gvec_ref[47 + 3 * tap : 50 + 3 * tap, :] = ghead_ref[8 * tap : 8 * tap + 3, :]
    gvec_ref[27:28, :] = gin_ref[72:73, :]
    gvec_ref[74:75, :] = loss_ref[0:1, :]
    piece_ref[...] = jnp.zeros_like(piece_ref)
    tile_ref[0:80, :] = gvec_ref[:, 0:BLOCK]
    tile_ref[80:160, :] = gvec_ref[:, BLOCK:]
    rows = piece_rows(devices)
    for k in range(-(-160 // rows)):
        end = min(160, (k + 1) * rows)
        piece_ref[k, 0 : end - k * rows, :] = tile_ref[k * rows : end, :]
    value = piece_ref[...]
    high = value.astype(BF16).astype(F32)
    piece_low[...] = jnp.concatenate([high, value - high], axis=1).astype(BF16)
    keep = pltpu.make_async_copy(piece_low, grads_ref.at[:, pl.ds(per_device * BLOCK, 16), :], piece_sem)
    keep.start()
    keep.wait()
    for key in parts:
        wait_store(key)


def network_grads(owner_map, numbers, table, big_level, small_level, big, big_noise, small, small_noise, mask, vectors, whole, devices):
    per_device = whole.shape[0] // devices
    images = -(-(big.shape[1] + small.shape[1]) // 16) * 16
    vmem = pl.BlockSpec(memory_space=pltpu.VMEM)
    smem = pl.BlockSpec(memory_space=pltpu.SMEM)
    hbm = pl.BlockSpec(memory_space=ANY)
    return pl.pallas_call(
        net_kernel,
        out_shape=jax.ShapeDtypeStruct((devices, per_device * BLOCK + 16, BLOCK), BF16),
        in_specs=[smem] * 4 + [vmem] * 7 + [hbm],
        out_specs=hbm,
        scratch_shapes=[
            pltpu.VMEM((4, 9 * CH, CH), BF16),
            pltpu.VMEM((2, CH, 2 * CH), BF16),
            pltpu.VMEM((CH, 3 * CH), BF16),
            pltpu.VMEM((CH, CH), BF16),
            pltpu.VMEM((4, CH, 9 * CH), F32),
            pltpu.VMEM((3 * CH, CH), F32),
            pltpu.VMEM((CH, CH), F32),
            pltpu.VMEM((2, images, 2 * CH), F32),
            pltpu.VMEM((2, images, 2 * CH), F32),
            pltpu.VMEM((80, CH), F32),
            pltpu.VMEM((80, CH), F32),
            pltpu.VMEM((8, CH), F32),
            pltpu.VMEM((images, CH), F32),
            pltpu.VMEM((80, CH), F32),
            pltpu.VMEM((80, CH), F32),
            pltpu.VMEM((80, CH), F32),
            pltpu.VMEM((devices, 8, BLOCK), F32),
            pltpu.VMEM((160, BLOCK), F32),
            pltpu.VMEM((devices, 16, BLOCK), BF16),
            pltpu.SemaphoreType.DMA((8,)),
            pltpu.SemaphoreType.DMA((8,)),
            pltpu.SemaphoreType.DMA,
        ]
        + job_scratch(SIDE)
        + job_scratch(SMALL_SIDE),
        compiler_params=pltpu.CompilerParams(vmem_limit_bytes=62 * 1024 * 1024),
        cost_estimate=pl.CostEstimate(flops=57 * 10**9, bytes_accessed=20 * 10**6, transcendentals=10**7),
    )(owner_map, numbers, big_level, small_level, table, big, big_noise, small, small_noise, mask, vectors, whole)


MESH_ID = pl.DeviceIdType.MESH


def where_am_i():
    dp = lax.axis_index("dp")
    return lax.axis_index("pair"), dp // 4, (dp // 2) % 2, dp % 2


def device(pair, line, mid, core):
    return (pair, (line * 2 + mid) * 2 + core)


def neighbours():
    pair, line, mid, core = where_am_i()
    flip_pair, flip_mid = 1 - 2 * pair, 1 - 2 * mid
    second = device(pair + (1 - core) * flip_pair, line, mid + core * flip_mid, core)
    third = device(pair + core * flip_pair, line, mid + (1 - core) * flip_mid, core)
    sibling = device(pair, line, mid, 1 - core)
    at_second = (1 - core) * pair + core * mid
    at_third = core * pair + (1 - core) * mid
    return pair, line, mid, core, at_second, at_third, second, third, sibling


def greet(lines, devices, lower, upper, line):
    barrier = pltpu.get_barrier_semaphore()
    for other in devices:
        pl.semaphore_signal(barrier, inc=1, device_id=other, device_id_type=MESH_ID)
    for there, other in ((lower >= 0, lower), (upper < lines, upper)):

        @pl.when(there)
        def _(other=other):
            pl.semaphore_signal(barrier, inc=1, device_id=line(other), device_id_type=MESH_ID)

    beside = jnp.where(lower >= 0, 1, 0) + jnp.where(upper < lines, 1, 0)
    pl.semaphore_wait(barrier, len(devices) + beside)


def gather_kernel(
    lines, blocks_ref, whole_ref, own, up_send, down_send, second_send, third_send, sib_send, line_recv, second_recv, third_recv, sib_recv, own_sem
):
    pair, line, mid, core, at_second, at_third, second, third, sibling = neighbours()
    count = blocks_ref.shape[0]
    group = 4 * lines
    upper = device(pair, line + 1, mid, core)
    lower = device(pair, line - 1, mid, core)

    def place(l, s, t, c):
        p = (1 - c) * s + c * t
        m = c * s + (1 - c) * t
        return whole_ref.at[pl.ds((p * group + (l * 2 + m) * 2 + c) * count, count)]

    def copy(source, target, send, recv, to):
        return pltpu.make_async_remote_copy(
            src_ref=source, dst_ref=target, send_sem=send, recv_sem=recv, device_id=to, device_id_type=MESH_ID
        )

    def to_sibling(l, s, t, source=None):
        where = place(l, s, t, core)
        p = (1 - core) * s + core * t
        m = core * s + (1 - core) * t
        index = l * 4 + p * 2 + m
        return copy(where if source is None else source, where, sib_send.at[index], sib_recv.at[index], sibling)

    def to_second(l, source=None):
        where = place(l, at_second, at_third, core)
        return copy(where if source is None else source, where, second_send.at[l], second_recv.at[l], second)

    def to_third(l, s, source=None):
        where = place(l, s, at_third, core)
        index = l * 2 + s
        return copy(where if source is None else source, where, third_send.at[index], third_recv.at[index], third)

    def to_upper(l, source=None):
        where = place(l, at_second, at_third, core)
        return copy(where if source is None else source, where, up_send.at[l], line_recv.at[l], upper)

    def to_lower(l, source=None):
        where = place(l, at_second, at_third, core)
        return copy(where if source is None else source, where, down_send.at[l], line_recv.at[l], lower)

    own[...] = blocks_ref[...].astype(BF16)
    greet(lines, (second, third, sibling), line - 1, line + 1, lambda l: device(pair, l, mid, core))

    @pl.when(line < lines - 1)
    def _():
        to_upper(line, own).start()

    @pl.when(line > 0)
    def _():
        to_lower(line, own).start()

    to_third(line, at_second, own).start()
    to_second(line, own).start()
    to_sibling(line, at_second, at_third, own).start()
    keep = pltpu.make_async_copy(own, place(line, at_second, at_third, core), own_sem)
    keep.start()

    def from_second(l):
        to_second(l).wait_recv()
        to_third(l, 1 - at_second).start()
        to_sibling(l, 1 - at_second, at_third).start()

    def from_line(l):
        to_upper(l).wait_recv()

        @pl.when((l < line) & (line < lines - 1))
        def _():
            to_upper(l).start()

        @pl.when((l > line) & (line > 0))
        def _():
            to_lower(l).start()

        to_second(l).start()
        to_third(l, at_second).start()
        to_sibling(l, at_second, at_third).start()

    def both(distance, carry):
        @pl.when(line - distance >= 0)
        def _():
            from_line(line - distance)

        @pl.when(line + distance < lines)
        def _():
            from_line(line + distance)

        @pl.when(line - distance + 1 >= 0)
        def _():
            from_second(line - distance + 1)

        @pl.when((line + distance - 1 < lines) & (distance > 1))
        def _():
            from_second(line + distance - 1)

        return carry

    lax.fori_loop(1, lines + 1, both, 0)

    def from_third(l, carry):
        for s in range(2):
            to_third(l, s).wait_recv()
            to_sibling(l, s, 1 - at_third).start()
        return carry

    lax.fori_loop(0, lines, from_third, 0)

    def finish(l, carry):
        @pl.when((l <= line) & (line < lines - 1))
        def _():
            to_upper(l).wait_send()

        @pl.when((l >= line) & (line > 0))
        def _():
            to_lower(l).wait_send()

        to_second(l).wait_send()
        for s in range(2):
            to_third(l, s).wait_send()
            for t in range(2):
                done = to_sibling(l, s, t)
                done.wait_send()
                done.wait_recv()
        return carry

    lax.fori_loop(0, lines, finish, 0)
    keep.wait()


def gather_blocks(blocks):
    lines = lax.axis_size("dp") // 4
    count = blocks.shape[0]
    total = count * lines * 8
    dma = pltpu.SemaphoreType.DMA
    return pl.pallas_call(
        partial(gather_kernel, lines),
        out_shape=jax.ShapeDtypeStruct((total, BLOCK, BLOCK), BF16),
        in_specs=[pl.BlockSpec(memory_space=pltpu.VMEM)],
        out_specs=pl.BlockSpec(memory_space=ANY),
        scratch_shapes=[
            pltpu.VMEM((count, BLOCK, BLOCK), BF16),
            dma((lines,)),
            dma((lines,)),
            dma((lines,)),
            dma((2 * lines,)),
            dma((4 * lines,)),
            dma((lines,)),
            dma((lines,)),
            dma((2 * lines,)),
            dma((4 * lines,)),
            dma,
        ],
        compiler_params=pltpu.CompilerParams(collective_id=0, has_side_effects=True),
        cost_estimate=pl.CostEstimate(flops=0, bytes_accessed=2 * total * BLOCK * BLOCK * 2, transcendentals=0),
    )(blocks)


def sum_kernel(
    lines,
    grads_ref,
    owner_ref,
    sum_ref,
    tiles_ref,
    mine,
    from_sib,
    from_third,
    from_second,
    from_lower,
    from_upper,
    tiles,
    load_sem,
    sib_send,
    third_send,
    second_send,
    up_send,
    down_send,
    sib_recv,
    third_recv,
    second_recv,
    up_recv,
    down_recv,
    near_send,
    near_recv,
    far_send,
    far_recv,
):
    pair, line, mid, core, at_second, at_third, second, third, sibling = neighbours()
    count = sum_ref.shape[0]
    main = count * BLOCK
    group = 4 * lines
    upper = device(pair, line + 1, mid, core)
    lower = device(pair, line - 1, mid, core)
    here = pair * 4 + mid * 2 + core

    def peer(k):
        return device(k // 4, line, (k // 2) % 2, k % 2)

    def on_line(l):
        return device(pair, l, mid, core)

    def copy(source, target, send, recv, to):
        return pltpu.make_async_remote_copy(
            src_ref=source, dst_ref=target, send_sem=send, recv_sem=recv, device_id=to, device_id_type=MESH_ID
        )

    def spot(l, s, t):
        return l * 4 + s * 2 + t

    def shard(l, s, t, c):
        p = (1 - c) * s + c * t
        m = c * s + (1 - c) * t
        return p * group + (l * 2 + m) * 2 + c

    def to_sibling(l, s, t):
        index = spot(l, s, t)
        return copy(grads_ref.at[shard(l, s, t, 1 - core)], from_sib.at[index], sib_send.at[index], sib_recv.at[index], sibling)

    def load(l, s, t):
        index = spot(l, s, t)
        return pltpu.make_async_copy(grads_ref.at[shard(l, s, t, core)], mine.at[index], load_sem.at[index])

    def to_third(l, s):
        index = l * 2 + s
        return copy(mine.at[spot(l, s, 1 - at_third)], from_third.at[index], third_send.at[index], third_recv.at[index], third)

    def to_second(l):
        return copy(mine.at[spot(l, 1 - at_second, at_third)], from_second.at[l], second_send.at[l], second_recv.at[l], second)

    def to_upper(l):
        return copy(mine.at[spot(l, at_second, at_third)], from_lower.at[l], up_send.at[l], up_recv.at[l], upper)

    def to_lower(l):
        return copy(mine.at[spot(l, at_second, at_third)], from_upper.at[l], down_send.at[l], down_recv.at[l], lower)

    barrier = pltpu.get_barrier_semaphore()
    for k in range(8):

        @pl.when(here != k)
        def _(k=k):
            pl.semaphore_signal(barrier, inc=1, device_id=peer(k), device_id_type=MESH_ID)

    def greet_line(l, carry):
        @pl.when(l != line)
        def _():
            pl.semaphore_signal(barrier, inc=1, device_id=on_line(l), device_id_type=MESH_ID)

        return carry

    lax.fori_loop(0, lines, greet_line, 0)
    pl.semaphore_wait(barrier, 7 + lines - 1)

    def far_first(function):
        def step(k, carry):
            distance = lines - 1 - k

            @pl.when(line + distance < lines)
            def _():
                function(line + distance)

            @pl.when((line - distance >= 0) & (distance > 0))
            def _():
                function(line - distance)

            return carry

        lax.fori_loop(0, lines, step, 0)

    def start_both(l, places):
        s_at, t_at, s_own, t_own = places
        to_sibling(l, s_at, t_at).start()
        load(l, s_own, t_own).start()

    sib_second, sib_third = at_third, at_second
    for s, t in ((1, 1), (0, 1), (1, 0), (0, 0)):
        places = (
            sib_second + s * (1 - 2 * sib_second),
            sib_third + t * (1 - 2 * sib_third),
            at_second + s * (1 - 2 * at_second),
            at_third + t * (1 - 2 * at_third),
        )
        far_first(partial(start_both, places=places))

    def read(ref, index):
        tile = ref[index, main:, :].astype(F32)
        return ref[index, 0:main, :].astype(F32), tile[0:8] + tile[8:16]

    def add(value, ref, index):
        other = read(ref, index)
        return value[0] + other[0], value[1] + other[1]

    def write(index, value):
        high = value[1].astype(BF16).astype(F32)
        mine[index, 0:main, :] = value[0].astype(BF16)
        mine[index, main:, :] = jnp.concatenate([high, value[1] - high], axis=0).astype(BF16)

    def both_cores(l, s, t):
        load(l, s, t).wait()
        to_sibling(l, s, t).wait_recv()
        index = spot(l, s, t)
        return add(read(mine, index), from_sib, index)

    def send_third(l, s):
        write(spot(l, s, 1 - at_third), both_cores(l, s, 1 - at_third))
        to_third(l, s).start()

    far_first(lambda l: send_third(l, 1 - at_second))
    far_first(lambda l: send_third(l, at_second))

    def with_third(l, s):
        total = both_cores(l, s, at_third)
        to_third(l, s).wait_recv()
        return add(total, from_third, l * 2 + s)

    def send_second(l):
        write(spot(l, 1 - at_second, at_third), with_third(l, 1 - at_second))
        to_second(l).start()

    far_first(send_second)

    def with_second(l):
        total = with_third(l, at_second)
        to_second(l).wait_recv()
        return add(total, from_second, l)

    def send_line(k, carry):
        distance = lines - 1 - k
        above = line + distance
        below = line - distance

        @pl.when(above < lines)
        def _():
            index = spot(above, at_second, at_third)
            write(index, with_second(above))

            @pl.when(line > 0)
            def _():
                to_upper(above).wait_recv()
                write(index, add(read(mine, index), from_lower, above))

            to_upper(above).start()

        @pl.when(below >= 0)
        def _():
            index = spot(below, at_second, at_third)
            write(index, with_second(below))

            @pl.when(line < lines - 1)
            def _():
                to_lower(below).wait_recv()
                write(index, add(read(mine, index), from_upper, below))

            to_lower(below).start()

        return carry

    lax.fori_loop(0, lines - 1, send_line, 0)
    blocks, piece = with_second(line)
    sum_ref[...] = blocks.reshape(count, BLOCK, BLOCK)
    tiles[line, here] = piece

    def last(ref):
        more, piece = read(ref, line)
        sum_ref[...] += more.reshape(count, BLOCK, BLOCK)
        tiles[line, here] += piece

    @pl.when(line > 0)
    def _():
        to_upper(line).wait_recv()
        last(from_lower)

    @pl.when(line < lines - 1)
    def _():
        to_lower(line).wait_recv()
        last(from_upper)

    square = jnp.zeros((8, BLOCK), F32)
    for k in range(count):
        slot = (pair * group + (line * 2 + mid) * 2 + core) * count + k
        held = jnp.max(jnp.where(owner_ref[...] == slot, 1.0, 0.0), axis=1, keepdims=True)
        value = jnp.where(held > 0.0, sum_ref[k], 0.0)
        sum_ref[k] = value
        square = square + fold(value * value)
    at_last = lax.broadcasted_iota(jnp.int32, (8, BLOCK), 0) == 7
    tiles[line, here] = jnp.where(at_last, over_rows(square), tiles[line, here])

    def near(k):
        tile = tiles.at[line, here]
        return copy(tile, tile, near_send.at[k], near_recv.at[here], peer(k))

    def near_from(k):
        tile = tiles.at[line, k]
        return copy(tile, tile, near_send.at[k], near_recv.at[k], peer(k))

    def far(l):
        return copy(tiles.at[line], tiles.at[line], far_send.at[l], far_recv.at[line], on_line(l))

    def far_from(l):
        return copy(tiles.at[l], tiles.at[l], far_send.at[l], far_recv.at[l], on_line(l))

    def others(function):
        for k in range(8):

            @pl.when(here != k)
            def _(k=k):
                function(k)

    def other_lines(function):
        def step(l, carry):
            @pl.when(l != line)
            def _():
                function(l)

            return carry

        lax.fori_loop(0, lines, step, 0)

    others(lambda k: near(k).start())
    others(lambda k: near_from(k).wait_recv())
    other_lines(lambda l: far(l).start())

    def finish(l, carry):
        for s in range(2):
            for t in range(2):
                to_sibling(l, s, t).wait_send()
            to_third(l, s).wait_send()
        to_second(l).wait_send()

        @pl.when((l > line) & (line < lines - 1))
        def _():
            to_upper(l).wait_send()

        @pl.when((l < line) & (line > 0))
        def _():
            to_lower(l).wait_send()

        return carry

    lax.fori_loop(0, lines, finish, 0)
    others(lambda k: near(k).wait_send())
    other_lines(lambda l: far_from(l).wait_recv())
    other_lines(lambda l: far(l).wait_send())
    tiles_ref[...] = tiles[...]


def sum_by_slot(grads, owner_map):
    lines = lax.axis_size("dp") // 4
    rows = grads.shape[1]
    count = rows // BLOCK
    dma = pltpu.SemaphoreType.DMA
    vmem = pl.BlockSpec(memory_space=pltpu.VMEM)
    shard = (rows, BLOCK)
    return pl.pallas_call(
        partial(sum_kernel, lines),
        out_shape=(
            jax.ShapeDtypeStruct((count, BLOCK, BLOCK), F32),
            jax.ShapeDtypeStruct((lines, 8, 8, BLOCK), F32),
        ),
        in_specs=[pl.BlockSpec(memory_space=ANY), vmem],
        out_specs=(vmem, vmem),
        scratch_shapes=[
            pltpu.VMEM((4 * lines,) + shard, BF16),
            pltpu.VMEM((4 * lines,) + shard, BF16),
            pltpu.VMEM((2 * lines,) + shard, BF16),
            pltpu.VMEM((lines,) + shard, BF16),
            pltpu.VMEM((lines,) + shard, BF16),
            pltpu.VMEM((lines,) + shard, BF16),
            pltpu.VMEM((lines, 8, 8, BLOCK), F32),
            dma((4 * lines,)),
            dma((4 * lines,)),
            dma((2 * lines,)),
            dma((lines,)),
            dma((lines,)),
            dma((lines,)),
            dma((4 * lines,)),
            dma((2 * lines,)),
            dma((lines,)),
            dma((lines,)),
            dma((lines,)),
            dma((8,)),
            dma((8,)),
            dma((lines,)),
            dma((lines,)),
        ],
        compiler_params=pltpu.CompilerParams(collective_id=1, has_side_effects=True, vmem_limit_bytes=48 * 1024 * 1024),
        cost_estimate=pl.CostEstimate(flops=0, bytes_accessed=2 * grads.size * 2, transcendentals=0),
    )(grads, owner_map.reshape(1, -1))


def mm_exact(left, right, over):
    return lax.dot_general(left, right, (over, ((), ())), precision=HIGH, preferred_element_type=F32)


def update_kernel(
    sum_ref,
    tiles_ref,
    blocks_ref,
    moments_ref,
    left_ref,
    right_ref,
    left_root_ref,
    right_root_ref,
    vec_ref,
    vec_first_ref,
    vec_second_ref,
    loss_ref,
    norm_ref,
    new_blocks_ref,
    new_moments_ref,
    new_left_ref,
    new_right_ref,
    new_vec_ref,
    new_first_ref,
    new_second_ref,
    rows_ref,
):
    lines = tiles_ref.shape[0]
    piece = piece_rows(8 * lines)
    for line in range(lines):
        for k in range(8):
            shard = (k // 4) * 4 * lines + (line * 2 + (k // 2) % 2) * 2 + k % 2
            rows_ref[shard * piece : (shard + 1) * piece, :] = tiles_ref[line, k, 0:piece, :]
    count = vec_ref.shape[0]
    grads = jnp.concatenate([rows_ref[0:80, :], rows_ref[80:160, :]], axis=1)
    loss_ref[0, 0] = jnp.max(grads[74:75, :])
    vec_grad = grads[0:count]
    square = jnp.sum(tiles_ref[...].reshape(64 * lines, BLOCK).reshape(8 * lines, 8, BLOCK)[:, 7, :])
    total = jnp.full((1, 1), square + jnp.sum(vec_grad * vec_grad), F32)
    norm = jnp.sqrt(total)
    norm_ref[0, 0] = jnp.max(norm)
    factor = jnp.minimum(1.0, CLIP / (norm + 1e-06))

    for k in range(sum_ref.shape[0]):
        turned_grad = sum_ref[k] * factor
        first = BETA_ONE * moments_ref[k] + (1 - BETA_ONE) * jnp.transpose(turned_grad)
        new_moments_ref[k] = first
        new_left_ref[k] = BETA_TWO * left_ref[k] + (1 - BETA_TWO) * mm_exact(turned_grad, turned_grad, ((0,), (0,)))
        new_right_ref[k] = BETA_TWO * right_ref[k] + (1 - BETA_TWO) * mm_exact(turned_grad, turned_grad, ((1,), (1,)))
        turned = mm_exact(left_root_ref[k], first, ((1,), (0,)))
        turned = mm_exact(turned, right_root_ref[k], ((1,), (0,)))
        mean = jnp.sum(over_rows(fold(turned * turned)), axis=1, keepdims=True) * (1.0 / BLOCK**2)
        master = blocks_ref[k]
        new_blocks_ref[k] = master - RATE_MATRIX * (turned * (1.0 / jnp.sqrt(mean + 1e-20)) + DECAY * master)

    grad = vec_grad * factor
    params = vec_ref[...]
    first = BETA_ONE * vec_first_ref[...] + (1 - BETA_ONE) * grad
    second = BETA_TWO * vec_second_ref[...] + (1 - BETA_TWO) * grad * grad
    fixed_first = first * (1.0 / (1 - BETA_ONE**STEP))
    fixed_second = second * (1.0 / (1 - BETA_TWO**STEP))
    new_vec_ref[...] = params - RATE_VECTOR * (fixed_first / (jnp.sqrt(fixed_second) + 1e-08) + DECAY * params)
    new_first_ref[...] = first
    new_second_ref[...] = second


def piece_rows(devices):
    return -(-160 // devices)


def update(summed, tiles, blocks, moments, left_stats, right_stats, left_roots, right_roots, vectors, vec_first, vec_second):
    vmem = pl.BlockSpec(memory_space=pltpu.VMEM)
    smem = pl.BlockSpec(memory_space=pltpu.SMEM)
    devices = 8 * tiles.shape[0]
    like = lambda value: jax.ShapeDtypeStruct(value.shape, F32)
    scalar = jax.ShapeDtypeStruct((1, 1), F32)
    return pl.pallas_call(
        update_kernel,
        out_shape=(scalar, scalar) + (like(blocks),) * 4 + (like(vectors),) * 3,
        in_specs=[vmem] * 11,
        out_specs=(smem, smem) + (vmem,) * 7,
        scratch_shapes=[pltpu.VMEM((max(160, devices * piece_rows(devices)), BLOCK), F32)],
        compiler_params=pltpu.CompilerParams(vmem_limit_bytes=48 * 1024 * 1024),
        cost_estimate=pl.CostEstimate(flops=10**9, bytes_accessed=6 * 10**6, transcendentals=10**5),
    )(summed, tiles, blocks, moments, left_stats, right_stats, left_roots, right_roots, vectors, vec_first, vec_second)


def sigma_of(level):
    lowest = SIGMA_MIN ** (1.0 / RHO)
    highest = SIGMA_MAX ** (1.0 / RHO)
    return (lowest + level / (NSTEPS - 1) * (highest - lowest)) ** RHO


def level_tables():
    level = np.arange(NSTEPS, dtype=np.float64)
    sigma = sigma_of(level)
    inner = 1.0 / np.sqrt(sigma**2 + SIGMA_DATA**2)
    skip = SIGMA_DATA**2 / ((sigma - SIGMA_MIN) ** 2 + SIGMA_DATA**2)
    outer = (sigma - SIGMA_MIN) * SIGMA_DATA * inner
    rate = 1.0 / (sigma_of(level + 1) - sigma)
    numbers = np.stack([sigma, inner, skip, outer, rate] + [np.zeros_like(sigma)] * 3, axis=1).reshape(-1)
    half = CH // 2
    phase = np.log(sigma)[:, None] / 4.0 * np.exp(np.arange(half) * (math.log(100.0) / (half - 1)))
    embed = np.zeros((16, CH))
    embed[:NSTEPS] = np.concatenate([np.sin(phase), np.cos(phase)], axis=1)
    return numbers.astype(np.float32), embed.astype(np.float32)


def image_rows(big_images, big_noise, small_images, small_noise):
    return tuple(jnp.swapaxes(value, 0, 1) for value in (big_images, big_noise, small_images, small_noise))


def local(
    big_images,
    big_noise,
    small_images,
    small_noise,
    big_level,
    small_level,
    small_mask,
    owner_map,
    blocks,
    moments,
    left_stats,
    right_stats,
    left_roots,
    right_roots,
    vectors,
    vec_first,
    vec_second,
):
    whole = gather_blocks(blocks)
    numbers, table = level_tables()
    grads = network_grads(
        owner_map,
        jnp.asarray(numbers),
        jnp.asarray(table),
        big_level,
        small_level,
        *image_rows(big_images, big_noise, small_images, small_noise),
        small_mask,
        vectors,
        whole,
        lax.axis_size("pair") * lax.axis_size("dp"),
    )
    summed, tiles = sum_by_slot(grads, owner_map)
    loss, norm, *rest = update(
        summed, tiles, blocks, moments, left_stats, right_stats, left_roots, right_roots, vectors, vec_first, vec_second
    )
    return (loss.reshape(()), norm.reshape(()), *rest)


def solution(mesh):
    by_slot = P(("pair", "dp"), None, None)
    by_image = P("dp", None, None)
    placed = (by_image,) * 4 + (P("dp"), P("dp"), P("dp", None), P()) + (by_slot,) * 6 + (P(),) * 3
    return jax.shard_map(
        local,
        mesh=mesh,
        in_specs=placed,
        out_specs=(P(), P()) + (by_slot,) * 4 + (P(),) * 3,
        check_vma=False,
    )
```

```python
from functools import partial
import math

import jax
import jax.numpy as jnp
from jax import lax
from jax.experimental import pallas as pl
from jax.experimental.pallas import tpu as pltpu
from jax.sharding import PartitionSpec as P
import numpy as np

GROUPS = 32
SIDE = 32
SMALL_SIDE = 16
NSTEPS = 11
STEP = 10
CH = 256
BLOCK = 128

SIGMA_DATA = 0.5
SIGMA_MIN = 0.002
SIGMA_MAX = 80.0
RHO = 7.0
HUBER = 0.00054
CLIP = 1.0
BETA_ONE = 0.9
BETA_TWO = 0.999
DECAY = 0.0001
RATE_MATRIX = 0.02
RATE_VECTOR = 0.02
ROOT_HALF = 1.0 / math.sqrt(2.0)
ANY = pl.ANY
F32 = jnp.float32
BF16 = jnp.bfloat16

CONV_BLOCKS = 36
TIME_FIRST, TIME_COUNT = 144, 8
TRIPLE_FIRST, TRIPLE_COUNT = 160, 12
PROJ_FIRST, PROJ_COUNT = 172, 4

ROWS = 128
MM_ROWS = 256
SKEW = 2


def mm(left, right):
    return jnp.dot(left, right, preferred_element_type=F32)


def mm_nt(left, right):
    return lax.dot_general(left, right, (((1,), (1,)), ((), ())), preferred_element_type=F32)


def mm_tn(left, right):
    return lax.dot_general(left, right, (((0,), (0,)), ((), ())), preferred_element_type=F32)


def split(value):
    high = value.astype(BF16)
    return high, (value - high.astype(F32)).astype(BF16)


def fold(value):
    return jnp.sum(value.reshape(value.shape[0] // 8, 8, value.shape[1]), axis=0)


def over_rows(value):
    return jnp.sum(value, axis=0, keepdims=True)


def group_mean(value, ones):
    high = value.astype(BF16).astype(F32)
    rest = value - high
    middle = rest.astype(BF16).astype(F32)
    parts = jnp.concatenate([high, middle, rest - middle, jnp.zeros_like(value)], axis=0).astype(BF16)
    sums = mm(parts, ones)
    return (sums[0:8] + sums[8:16] + sums[16:24]) * 0.125


def sigmoid(value):
    return 0.5 + 0.5 * jnp.tanh(0.5 * value)


def group_stats(ref, pixels, ones):
    total = jnp.zeros((8, CH), F32)
    for row in range(0, pixels, ROWS):
        total = total + fold(ref[row : row + ROWS, :])
    own = jnp.broadcast_to(over_rows(total) * (1.0 / pixels), (8, CH))
    mean = group_mean(own, ones)
    total = jnp.zeros((8, CH), F32)
    for row in range(0, pixels, ROWS):
        center = ref[row : row + ROWS, :] - own[0:1]
        total = total + fold(center * center)
    within = jnp.broadcast_to(over_rows(total) * (1.0 / pixels), (8, CH))
    between = own - mean
    spread = group_mean(within + between * between, ones)
    return mean[0:1], lax.rsqrt(spread[0:1] + 1e-06)


def write_shifted(ref, row, value, side):
    count = value.shape[0]
    column = lax.broadcasted_iota(jnp.int32, (count, CH), 0) & (side - 1)
    left = jnp.where(column == 0, 0.0, pltpu.roll(value, 1, 0))
    right = jnp.where(column == side - 1, 0.0, pltpu.roll(value, count - 1, 0))
    at = slice(side + row, side + row + count)
    ref[at, 0:CH] = left.astype(BF16)
    ref[at, CH : 2 * CH] = value.astype(BF16)
    ref[at, 2 * CH : 3 * CH] = right.astype(BF16)


def clear_ends(ref, side):
    pixels = side * side
    zeros = jnp.zeros((side, 3 * CH), BF16)
    ref[0:side, :] = zeros
    ref[side + pixels : 2 * side + pixels, :] = zeros


def tap_shifts(side):
    pixels = side * side
    place = lax.broadcasted_iota(jnp.int32, (8, pixels), 1)
    x = place & (side - 1)
    y = place >> (side.bit_length() - 1)
    taps = []
    for dy in (-1, 0, 1):
        for dx in (-1, 0, 1):
            inside = (x + dx >= 0) & (x + dx < side) & (y + dy >= 0) & (y + dy < side)
            taps.append((dy * side + dx, inside))
    return taps


class Shared:
    pass


class Job:
    def __init__(self, image, local, clean, noise, mask, side, refs):
        self.image, self.local, self.clean, self.noise, self.mask, self.side = image, local, clean, noise, mask, side
        self.pixels = side * side
        self.rows = min(ROWS, self.pixels)
        self.mrows = min(MM_ROWS, self.pixels)
        (
            self.hid,
            self.first,
            self.pat,
            self.gpat,
            self.grad_t,
            self.expo,
            self.dscore,
            self.keep,
            self.value_t,
            self.key_t,
            self.normed,
            self.mixed,
            self.mixed_t,
            self.rinv,
            self.act_hi,
            self.act_lo,
            self.dhid,
            self.dact,
            self.dtri,
            self.x80,
            self.scaled,
            self.dnext,
        ) = refs
        self.stats = {}
        self.outs = [None, None]
        self.noisy = [None, None]

    def chunks(self):
        return [slice(row, row + self.rows) for row in range(0, self.pixels, self.rows)]

    def blocks(self):
        return [slice(row, row + self.mrows) for row in range(0, self.pixels, self.mrows)]

    def hid_of(self, which, level):
        return self.hid.at[level] if which else self.dhid

    def first_of(self, which, number):
        return self.first.at[number] if which else self.dact

    def pat_of(self, which, number):
        return self.pat.at[number] if which else self.gpat

    def keep_of(self, which, part):
        return self.keep.at[part] if which else self.dtri.at[part]

    def expo_of(self, which):
        return self.expo if which else self.dscore

    def value_t_of(self, which):
        return self.value_t if which else self.grad_t.at[0]


def job_scratch(side):
    pixels = side * side
    tall = pixels + 2 * side
    return [
        pltpu.VMEM((4, pixels, CH), F32),
        pltpu.VMEM((2, pixels, CH), F32),
        pltpu.VMEM((4, tall, 3 * CH), BF16),
        pltpu.VMEM((tall, 3 * CH), BF16),
        pltpu.VMEM((3, CH, pixels), BF16),
        pltpu.VMEM((pixels, pixels), BF16),
        pltpu.VMEM((pixels, pixels), BF16),
        pltpu.VMEM((3, pixels, CH), BF16),
        pltpu.VMEM((CH, pixels), BF16),
        pltpu.VMEM((CH, pixels), BF16),
        pltpu.VMEM((pixels, CH), BF16),
        pltpu.VMEM((pixels, CH), BF16),
        pltpu.VMEM((CH, pixels), F32),
        pltpu.VMEM((8, pixels), F32),
        pltpu.VMEM((pixels, CH), BF16),
        pltpu.VMEM((pixels, CH), BF16),
        pltpu.VMEM((pixels, CH), F32),
        pltpu.VMEM((pixels, CH), F32),
        pltpu.VMEM((3, pixels, CH), BF16),
        pltpu.VMEM((160, pixels), BF16),
        pltpu.VMEM((pixels, CH), BF16),
        pltpu.VMEM((pixels, CH), F32),
    ]


JOB_REFS = 22


def forward_pass(job, which, net):
    vec, side, pixels = net.vec, job.side, job.pixels
    taps = tap_shifts(side)

    def scal(item):
        return net.scal(job, which, item)

    at = pl.ds(job.local, 1)
    noisy = [job.clean[channel, at, :] + scal(0) * job.noise[channel, at, :] for channel in range(3)]
    noisy = jnp.concatenate(noisy + [jnp.zeros((5, pixels), F32)], axis=0)
    job.noisy[which] = noisy
    scaled = noisy * scal(1)
    parts = [jnp.where(inside, pltpu.roll(scaled, (-shift) % pixels, 1), 0.0) for shift, inside in taps]
    parts.append(jnp.where(lax.broadcasted_iota(jnp.int32, (8, pixels), 0) == 0, 1.0, 0.0))
    high, low = split(jnp.concatenate(parts, axis=0))
    if which:
        job.x80[0:80, :] = high
        job.x80[80:160, :] = low
        for k in range(4):
            clear_ends(job.pat.at[k], side)
    else:
        clear_ends(job.gpat, side)
    job.hid_of(which, 0)[...] = mm_tn(jnp.concatenate([high, high, low], axis=0), net.vin3)
    yield

    def act_conv(key, src, gain, bias, dst, number, use):
        mean, rstd = group_stats(src, pixels, net.ones)
        job.stats[which, key] = (mean, rstd)
        scale = rstd * gain
        yield
        chunks = job.chunks()

        def put(until):
            while chunks and chunks[0].start < until:
                at = chunks.pop(0)
                z = (src[at, :] - mean) * scale + bias
                write_shifted(dst, at.start, z * sigmoid(z), side)

        put(job.mrows + side)
        net.ready(number)
        for at in job.blocks():
            put(at.stop + side)
            use(at, conv(dst, number, at.start))
            yield

    def conv(src, number, row):
        total = None
        for dy in range(3):
            start = dy * side + row
            part = mm(src[start : start + job.mrows, :], net.conv_w[number, dy * 768 : (dy + 1) * 768, :])
            total = part if total is None else total + part
        return total

    for number in range(2):
        base = 28 + 6 * number
        hid = job.hid_of(which, number)
        after = job.hid_of(which, number + 1)
        first = job.first_of(which, number)

        def use_first(at, value):
            first[at, :] = value + vec(base + 2)

        def use_second(at, value):
            after[at, :] = (hid[at, :] + (value + vec(base + 5))) * ROOT_HALF

        yield from act_conv(
            ("a", number), hid, vec(base), vec(base + 1), job.pat_of(which, 2 * number), 2 * number, use_first
        )
        gain_t, bias_t = net.shifts(job, which, number)
        yield from act_conv(
            ("b", number),
            first,
            1.0 + gain_t + vec(base + 3),
            bias_t + vec(base + 4),
            job.pat_of(which, 2 * number + 1),
            2 * number + 1,
            use_second,
        )

    net.ready("attention")
    src = job.hid_of(which, 2)
    mean, rstd = group_stats(src, pixels, net.ones)
    job.stats[which, "n"] = (mean, rstd)
    scale = rstd * vec(40)
    query, key, value_of = (job.keep_of(which, part) for part in range(3))
    value_t = job.value_t_of(which)
    for at in job.blocks():
        normed = ((src[at, :] - mean) * scale + vec(41)).astype(BF16)
        if which:
            job.normed[at, :] = normed
        triple = mm(normed, net.triple_w[...])
        query[at, :] = ((triple[:, 0:CH] + vec(42)) * (1.0 / math.sqrt(CH))).astype(BF16)
        key[at, :] = triple[:, CH : 2 * CH].astype(BF16)
        value = triple[:, 2 * CH :] + vec(43)
        value_of[at, :] = value.astype(BF16)
        value_t[:, at] = jnp.transpose(value).astype(BF16)
        if which:
            job.key_t[:, at] = (jnp.transpose(triple[:, CH : 2 * CH]) * (1.0 / math.sqrt(CH))).astype(BF16)
        yield
    expo = job.expo_of(which)
    scores = job.dnext if which else job.dact
    after = job.hid_of(which, 3)

    def mix(at, rinv):
        mixed_t = mm(value_t[...], expo[:, at]) * rinv
        mixed = jnp.transpose(mixed_t).astype(BF16)
        if which:
            job.rinv[:, at] = jnp.broadcast_to(rinv, (8, job.mrows))
            job.mixed_t[:, at] = mixed_t
            job.mixed[at, :] = mixed
        after[at, :] = (src[at, :] + (mm(mixed, net.proj_w[...]) + vec(44))) * ROOT_HALF

    before = None
    for at in job.blocks():
        scores[...] = mm_nt(key[...], query[at, :])
        if before is not None:
            mix(*before)
        yield
        top = jnp.max(scores[...], axis=0, keepdims=True)
        total = jnp.zeros((8, job.mrows), F32)
        for keys in job.chunks():
            weight = jnp.exp(scores[keys, :] - top)
            total = total + fold(weight)
            expo[keys, at] = weight.astype(BF16)
        before = (at, 1.0 / over_rows(total))
        yield
    mix(*before)
    yield
    mean, rstd = group_stats(after, pixels, net.ones)
    job.stats[which, "h"] = (mean, rstd)
    scale = rstd * vec(45)
    yield
    wide = []
    for at in job.blocks():
        z = (after[at, :] - mean) * scale + vec(46)
        high, low = split(z * sigmoid(z))
        if which:
            job.act_hi[at, :] = high
            job.act_lo[at, :] = low
        part = mm_nt(net.head2, high)
        wide.append(part[0:80] + part[80:160] + mm_nt(net.head_hi, low))
    wide = jnp.concatenate(wide, axis=1)
    out = jnp.zeros((8, pixels), F32)
    for k, (shift, inside) in enumerate(taps):
        out = out + jnp.where(inside, pltpu.roll(wide[8 * k : 8 * k + 8], (-shift) % pixels, 1), 0.0)
    job.outs[which] = scal(2) * noisy + scal(3) * out
    yield


def backward_pass(job, net, finish):
    vec, side, pixels = net.vec, job.side, job.pixels
    taps = tap_shifts(side)
    dact, dhid, gpat, grad_t = job.dact, job.dhid, job.gpat, job.grad_t

    def add_vec(row, value):
        net.gvec[row : row + 1, :] += value

    diff = job.outs[1] - job.outs[0]
    weighted = diff if job.mask is None else diff * job.mask[pl.ds(job.local, 1), :].astype(F32)
    bound = HUBER * math.sqrt(3 * pixels)
    total = jnp.sum(jnp.sum(weighted * diff, axis=1, keepdims=True), axis=0, keepdims=True)
    root = jnp.sqrt(total + bound * bound)
    rate = net.scal(job, 0, 4)
    net.loss[...] += jnp.broadcast_to((root - bound) * rate, (8, CH))
    dout = weighted * ((rate * net.scal(job, 1, 3)) / root)

    parts = [pltpu.roll(jnp.where(inside, dout, 0.0), shift % pixels, 1) for shift, inside in taps]
    parts.append(jnp.zeros((8, pixels), F32))
    high, low = split(jnp.concatenate(parts, axis=0))
    three = jnp.concatenate([high, high, low], axis=0)
    dact[...] = mm_tn(three, net.head3)
    wide = mm(jnp.concatenate([high, low], axis=0), job.act_hi[...])
    net.ghead[...] += wide[0:80] + wide[80:160] + mm(high, job.act_lo[...])
    yield

    def act_sums(key, src, gain, bias, active, beside=()):
        mean, rstd = job.stats[1, key]
        beside = list(beside)
        sum_b = jnp.zeros((8, CH), F32)
        sum_g = jnp.zeros((8, CH), F32)
        for index, at in enumerate(job.chunks()):
            value = (src[at, :] - mean) * rstd
            grad = dact[at, :]
            if active:
                z = value * gain + bias
                sig = sigmoid(z)
                grad = grad * (sig * (1.0 + z * (1.0 - sig)))
                dact[at, :] = grad
            sum_b = sum_b + fold(grad)
            sum_g = sum_g + fold(grad * value)
            if index % 3 == 2 and beside:
                beside.pop(0)()
        for more in beside:
            more()
        sum_b = over_rows(sum_b)
        sum_g = over_rows(sum_g)
        both = jnp.concatenate([sum_b * gain, sum_g * gain, jnp.zeros((6, CH), F32)], axis=0)
        means = group_mean(both, net.ones) * (1.0 / pixels)
        of_grad = rstd * gain
        of_value = rstd * rstd * means[1:2]
        constant = rstd * means[0:1]

        def final(at):
            return of_grad * dact[at, :] - (src[at, :] - mean) * of_value - constant

        return sum_b, sum_g, final

    sum_b, sum_g, final = act_sums("h", job.hid.at[3], vec(45), vec(46), True)
    add_vec(45, sum_g)
    add_vec(46, sum_b)
    yield
    total = jnp.zeros((8, CH), F32)
    for at in job.chunks():
        grad = final(at) * ROOT_HALF
        dhid[at, :] = grad
        total = total + fold(grad)
        gpat[at, 0:CH] = grad.astype(BF16)
        grad_t[0, :, at] = jnp.transpose(grad).astype(BF16)
    add_vec(44, over_rows(total))
    yield

    def wgrad(key, acc, at, value, last):
        if key in net.begun:
            value = value + acc[at]
        net.begun.add(key)
        if finish:
            last(value)
        else:
            acc[at] = value

    wgrad("proj", net.proj_g, (slice(None), slice(None)), mm(grad_t[0], job.mixed[...]), net.put_proj)
    total = jnp.zeros((8, CH), F32)
    query, key, value_of = (job.keep.at[part] for part in range(3))
    for at in job.blocks():
        out_t = mm_nt(net.proj_w[...], gpat[at, 0:CH])
        low_t = out_t.astype(BF16)
        inner = jnp.sum(low_t.astype(F32) * job.mixed_t[:, at], axis=0, keepdims=True)
        rinv = job.rinv[0:1, at]
        job.scaled[at, :] = jnp.transpose(out_t * rinv).astype(BF16)
        grad = mm(value_of[...], low_t)
        job.dscore[:, at] = (job.expo[:, at].astype(F32) * ((grad - inner) * rinv)).astype(BF16)
        dq_t = mm(job.key_t[...], job.dscore[:, at])
        dq = jnp.transpose(dq_t)
        total = total + fold(dq)
        job.dtri[0, at, :] = dq.astype(BF16)
        grad_t[0, :, at] = dq_t.astype(BF16)
        yield
    if finish:
        net.send("proj")
    add_vec(42, over_rows(total))
    total = jnp.zeros((8, CH), F32)
    for at in job.blocks():
        dk = mm(job.dscore[at, :], query[...])
        dv = mm(job.expo[at, :], job.scaled[...])
        total = total + fold(dv)
        job.dtri[1, at, :] = dk.astype(BF16)
        job.dtri[2, at, :] = dv.astype(BF16)
        grad_t[1, :, at] = jnp.transpose(dk).astype(BF16)
        grad_t[2, :, at] = jnp.transpose(dv).astype(BF16)
    add_vec(43, over_rows(total))
    yield
    for at in job.blocks():
        grad = None
        for part in range(3):
            more = mm_nt(job.dtri[part, at, :], net.triple_w[:, part * CH : (part + 1) * CH])
            grad = more if grad is None else grad + more
        dact[at, :] = grad
    for part in range(3):
        wgrad(
            ("triple", part),
            net.triple_g,
            (slice(part * CH, (part + 1) * CH), slice(None)),
            mm(grad_t[part], job.normed[...]),
            partial(net.put_triple, part),
        )
    if finish:
        net.send("triple")
    yield
    clear_ends(gpat, side)
    sum_b, sum_g, final = act_sums("n", job.hid.at[2], vec(40), vec(41), False)
    add_vec(40, sum_g)
    add_vec(41, sum_b)
    yield

    def conv_in(number, chunk_grad, slot):
        chunks = job.chunks()
        sums = [jnp.zeros((8, CH), F32)]

        def put(until):
            while chunks and chunks[0].start < until:
                at = chunks.pop(0)
                grad = chunk_grad(at)
                sums[0] = sums[0] + fold(grad)
                write_shifted(gpat, at.start, grad, side)
                grad_t[slot, :, at] = jnp.transpose(grad).astype(BF16)

        results = []
        for at in job.blocks():
            put(at.stop + side + job.rows)
            total = None
            for dy in range(3):
                for dx in range(3):
                    tap = dy * 3 + dx
                    start = (2 - dy) * side + at.start
                    part = mm_nt(
                        gpat[start : start + job.mrows, (2 - dx) * CH : (3 - dx) * CH],
                        net.conv_w[number, tap * CH : (tap + 1) * CH, :],
                    )
                    total = part if total is None else total + part
            job.dnext[at, :] = total
            yield
        sums_of[0] = over_rows(sums[0])

    sums_of = [None]

    def conv_matrix(number, slot):
        def one(dy):
            wgrad(
                (number, dy),
                net.conv_g,
                (number, slice(None), slice(dy * 768, (dy + 1) * 768)),
                mm(grad_t[slot], job.pat[number, dy * side : dy * side + pixels, :]),
                partial(net.put_conv, number, dy),
            )

        return [partial(one, dy) for dy in range(3)]

    for number in (1, 0):
        base = 28 + 6 * number

        def grad_second(at, final=final):
            grad = (dhid[at, :] + final(at)) * ROOT_HALF
            dhid[at, :] = grad
            return grad

        yield from conv_in(2 * number + 1, grad_second, 0)
        add_vec(base + 5, sums_of[0])
        dact, job.dnext = job.dnext, dact
        gain_t, bias_t = net.shifts(job, 1, number)
        sum_b, sum_g, final = act_sums(
            ("b", number),
            job.first.at[number],
            1.0 + gain_t + vec(base + 3),
            bias_t + vec(base + 4),
            True,
            conv_matrix(2 * number + 1, 0),
        )
        if finish:
            net.send(2 * number + 1)
        add_vec(base + 3, sum_g)
        add_vec(base + 4, sum_b)
        net.gtime[number, job.image : job.image + 1, 0:CH] = sum_g
        net.gtime[number, job.image : job.image + 1, CH:] = sum_b
        yield
        yield from conv_in(2 * number, final, 1)
        add_vec(base + 2, sums_of[0])
        dact, job.dnext = job.dnext, dact
        sum_b, sum_g, final = act_sums(
            ("a", number), job.hid.at[number], vec(base), vec(base + 1), True, conv_matrix(2 * number, 1)
        )
        if finish:
            net.send(2 * number)
        add_vec(base, sum_g)
        add_vec(base + 1, sum_b)
        yield

    total = jnp.zeros((80, CH), F32)
    for at in job.blocks():
        high, low = split(dhid[at, :] + final(at))
        wide = mm(job.x80[:, at], high)
        total = total + wide[0:80] + wide[80:160] + mm(job.x80[0:80, at], low)
    net.gin[...] += total
    yield


def together(passes):
    passes = list(passes)
    while passes:
        for one in list(passes):
            try:
                next(one)
            except StopIteration:
                passes.remove(one)


def later(one, steps):
    for _ in range(steps):
        yield
    yield from one


def net_kernel(
    owner_ref,
    number_ref,
    big_level_ref,
    small_level_ref,
    table_ref,
    big_ref,
    big_noise_ref,
    small_ref,
    small_noise_ref,
    mask_ref,
    vec_ref,
    whole_ref,
    grads_ref,
    conv_w,
    time_w,
    triple_w,
    proj_w,
    conv_g,
    triple_g,
    proj_g,
    tsh,
    gtime,
    gin_ref,
    ghead_ref,
    loss_ref,
    emb_ref,
    vin_ref,
    head_ref,
    gvec_ref,
    piece_ref,
    tile_ref,
    piece_low,
    load_sem,
    store_sem,
    piece_sem,
    *job_refs,
):
    bigs = big_ref.shape[1] // 2
    smalls = small_ref.shape[1] // 2
    count = bigs + smalls
    pair = lax.axis_index("pair")
    devices, shard_rows = grads_ref.shape[0], grads_ref.shape[1]
    per_device = shard_rows // BLOCK

    parts = {}
    for number in range(2):
        parts["time", number] = [
            (TIME_FIRST + TIME_COUNT * number + k, time_w.at[number], k // 4, k % 4) for k in range(TIME_COUNT)
        ]
    for m in range(4):
        parts[m] = [(m * CONV_BLOCKS + k, conv_w.at[m], k // 2, k % 2) for k in range(CONV_BLOCKS)]
    parts["triple"] = [(TRIPLE_FIRST + k, triple_w, k // 6, k % 6) for k in range(TRIPLE_COUNT)]
    parts["proj"] = [(PROJ_FIRST + k, proj_w, k // 2, k % 2) for k in range(PROJ_COUNT)]
    sem_of = {key: k for k, key in enumerate(parts)}

    def block(ref, i, j):
        return ref.at[i * BLOCK : (i + 1) * BLOCK, j * BLOCK : (j + 1) * BLOCK]

    def load(key):
        for index, ref, i, j in parts[key]:
            pltpu.make_async_copy(whole_ref.at[owner_ref[index]], block(ref, i, j), load_sem.at[sem_of[key]]).start()

    def wait_load(key):
        ref = parts[key][0][1]
        pltpu.make_async_copy(ref, ref, load_sem.at[sem_of[key]]).wait()

    def store(key):
        for index, ref, i, j in parts[key]:
            slot = owner_ref[index]
            home = slot // per_device
            row = pl.multiple_of((slot - home * per_device) * BLOCK, BLOCK)
            target = grads_ref.at[home, pl.ds(row, BLOCK), :]
            pltpu.make_async_copy(block(ref, i, j), target, store_sem.at[sem_of[key]]).start()

    def wait_store(key):
        ref = parts[key][0][1]
        pltpu.make_async_copy(ref, ref, store_sem.at[sem_of[key]]).wait()

    for key in parts:
        load(key)

    gvec_ref[...] = jnp.zeros_like(gvec_ref)
    gin_ref[...] = jnp.zeros_like(gin_ref)
    ghead_ref[...] = jnp.zeros_like(ghead_ref)
    loss_ref[...] = jnp.zeros_like(loss_ref)
    gtime[...] = jnp.zeros_like(gtime)

    vin_ref[...] = jnp.zeros_like(vin_ref)
    head_ref[...] = jnp.zeros_like(head_ref)
    for tap in range(9):
        vin_ref[8 * tap : 8 * tap + 3, :] = vec_ref[3 * tap : 3 * tap + 3, :]
        head_ref[8 * tap : 8 * tap + 3, :] = vec_ref[47 + 3 * tap : 50 + 3 * tap, :]
    vin_ref[72:73, :] = vec_ref[27:28, :]

    levels = [big_level_ref[pair * bigs + k] for k in range(bigs)]
    levels += [small_level_ref[pair * smalls + k] for k in range(smalls)]
    emb_ref[...] = jnp.zeros_like(emb_ref)
    for k in range(count):
        for which in range(2):
            emb_ref[2 * k + which : 2 * k + which + 1, :] = table_ref[pl.ds(levels[k] + which, 1), :]

    net = Shared()
    vin_hi, vin_lo = split(vin_ref[...])
    net.vin3 = jnp.concatenate([vin_hi, vin_lo, vin_hi], axis=0)
    head_hi, head_lo = split(head_ref[...])
    net.head_hi = head_hi
    net.head2 = jnp.concatenate([head_hi, head_lo], axis=0)
    net.head3 = jnp.concatenate([head_hi, head_lo, head_hi], axis=0)
    group_row = lax.broadcasted_iota(jnp.int32, (CH, CH), 0) >> 3
    group_col = lax.broadcasted_iota(jnp.int32, (CH, CH), 1) >> 3
    net.ones = jnp.where(group_row == group_col, 1.0, 0.0).astype(BF16)
    net.conv_w, net.triple_w, net.proj_w = conv_w, triple_w, proj_w
    net.conv_g, net.triple_g, net.proj_g = conv_g, triple_g, proj_g
    net.gvec, net.gin, net.ghead, net.loss, net.gtime = gvec_ref, gin_ref, ghead_ref, loss_ref, gtime
    net.vec = lambda row: vec_ref[row : row + 1, :]
    net.scal = lambda job, which, item: number_ref[(levels[job.image] + which) * 8 + item]

    def shifts(job, which, number):
        row = tsh[number, 2 * job.image + which : 2 * job.image + which + 1, :]
        return row[:, 0:CH], row[:, CH:]

    net.shifts = shifts
    loaded = set()

    def ready(what):
        if what == 0:
            keys = (("time", 0), ("time", 1), 0)
        else:
            keys = ("triple", "proj") if what == "attention" else (what,)
        for key in keys:
            if key not in loaded:
                loaded.add(key)
                wait_load(key)
                if isinstance(key, tuple):
                    tsh[key[1]] = mm(emb_ref[...].astype(BF16), time_w[key[1]])

    net.ready = ready

    def put_conv(number, dy, value):
        for i in range(6):
            row = (dy * 6 + i) * BLOCK
            for j in range(2):
                conv_w[number, row : row + BLOCK, j * BLOCK : (j + 1) * BLOCK] = value[
                    j * BLOCK : (j + 1) * BLOCK, i * BLOCK : (i + 1) * BLOCK
                ].astype(BF16)

    def put_triple(part, value):
        for j in range(2):
            for i in range(2):
                column = part * CH + j * BLOCK
                triple_w[i * BLOCK : (i + 1) * BLOCK, column : column + BLOCK] = value[
                    j * BLOCK : (j + 1) * BLOCK, i * BLOCK : (i + 1) * BLOCK
                ].astype(BF16)

    def put_proj(value):
        net.proj_value = value

    def send(key):
        if key == "proj":
            for i in range(2):
                for j in range(2):
                    proj_w[i * BLOCK : (i + 1) * BLOCK, j * BLOCK : (j + 1) * BLOCK] = net.proj_value[
                        j * BLOCK : (j + 1) * BLOCK, i * BLOCK : (i + 1) * BLOCK
                    ].astype(BF16)
        store(key)

    net.put_conv, net.put_triple, net.put_proj, net.send = put_conv, put_triple, put_proj, send

    big_jobs = [Job(k, pair * bigs + k, big_ref, big_noise_ref, None, SIDE, job_refs[:JOB_REFS]) for k in range(bigs)]
    small_jobs = [
        Job(bigs + k, pair * smalls + k, small_ref, small_noise_ref, mask_ref, SMALL_SIDE, job_refs[JOB_REFS:]) for k in range(smalls)
    ]
    net.begun = set()
    turns = [big_jobs[k : k + 1] + small_jobs[k : k + 1] for k in range(max(bigs, smalls))]
    if len(turns[-1]) > 1:
        turns[-1:] = [turns[-1][1:], turns[-1][:1]]
    for k, jobs in enumerate(turns):
        together(later(forward_pass(job, which, net), SKEW * which + k) for k, job in enumerate(jobs) for which in range(2))
        together(backward_pass(job, net, k == len(turns) - 1) for job in jobs)

    emb = emb_ref[...]
    mine = jnp.concatenate(
        [emb[2 * k + 1 : 2 * k + 2] for k in range(count)] + [jnp.zeros((gtime.shape[1] - count, CH), F32)], axis=0
    ).astype(BF16)
    for number in range(2):
        value = mm_tn(gtime[number].astype(BF16), mine)
        for k in range(TIME_COUNT):
            i, j = k // 4, k % 4
            time_w[number, i * BLOCK : (i + 1) * BLOCK, j * BLOCK : (j + 1) * BLOCK] = value[
                j * BLOCK : (j + 1) * BLOCK, i * BLOCK : (i + 1) * BLOCK
            ].astype(BF16)
        store(("time", number))

    for tap in range(9):
        gvec_ref[3 * tap : 3 * tap + 3, :] = gin_ref[8 * tap : 8 * tap + 3, :]
        gvec_ref[47 + 3 * tap : 50 + 3 * tap, :] = ghead_ref[8 * tap : 8 * tap + 3, :]
    gvec_ref[27:28, :] = gin_ref[72:73, :]
    gvec_ref[74:75, :] = loss_ref[0:1, :]
    piece_ref[...] = jnp.zeros_like(piece_ref)
    tile_ref[0:80, :] = gvec_ref[:, 0:BLOCK]
    tile_ref[80:160, :] = gvec_ref[:, BLOCK:]
    rows = piece_rows(devices)
    for k in range(-(-160 // rows)):
        end = min(160, (k + 1) * rows)
        piece_ref[k, 0 : end - k * rows, :] = tile_ref[k * rows : end, :]
    value = piece_ref[...]
    high = value.astype(BF16).astype(F32)
    piece_low[...] = jnp.concatenate([high, value - high], axis=1).astype(BF16)
    keep = pltpu.make_async_copy(piece_low, grads_ref.at[:, pl.ds(per_device * BLOCK, 16), :], piece_sem)
    keep.start()
    keep.wait()
    for key in parts:
        wait_store(key)


def network_grads(owner_map, numbers, table, big_level, small_level, big, big_noise, small, small_noise, mask, vectors, whole, devices):
    per_device = whole.shape[0] // devices
    images = -(-(big.shape[1] + small.shape[1]) // 16) * 16
    vmem = pl.BlockSpec(memory_space=pltpu.VMEM)
    smem = pl.BlockSpec(memory_space=pltpu.SMEM)
    hbm = pl.BlockSpec(memory_space=ANY)
    return pl.pallas_call(
        net_kernel,
        out_shape=jax.ShapeDtypeStruct((devices, per_device * BLOCK + 16, BLOCK), BF16),
        in_specs=[smem] * 4 + [vmem] * 7 + [hbm],
        out_specs=hbm,
        scratch_shapes=[
            pltpu.VMEM((4, 9 * CH, CH), BF16),
            pltpu.VMEM((2, CH, 2 * CH), BF16),
            pltpu.VMEM((CH, 3 * CH), BF16),
            pltpu.VMEM((CH, CH), BF16),
            pltpu.VMEM((4, CH, 9 * CH), F32),
            pltpu.VMEM((3 * CH, CH), F32),
            pltpu.VMEM((CH, CH), F32),
            pltpu.VMEM((2, images, 2 * CH), F32),
            pltpu.VMEM((2, images, 2 * CH), F32),
            pltpu.VMEM((80, CH), F32),
            pltpu.VMEM((80, CH), F32),
            pltpu.VMEM((8, CH), F32),
            pltpu.VMEM((images, CH), F32),
            pltpu.VMEM((80, CH), F32),
            pltpu.VMEM((80, CH), F32),
            pltpu.VMEM((80, CH), F32),
            pltpu.VMEM((devices, 8, BLOCK), F32),
            pltpu.VMEM((160, BLOCK), F32),
            pltpu.VMEM((devices, 16, BLOCK), BF16),
            pltpu.SemaphoreType.DMA((8,)),
            pltpu.SemaphoreType.DMA((8,)),
            pltpu.SemaphoreType.DMA,
        ]
        + job_scratch(SIDE)
        + job_scratch(SMALL_SIDE),
        compiler_params=pltpu.CompilerParams(vmem_limit_bytes=62 * 1024 * 1024),
        cost_estimate=pl.CostEstimate(flops=57 * 10**9, bytes_accessed=20 * 10**6, transcendentals=10**7),
    )(owner_map, numbers, big_level, small_level, table, big, big_noise, small, small_noise, mask, vectors, whole)


MESH_ID = pl.DeviceIdType.MESH


def where_am_i():
    dp = lax.axis_index("dp")
    return lax.axis_index("pair"), dp // 4, (dp // 2) % 2, dp % 2


def device(pair, line, mid, core):
    return (pair, (line * 2 + mid) * 2 + core)


def neighbours():
    pair, line, mid, core = where_am_i()
    flip_pair, flip_mid = 1 - 2 * pair, 1 - 2 * mid
    second = device(pair + (1 - core) * flip_pair, line, mid + core * flip_mid, core)
    third = device(pair + core * flip_pair, line, mid + (1 - core) * flip_mid, core)
    sibling = device(pair, line, mid, 1 - core)
    at_second = (1 - core) * pair + core * mid
    at_third = core * pair + (1 - core) * mid
    return pair, line, mid, core, at_second, at_third, second, third, sibling


def greet(lines, devices, lower, upper, line):
    barrier = pltpu.get_barrier_semaphore()
    for other in devices:
        pl.semaphore_signal(barrier, inc=1, device_id=other, device_id_type=MESH_ID)
    for there, other in ((lower >= 0, lower), (upper < lines, upper)):

        @pl.when(there)
        def _(other=other):
            pl.semaphore_signal(barrier, inc=1, device_id=line(other), device_id_type=MESH_ID)

    beside = jnp.where(lower >= 0, 1, 0) + jnp.where(upper < lines, 1, 0)
    pl.semaphore_wait(barrier, len(devices) + beside)


def gather_kernel(
    lines, blocks_ref, whole_ref, own, up_send, down_send, second_send, third_send, sib_send, line_recv, second_recv, third_recv, sib_recv, own_sem
):
    pair, line, mid, core, at_second, at_third, second, third, sibling = neighbours()
    count = blocks_ref.shape[0]
    group = 4 * lines
    upper = device(pair, (line + 1) % lines, mid, core)
    lower = device(pair, (line + lines - 1) % lines, mid, core)

    def place(l, s, t, c):
        p = (1 - c) * s + c * t
        m = c * s + (1 - c) * t
        return whole_ref.at[pl.ds((p * group + (l * 2 + m) * 2 + c) * count, count)]

    def copy(source, target, send, recv, to):
        return pltpu.make_async_remote_copy(
            src_ref=source, dst_ref=target, send_sem=send, recv_sem=recv, device_id=to, device_id_type=MESH_ID
        )

    def to_sibling(l, s, t, source=None):
        where = place(l, s, t, core)
        p = (1 - core) * s + core * t
        m = core * s + (1 - core) * t
        index = l * 4 + p * 2 + m
        return copy(where if source is None else source, where, sib_send.at[index], sib_recv.at[index], sibling)

    def to_second(l, source=None):
        where = place(l, at_second, at_third, core)
        return copy(where if source is None else source, where, second_send.at[l], second_recv.at[l], second)

    def to_third(l, s, source=None):
        where = place(l, s, at_third, core)
        index = l * 2 + s
        return copy(where if source is None else source, where, third_send.at[index], third_recv.at[index], third)

    def to_upper(l, source=None):
        where = place(l, at_second, at_third, core)
        return copy(where if source is None else source, where, up_send.at[l], line_recv.at[l], upper)

    def to_lower(l, source=None):
        where = place(l, at_second, at_third, core)
        return copy(where if source is None else source, where, down_send.at[l], line_recv.at[l], lower)

    own[...] = blocks_ref[...].astype(BF16)
    greet(lines, (second, third, sibling), line - 1, line + 1, lambda l: device(pair, l, mid, core))

    @pl.when(line < lines - 1)
    def _():
        to_upper(line, own).start()

    @pl.when(line > 0)
    def _():
        to_lower(line, own).start()

    to_third(line, at_second, own).start()
    to_second(line, own).start()
    to_sibling(line, at_second, at_third, own).start()
    keep = pltpu.make_async_copy(own, place(line, at_second, at_third, core), own_sem)
    keep.start()

    def from_second(l):
        to_second(l).wait_recv()
        to_third(l, 1 - at_second).start()
        to_sibling(l, 1 - at_second, at_third).start()

    def from_line(l):
        to_upper(l).wait_recv()

        @pl.when((l < line) & (line < lines - 1))
        def _():
            to_upper(l).start()

        @pl.when((l > line) & (line > 0))
        def _():
            to_lower(l).start()

        to_second(l).start()
        to_third(l, at_second).start()
        to_sibling(l, at_second, at_third).start()

    def both(distance, carry):
        @pl.when(line - distance >= 0)
        def _():
            from_line(line - distance)

        @pl.when(line + distance < lines)
        def _():
            from_line(line + distance)

        @pl.when(line - distance + 1 >= 0)
        def _():
            from_second(line - distance + 1)

        @pl.when((line + distance - 1 < lines) & (distance > 1))
        def _():
            from_second(line + distance - 1)

        return carry

    lax.fori_loop(1, lines + 1, both, 0)

    def from_third(l, carry):
        for s in range(2):
            to_third(l, s).wait_recv()
            to_sibling(l, s, 1 - at_third).start()
        return carry

    lax.fori_loop(0, lines, from_third, 0)

    def finish(l, carry):
        @pl.when((l <= line) & (line < lines - 1))
        def _():
            to_upper(l).wait_send()

        @pl.when((l >= line) & (line > 0))
        def _():
            to_lower(l).wait_send()

        to_second(l).wait_send()
        for s in range(2):
            to_third(l, s).wait_send()
            for t in range(2):
                done = to_sibling(l, s, t)
                done.wait_send()
                done.wait_recv()
        return carry

    lax.fori_loop(0, lines, finish, 0)
    keep.wait()


def gather_blocks(blocks):
    lines = lax.axis_size("dp") // 4
    count = blocks.shape[0]
    total = count * lines * 8
    dma = pltpu.SemaphoreType.DMA
    return pl.pallas_call(
        partial(gather_kernel, lines),
        out_shape=jax.ShapeDtypeStruct((total, BLOCK, BLOCK), BF16),
        in_specs=[pl.BlockSpec(memory_space=pltpu.VMEM)],
        out_specs=pl.BlockSpec(memory_space=ANY),
        scratch_shapes=[
            pltpu.VMEM((count, BLOCK, BLOCK), BF16),
            dma((lines,)),
            dma((lines,)),
            dma((lines,)),
            dma((2 * lines,)),
            dma((4 * lines,)),
            dma((lines,)),
            dma((lines,)),
            dma((2 * lines,)),
            dma((4 * lines,)),
            dma,
        ],
        compiler_params=pltpu.CompilerParams(collective_id=0, has_side_effects=True),
        cost_estimate=pl.CostEstimate(flops=0, bytes_accessed=2 * total * BLOCK * BLOCK * 2, transcendentals=0),
    )(blocks)


def sum_kernel(
    lines,
    grads_ref,
    owner_ref,
    sum_ref,
    tiles_ref,
    mine,
    from_sib,
    from_third,
    from_second,
    from_lower,
    from_upper,
    tiles,
    load_sem,
    sib_send,
    third_send,
    second_send,
    up_send,
    down_send,
    sib_recv,
    third_recv,
    second_recv,
    up_recv,
    down_recv,
    near_send,
    near_recv,
    far_send,
    far_recv,
):
    pair, line, mid, core, at_second, at_third, second, third, sibling = neighbours()
    count = sum_ref.shape[0]
    main = count * BLOCK
    group = 4 * lines
    upper = device(pair, (line + 1) % lines, mid, core)
    lower = device(pair, (line + lines - 1) % lines, mid, core)
    here = pair * 4 + mid * 2 + core

    def peer(k):
        return device(k // 4, line, (k // 2) % 2, k % 2)

    def on_line(l):
        return device(pair, l, mid, core)

    def copy(source, target, send, recv, to):
        return pltpu.make_async_remote_copy(
            src_ref=source, dst_ref=target, send_sem=send, recv_sem=recv, device_id=to, device_id_type=MESH_ID
        )

    def spot(l, s, t):
        return l * 4 + s * 2 + t

    def shard(l, s, t, c):
        p = (1 - c) * s + c * t
        m = c * s + (1 - c) * t
        return p * group + (l * 2 + m) * 2 + c

    def to_sibling(l, s, t):
        index = spot(l, s, t)
        return copy(grads_ref.at[shard(l, s, t, 1 - core)], from_sib.at[index], sib_send.at[index], sib_recv.at[index], sibling)

    def load(l, s, t):
        index = spot(l, s, t)
        return pltpu.make_async_copy(grads_ref.at[shard(l, s, t, core)], mine.at[index], load_sem.at[index])

    def to_third(l, s):
        index = l * 2 + s
        return copy(mine.at[spot(l, s, 1 - at_third)], from_third.at[index], third_send.at[index], third_recv.at[index], third)

    def to_second(l):
        return copy(mine.at[spot(l, 1 - at_second, at_third)], from_second.at[l], second_send.at[l], second_recv.at[l], second)

    def to_upper(l):
        return copy(mine.at[spot(l, at_second, at_third)], from_lower.at[l], up_send.at[l], up_recv.at[l], upper)

    def to_lower(l):
        return copy(mine.at[spot(l, at_second, at_third)], from_upper.at[l], down_send.at[l], down_recv.at[l], lower)

    barrier = pltpu.get_barrier_semaphore()
    for k in range(8):

        @pl.when(here != k)
        def _(k=k):
            pl.semaphore_signal(barrier, inc=1, device_id=peer(k), device_id_type=MESH_ID)

    def greet_line(l, carry):
        @pl.when(l != line)
        def _():
            pl.semaphore_signal(barrier, inc=1, device_id=on_line(l), device_id_type=MESH_ID)

        return carry

    lax.fori_loop(0, lines, greet_line, 0)
    pl.semaphore_wait(barrier, 7 + lines - 1)

    def far_first(function):
        def step(k, carry):
            distance = lines - 1 - k

            @pl.when(line + distance < lines)
            def _():
                function(line + distance)

            @pl.when((line - distance >= 0) & (distance > 0))
            def _():
                function(line - distance)

            return carry

        lax.fori_loop(0, lines, step, 0)

    def start_both(l, places):
        s_at, t_at, s_own, t_own = places
        to_sibling(l, s_at, t_at).start()
        load(l, s_own, t_own).start()

    sib_second, sib_third = at_third, at_second
    for s, t in ((1, 1), (0, 1), (1, 0), (0, 0)):
        places = (
            sib_second + s * (1 - 2 * sib_second),
            sib_third + t * (1 - 2 * sib_third),
            at_second + s * (1 - 2 * at_second),
            at_third + t * (1 - 2 * at_third),
        )
        far_first(partial(start_both, places=places))

    def read(ref, index):
        tile = ref[index, main:, :].astype(F32)
        return ref[index, 0:main, :].astype(F32), tile[0:8] + tile[8:16]

    def add(value, ref, index):
        other = read(ref, index)
        return value[0] + other[0], value[1] + other[1]

    def write(index, value):
        high = value[1].astype(BF16).astype(F32)
        mine[index, 0:main, :] = value[0].astype(BF16)
        mine[index, main:, :] = jnp.concatenate([high, value[1] - high], axis=0).astype(BF16)

    def both_cores(l, s, t):
        load(l, s, t).wait()
        to_sibling(l, s, t).wait_recv()
        index = spot(l, s, t)
        return add(read(mine, index), from_sib, index)

    def send_third(l, s):
        write(spot(l, s, 1 - at_third), both_cores(l, s, 1 - at_third))
        to_third(l, s).start()

    far_first(lambda l: send_third(l, 1 - at_second))
    far_first(lambda l: send_third(l, at_second))

    def with_third(l, s):
        total = both_cores(l, s, at_third)
        to_third(l, s).wait_recv()
        return add(total, from_third, l * 2 + s)

    def send_second(l):
        write(spot(l, 1 - at_second, at_third), with_third(l, 1 - at_second))
        to_second(l).start()

    far_first(send_second)

    def with_second(l):
        total = with_third(l, at_second)
        to_second(l).wait_recv()
        return add(total, from_second, l)

    def send_line(k, carry):
        distance = lines - 1 - k
        above = line + distance
        below = line - distance

        @pl.when(above < lines)
        def _():
            index = spot(above, at_second, at_third)
            write(index, with_second(above))

            @pl.when(line > 0)
            def _():
                to_upper(above).wait_recv()
                write(index, add(read(mine, index), from_lower, above))

            to_upper(above).start()

        @pl.when(below >= 0)
        def _():
            index = spot(below, at_second, at_third)
            write(index, with_second(below))

            @pl.when(line < lines - 1)
            def _():
                to_lower(below).wait_recv()
                write(index, add(read(mine, index), from_upper, below))

            to_lower(below).start()

        return carry

    lax.fori_loop(0, lines - 1, send_line, 0)
    blocks, piece = with_second(line)
    sum_ref[...] = blocks.reshape(count, BLOCK, BLOCK)
    tiles[line, here] = piece

    def last(ref):
        more, piece = read(ref, line)
        sum_ref[...] += more.reshape(count, BLOCK, BLOCK)
        tiles[line, here] += piece

    @pl.when(line > 0)
    def _():
        to_upper(line).wait_recv()
        last(from_lower)

    @pl.when(line < lines - 1)
    def _():
        to_lower(line).wait_recv()
        last(from_upper)

    square = jnp.zeros((8, BLOCK), F32)
    for k in range(count):
        slot = (pair * group + (line * 2 + mid) * 2 + core) * count + k
        held = jnp.max(jnp.where(owner_ref[...] == slot, 1.0, 0.0), axis=1, keepdims=True)
        value = jnp.where(held > 0.0, sum_ref[k], 0.0)
        sum_ref[k] = value
        square = square + fold(value * value)
    at_last = lax.broadcasted_iota(jnp.int32, (8, BLOCK), 0) == 7
    tiles[line, here] = jnp.where(at_last, over_rows(square), tiles[line, here])

    def near(k):
        tile = tiles.at[line, here]
        return copy(tile, tile, near_send.at[k], near_recv.at[here], peer(k))

    def near_from(k):
        tile = tiles.at[line, k]
        return copy(tile, tile, near_send.at[k], near_recv.at[k], peer(k))

    def far(l):
        return copy(tiles.at[line], tiles.at[line], far_send.at[l], far_recv.at[line], on_line(l))

    def far_from(l):
        return copy(tiles.at[l], tiles.at[l], far_send.at[l], far_recv.at[l], on_line(l))

    def others(function):
        for k in range(8):

            @pl.when(here != k)
            def _(k=k):
                function(k)

    def other_lines(function):
        def step(l, carry):
            @pl.when(l != line)
            def _():
                function(l)

            return carry

        lax.fori_loop(0, lines, step, 0)

    others(lambda k: near(k).start())
    others(lambda k: near_from(k).wait_recv())
    other_lines(lambda l: far(l).start())

    def finish(l, carry):
        for s in range(2):
            for t in range(2):
                to_sibling(l, s, t).wait_send()
            to_third(l, s).wait_send()
        to_second(l).wait_send()

        @pl.when((l > line) & (line < lines - 1))
        def _():
            to_upper(l).wait_send()

        @pl.when((l < line) & (line > 0))
        def _():
            to_lower(l).wait_send()

        return carry

    lax.fori_loop(0, lines, finish, 0)
    others(lambda k: near(k).wait_send())
    other_lines(lambda l: far_from(l).wait_recv())
    other_lines(lambda l: far(l).wait_send())
    tiles_ref[...] = tiles[...]


def sum_by_slot(grads, owner_map):
    lines = lax.axis_size("dp") // 4
    rows = grads.shape[1]
    count = rows // BLOCK
    dma = pltpu.SemaphoreType.DMA
    vmem = pl.BlockSpec(memory_space=pltpu.VMEM)
    shard = (rows, BLOCK)
    return pl.pallas_call(
        partial(sum_kernel, lines),
        out_shape=(
            jax.ShapeDtypeStruct((count, BLOCK, BLOCK), F32),
            jax.ShapeDtypeStruct((lines, 8, 8, BLOCK), F32),
        ),
        in_specs=[pl.BlockSpec(memory_space=ANY), vmem],
        out_specs=(vmem, vmem),
        scratch_shapes=[
            pltpu.VMEM((4 * lines,) + shard, BF16),
            pltpu.VMEM((4 * lines,) + shard, BF16),
            pltpu.VMEM((2 * lines,) + shard, BF16),
            pltpu.VMEM((lines,) + shard, BF16),
            pltpu.VMEM((lines,) + shard, BF16),
            pltpu.VMEM((lines,) + shard, BF16),
            pltpu.VMEM((lines, 8, 8, BLOCK), F32),
            dma((4 * lines,)),
            dma((4 * lines,)),
            dma((2 * lines,)),
            dma((lines,)),
            dma((lines,)),
            dma((lines,)),
            dma((4 * lines,)),
            dma((2 * lines,)),
            dma((lines,)),
            dma((lines,)),
            dma((lines,)),
            dma((8,)),
            dma((8,)),
            dma((lines,)),
            dma((lines,)),
        ],
        compiler_params=pltpu.CompilerParams(collective_id=1, has_side_effects=True, vmem_limit_bytes=48 * 1024 * 1024),
        cost_estimate=pl.CostEstimate(flops=0, bytes_accessed=2 * grads.size * 2, transcendentals=0),
    )(grads, owner_map.reshape(1, -1))


def mm_split(left, right, over):
    high, low = split(left)
    other_high, other_low = split(right)

    def one(first, second):
        return lax.dot_general(first, second, (over, ((), ())), preferred_element_type=F32)

    return one(high, other_high) + (one(high, other_low) + one(low, other_high))


def update_kernel(
    sum_ref,
    tiles_ref,
    blocks_ref,
    moments_ref,
    left_ref,
    right_ref,
    left_root_ref,
    right_root_ref,
    vec_ref,
    vec_first_ref,
    vec_second_ref,
    loss_ref,
    norm_ref,
    new_blocks_ref,
    new_moments_ref,
    new_left_ref,
    new_right_ref,
    new_vec_ref,
    new_first_ref,
    new_second_ref,
    rows_ref,
):
    lines = tiles_ref.shape[0]
    piece = piece_rows(8 * lines)
    for line in range(lines):
        for k in range(8):
            shard = (k // 4) * 4 * lines + (line * 2 + (k // 2) % 2) * 2 + k % 2
            rows_ref[shard * piece : (shard + 1) * piece, :] = tiles_ref[line, k, 0:piece, :]
    count = vec_ref.shape[0]
    grads = jnp.concatenate([rows_ref[0:80, :], rows_ref[80:160, :]], axis=1)
    loss_ref[0, 0] = jnp.max(grads[74:75, :])
    vec_grad = grads[0:count]
    square = jnp.sum(tiles_ref[...].reshape(64 * lines, BLOCK).reshape(8 * lines, 8, BLOCK)[:, 7, :])
    total = jnp.full((1, 1), square + jnp.sum(vec_grad * vec_grad), F32)
    norm = jnp.sqrt(total)
    norm_ref[0, 0] = jnp.max(norm)
    factor = jnp.minimum(1.0, CLIP / (norm + 1e-06))

    for k in range(sum_ref.shape[0]):
        turned_grad = sum_ref[k] * factor
        first = BETA_ONE * moments_ref[k] + (1 - BETA_ONE) * jnp.transpose(turned_grad)
        new_moments_ref[k] = first
        new_left_ref[k] = BETA_TWO * left_ref[k] + (1 - BETA_TWO) * mm_split(turned_grad, turned_grad, ((0,), (0,)))
        new_right_ref[k] = BETA_TWO * right_ref[k] + (1 - BETA_TWO) * mm_split(turned_grad, turned_grad, ((1,), (1,)))
        turned = mm_split(left_root_ref[k], first, ((1,), (0,)))
        turned = mm_split(turned, right_root_ref[k], ((1,), (0,)))
        mean = jnp.sum(over_rows(fold(turned * turned)), axis=1, keepdims=True) * (1.0 / BLOCK**2)
        master = blocks_ref[k]
        new_blocks_ref[k] = master - RATE_MATRIX * (turned * (1.0 / jnp.sqrt(mean + 1e-20)) + DECAY * master)

    grad = vec_grad * factor
    params = vec_ref[...]
    first = BETA_ONE * vec_first_ref[...] + (1 - BETA_ONE) * grad
    second = BETA_TWO * vec_second_ref[...] + (1 - BETA_TWO) * grad * grad
    fixed_first = first * (1.0 / (1 - BETA_ONE**STEP))
    fixed_second = second * (1.0 / (1 - BETA_TWO**STEP))
    new_vec_ref[...] = params - RATE_VECTOR * (fixed_first / (jnp.sqrt(fixed_second) + 1e-08) + DECAY * params)
    new_first_ref[...] = first
    new_second_ref[...] = second


def piece_rows(devices):
    return -(-160 // devices)


def update(summed, tiles, blocks, moments, left_stats, right_stats, left_roots, right_roots, vectors, vec_first, vec_second):
    vmem = pl.BlockSpec(memory_space=pltpu.VMEM)
    smem = pl.BlockSpec(memory_space=pltpu.SMEM)
    devices = 8 * tiles.shape[0]
    like = lambda value: jax.ShapeDtypeStruct(value.shape, F32)
    scalar = jax.ShapeDtypeStruct((1, 1), F32)
    return pl.pallas_call(
        update_kernel,
        out_shape=(scalar, scalar) + (like(blocks),) * 4 + (like(vectors),) * 3,
        in_specs=[vmem] * 11,
        out_specs=(smem, smem) + (vmem,) * 7,
        scratch_shapes=[pltpu.VMEM((max(160, devices * piece_rows(devices)), BLOCK), F32)],
        compiler_params=pltpu.CompilerParams(vmem_limit_bytes=48 * 1024 * 1024),
        cost_estimate=pl.CostEstimate(flops=10**9, bytes_accessed=6 * 10**6, transcendentals=10**5),
    )(summed, tiles, blocks, moments, left_stats, right_stats, left_roots, right_roots, vectors, vec_first, vec_second)


def sigma_of(level):
    lowest = SIGMA_MIN ** (1.0 / RHO)
    highest = SIGMA_MAX ** (1.0 / RHO)
    return (lowest + level / (NSTEPS - 1) * (highest - lowest)) ** RHO


def level_tables():
    level = np.arange(NSTEPS, dtype=np.float64)
    sigma = sigma_of(level)
    inner = 1.0 / np.sqrt(sigma**2 + SIGMA_DATA**2)
    skip = SIGMA_DATA**2 / ((sigma - SIGMA_MIN) ** 2 + SIGMA_DATA**2)
    outer = (sigma - SIGMA_MIN) * SIGMA_DATA * inner
    rate = 1.0 / (sigma_of(level + 1) - sigma)
    numbers = np.stack([sigma, inner, skip, outer, rate] + [np.zeros_like(sigma)] * 3, axis=1).reshape(-1)
    half = CH // 2
    phase = np.log(sigma)[:, None] / 4.0 * np.exp(np.arange(half) * (math.log(100.0) / (half - 1)))
    embed = np.zeros((16, CH))
    embed[:NSTEPS] = np.concatenate([np.sin(phase), np.cos(phase)], axis=1)
    return numbers.astype(np.float32), embed.astype(np.float32)


def image_rows(big_images, big_noise, small_images, small_noise):
    return tuple(jnp.swapaxes(value, 0, 1) for value in (big_images, big_noise, small_images, small_noise))


def local(
    big_images,
    big_noise,
    small_images,
    small_noise,
    big_level,
    small_level,
    small_mask,
    owner_map,
    blocks,
    moments,
    left_stats,
    right_stats,
    left_roots,
    right_roots,
    vectors,
    vec_first,
    vec_second,
):
    whole = gather_blocks(blocks)
    numbers, table = level_tables()
    grads = network_grads(
        owner_map,
        jnp.asarray(numbers),
        jnp.asarray(table),
        big_level,
        small_level,
        *image_rows(big_images, big_noise, small_images, small_noise),
        small_mask,
        vectors,
        whole,
        lax.axis_size("pair") * lax.axis_size("dp"),
    )
    summed, tiles = sum_by_slot(grads, owner_map)
    loss, norm, *rest = update(
        summed, tiles, blocks, moments, left_stats, right_stats, left_roots, right_roots, vectors, vec_first, vec_second
    )
    return (loss.reshape(()), norm.reshape(()), *rest)


def solution(mesh):
    by_slot = P(("pair", "dp"), None, None)
    by_image = P("dp", None, None)
    placed = (by_image,) * 4 + (P("dp"), P("dp"), P("dp", None), P()) + (by_slot,) * 6 + (P(),) * 3
    return jax.shard_map(
        local,
        mesh=mesh,
        in_specs=placed,
        out_specs=(P(), P()) + (by_slot,) * 4 + (P(),) * 3,
        check_vma=False,
    )
```

```python
from functools import partial
import math

import jax
import jax.numpy as jnp
from jax import lax
from jax.experimental import pallas as pl
from jax.experimental.pallas import tpu as pltpu
from jax.sharding import PartitionSpec as P
import numpy as np

GROUPS = 32
SIDE = 32
SMALL_SIDE = 16
NSTEPS = 11
STEP = 10
CH = 256
BLOCK = 128

SIGMA_DATA = 0.5
SIGMA_MIN = 0.002
SIGMA_MAX = 80.0
RHO = 7.0
HUBER = 0.00054
CLIP = 1.0
BETA_ONE = 0.9
BETA_TWO = 0.999
DECAY = 0.0001
RATE_MATRIX = 0.02
RATE_VECTOR = 0.02
ROOT_HALF = 1.0 / math.sqrt(2.0)
ANY = pl.ANY
F32 = jnp.float32
BF16 = jnp.bfloat16

CONV_BLOCKS = 36
TIME_FIRST, TIME_COUNT = 144, 8
TRIPLE_FIRST, TRIPLE_COUNT = 160, 12
PROJ_FIRST, PROJ_COUNT = 172, 4

ROWS = 128
MM_ROWS = 256
SKEW = 2


def mm(left, right):
    return jnp.dot(left, right, preferred_element_type=F32)


def mm_nt(left, right):
    return lax.dot_general(left, right, (((1,), (1,)), ((), ())), preferred_element_type=F32)


def mm_tn(left, right):
    return lax.dot_general(left, right, (((0,), (0,)), ((), ())), preferred_element_type=F32)


def split(value):
    high = value.astype(BF16)
    return high, (value - high.astype(F32)).astype(BF16)


def fold(value):
    return jnp.sum(value.reshape(value.shape[0] // 8, 8, value.shape[1]), axis=0)


def over_rows(value):
    return jnp.sum(value, axis=0, keepdims=True)


def group_mean(value, ones):
    high = value.astype(BF16).astype(F32)
    rest = value - high
    middle = rest.astype(BF16).astype(F32)
    parts = jnp.concatenate([high, middle, rest - middle, jnp.zeros_like(value)], axis=0).astype(BF16)
    sums = mm(parts, ones)
    return (sums[0:8] + sums[8:16] + sums[16:24]) * 0.125


def sigmoid(value):
    return 0.5 + 0.5 * jnp.tanh(0.5 * value)


def group_stats(ref, pixels, ones):
    total = jnp.zeros((8, CH), F32)
    for row in range(0, pixels, ROWS):
        total = total + fold(ref[row : row + ROWS, :])
    own = jnp.broadcast_to(over_rows(total) * (1.0 / pixels), (8, CH))
    mean = group_mean(own, ones)
    total = jnp.zeros((8, CH), F32)
    for row in range(0, pixels, ROWS):
        center = ref[row : row + ROWS, :] - own[0:1]
        total = total + fold(center * center)
    within = jnp.broadcast_to(over_rows(total) * (1.0 / pixels), (8, CH))
    between = own - mean
    spread = group_mean(within + between * between, ones)
    return mean[0:1], lax.rsqrt(spread[0:1] + 1e-06)


def write_shifted(ref, row, value, side):
    count = value.shape[0]
    column = lax.broadcasted_iota(jnp.int32, (count, CH), 0) & (side - 1)
    left = jnp.where(column == 0, 0.0, pltpu.roll(value, 1, 0))
    right = jnp.where(column == side - 1, 0.0, pltpu.roll(value, count - 1, 0))
    at = slice(side + row, side + row + count)
    ref[at, 0:CH] = left.astype(BF16)
    ref[at, CH : 2 * CH] = value.astype(BF16)
    ref[at, 2 * CH : 3 * CH] = right.astype(BF16)


def clear_ends(ref, side):
    pixels = side * side
    zeros = jnp.zeros((side, 3 * CH), BF16)
    ref[0:side, :] = zeros
    ref[side + pixels : 2 * side + pixels, :] = zeros


def tap_shifts(side):
    pixels = side * side
    place = lax.broadcasted_iota(jnp.int32, (8, pixels), 1)
    x = place & (side - 1)
    y = place >> (side.bit_length() - 1)
    taps = []
    for dy in (-1, 0, 1):
        for dx in (-1, 0, 1):
            inside = (x + dx >= 0) & (x + dx < side) & (y + dy >= 0) & (y + dy < side)
            taps.append((dy * side + dx, inside))
    return taps


class Shared:
    pass


class Job:
    def __init__(self, image, local, clean, noise, mask, side, refs):
        self.image, self.local, self.clean, self.noise, self.mask, self.side = image, local, clean, noise, mask, side
        self.pixels = side * side
        self.rows = min(ROWS, self.pixels)
        self.mrows = min(MM_ROWS, self.pixels)
        (
            self.hid,
            self.first,
            self.pat,
            self.gpat,
            self.grad_t,
            self.expo,
            self.dscore,
            self.keep,
            self.value_t,
            self.key_t,
            self.normed,
            self.mixed,
            self.mixed_t,
            self.rinv,
            self.act_hi,
            self.act_lo,
            self.dhid,
            self.dact,
            self.dtri,
            self.x80,
            self.scaled,
            self.dnext,
        ) = refs
        self.stats = {}
        self.outs = [None, None]
        self.noisy = [None, None]

    def chunks(self):
        return [slice(row, row + self.rows) for row in range(0, self.pixels, self.rows)]

    def blocks(self):
        return [slice(row, row + self.mrows) for row in range(0, self.pixels, self.mrows)]

    def hid_of(self, which, level):
        return self.hid.at[level] if which else self.dhid

    def first_of(self, which, number):
        return self.first.at[number] if which else self.dact

    def pat_of(self, which, number):
        return self.pat.at[number] if which else self.gpat

    def keep_of(self, which, part):
        return self.keep.at[part] if which else self.dtri.at[part]

    def expo_of(self, which):
        return self.expo if which else self.dscore

    def value_t_of(self, which):
        return self.value_t if which else self.grad_t.at[0]


def job_scratch(side):
    pixels = side * side
    tall = pixels + 2 * side
    return [
        pltpu.VMEM((4, pixels, CH), F32),
        pltpu.VMEM((2, pixels, CH), F32),
        pltpu.VMEM((4, tall, 3 * CH), BF16),
        pltpu.VMEM((tall, 3 * CH), BF16),
        pltpu.VMEM((3, CH, pixels), BF16),
        pltpu.VMEM((pixels, pixels), BF16),
        pltpu.VMEM((pixels, pixels), BF16),
        pltpu.VMEM((3, pixels, CH), BF16),
        pltpu.VMEM((CH, pixels), BF16),
        pltpu.VMEM((CH, pixels), BF16),
        pltpu.VMEM((pixels, CH), BF16),
        pltpu.VMEM((pixels, CH), BF16),
        pltpu.VMEM((CH, pixels), F32),
        pltpu.VMEM((8, pixels), F32),
        pltpu.VMEM((pixels, CH), BF16),
        pltpu.VMEM((pixels, CH), BF16),
        pltpu.VMEM((pixels, CH), F32),
        pltpu.VMEM((pixels, CH), F32),
        pltpu.VMEM((3, pixels, CH), BF16),
        pltpu.VMEM((160, pixels), BF16),
        pltpu.VMEM((pixels, CH), BF16),
        pltpu.VMEM((pixels, CH), F32),
    ]


JOB_REFS = 22


def forward_pass(job, which, net):
    vec, side, pixels = net.vec, job.side, job.pixels
    taps = tap_shifts(side)

    def scal(item):
        return net.scal(job, which, item)

    at = pl.ds(job.local, 1)
    noisy = [job.clean[channel, at, :] + scal(0) * job.noise[channel, at, :] for channel in range(3)]
    noisy = jnp.concatenate(noisy + [jnp.zeros((5, pixels), F32)], axis=0)
    job.noisy[which] = noisy
    scaled = noisy * scal(1)
    parts = [jnp.where(inside, pltpu.roll(scaled, (-shift) % pixels, 1), 0.0) for shift, inside in taps]
    parts.append(jnp.where(lax.broadcasted_iota(jnp.int32, (8, pixels), 0) == 0, 1.0, 0.0))
    high, low = split(jnp.concatenate(parts, axis=0))
    if which:
        job.x80[0:80, :] = high
        job.x80[80:160, :] = low
        for k in range(4):
            clear_ends(job.pat.at[k], side)
    else:
        clear_ends(job.gpat, side)
    job.hid_of(which, 0)[...] = mm_tn(jnp.concatenate([high, high, low], axis=0), net.vin3)
    yield

    def act_conv(key, src, gain, bias, dst, number, use):
        mean, rstd = group_stats(src, pixels, net.ones)
        job.stats[which, key] = (mean, rstd)
        scale = rstd * gain
        yield
        chunks = job.chunks()

        def put(until):
            while chunks and chunks[0].start < until:
                at = chunks.pop(0)
                z = (src[at, :] - mean) * scale + bias
                write_shifted(dst, at.start, z * sigmoid(z), side)

        put(job.mrows + side)
        net.ready(number)
        for at in job.blocks():
            put(at.stop + side)
            use(at, conv(dst, number, at.start))
            yield

    def conv(src, number, row):
        total = None
        for dy in range(3):
            start = dy * side + row
            part = mm(src[start : start + job.mrows, :], net.conv_w[number, dy * 768 : (dy + 1) * 768, :])
            total = part if total is None else total + part
        return total

    for number in range(2):
        base = 28 + 6 * number
        hid = job.hid_of(which, number)
        after = job.hid_of(which, number + 1)
        first = job.first_of(which, number)

        def use_first(at, value):
            first[at, :] = value + vec(base + 2)

        def use_second(at, value):
            after[at, :] = (hid[at, :] + (value + vec(base + 5))) * ROOT_HALF

        yield from act_conv(
            ("a", number), hid, vec(base), vec(base + 1), job.pat_of(which, 2 * number), 2 * number, use_first
        )
        gain_t, bias_t = net.shifts(job, which, number)
        yield from act_conv(
            ("b", number),
            first,
            1.0 + gain_t + vec(base + 3),
            bias_t + vec(base + 4),
            job.pat_of(which, 2 * number + 1),
            2 * number + 1,
            use_second,
        )

    net.ready("attention")
    src = job.hid_of(which, 2)
    mean, rstd = group_stats(src, pixels, net.ones)
    job.stats[which, "n"] = (mean, rstd)
    scale = rstd * vec(40)
    query, key, value_of = (job.keep_of(which, part) for part in range(3))
    value_t = job.value_t_of(which)
    for at in job.blocks():
        normed = ((src[at, :] - mean) * scale + vec(41)).astype(BF16)
        if which:
            job.normed[at, :] = normed
        triple = mm(normed, net.triple_w[...])
        query[at, :] = ((triple[:, 0:CH] + vec(42)) * (1.0 / math.sqrt(CH))).astype(BF16)
        key[at, :] = triple[:, CH : 2 * CH].astype(BF16)
        value = triple[:, 2 * CH :] + vec(43)
        value_of[at, :] = value.astype(BF16)
        value_t[:, at] = jnp.transpose(value).astype(BF16)
        if which:
            job.key_t[:, at] = (jnp.transpose(triple[:, CH : 2 * CH]) * (1.0 / math.sqrt(CH))).astype(BF16)
        yield
    expo = job.expo_of(which)
    scores = job.dnext if which else job.dact
    after = job.hid_of(which, 3)

    def mix(at, rinv):
        mixed_t = mm(value_t[...], expo[:, at]) * rinv
        mixed = jnp.transpose(mixed_t).astype(BF16)
        if which:
            job.rinv[:, at] = jnp.broadcast_to(rinv, (8, job.mrows))
            job.mixed_t[:, at] = mixed_t
            job.mixed[at, :] = mixed
        after[at, :] = (src[at, :] + (mm(mixed, net.proj_w[...]) + vec(44))) * ROOT_HALF

    before = None
    for at in job.blocks():
        scores[...] = mm_nt(key[...], query[at, :])
        if before is not None:
            mix(*before)
        yield
        top = jnp.max(scores[...], axis=0, keepdims=True)
        total = jnp.zeros((8, job.mrows), F32)
        for keys in job.chunks():
            weight = jnp.exp(scores[keys, :] - top)
            total = total + fold(weight)
            expo[keys, at] = weight.astype(BF16)
        before = (at, 1.0 / over_rows(total))
        yield
    mix(*before)
    yield
    mean, rstd = group_stats(after, pixels, net.ones)
    job.stats[which, "h"] = (mean, rstd)
    scale = rstd * vec(45)
    yield
    wide = []
    for at in job.blocks():
        z = (after[at, :] - mean) * scale + vec(46)
        high, low = split(z * sigmoid(z))
        if which:
            job.act_hi[at, :] = high
            job.act_lo[at, :] = low
        part = mm_nt(net.head2, high)
        wide.append(part[0:80] + part[80:160] + mm_nt(net.head_hi, low))
    wide = jnp.concatenate(wide, axis=1)
    out = jnp.zeros((8, pixels), F32)
    for k, (shift, inside) in enumerate(taps):
        out = out + jnp.where(inside, pltpu.roll(wide[8 * k : 8 * k + 8], (-shift) % pixels, 1), 0.0)
    job.outs[which] = scal(2) * noisy + scal(3) * out
    yield


def backward_pass(job, net, finish):
    vec, side, pixels = net.vec, job.side, job.pixels
    taps = tap_shifts(side)
    dact, dhid, gpat, grad_t = job.dact, job.dhid, job.gpat, job.grad_t

    def add_vec(row, value):
        net.gvec[row : row + 1, :] += value

    diff = job.outs[1] - job.outs[0]
    weighted = diff if job.mask is None else diff * job.mask[pl.ds(job.local, 1), :].astype(F32)
    bound = HUBER * math.sqrt(3 * pixels)
    total = jnp.sum(jnp.sum(weighted * diff, axis=1, keepdims=True), axis=0, keepdims=True)
    root = jnp.sqrt(total + bound * bound)
    rate = net.scal(job, 0, 4)
    net.loss[...] += jnp.broadcast_to((root - bound) * rate, (8, CH))
    dout = weighted * ((rate * net.scal(job, 1, 3)) / root)

    parts = [pltpu.roll(jnp.where(inside, dout, 0.0), shift % pixels, 1) for shift, inside in taps]
    parts.append(jnp.zeros((8, pixels), F32))
    high, low = split(jnp.concatenate(parts, axis=0))
    three = jnp.concatenate([high, high, low], axis=0)
    dact[...] = mm_tn(three, net.head3)
    wide = mm(jnp.concatenate([high, low], axis=0), job.act_hi[...])
    net.ghead[...] += wide[0:80] + wide[80:160] + mm(high, job.act_lo[...])
    yield

    def act_sums(key, src, gain, bias, active, beside=()):
        mean, rstd = job.stats[1, key]
        beside = list(beside)
        sum_b = jnp.zeros((8, CH), F32)
        sum_g = jnp.zeros((8, CH), F32)
        for index, at in enumerate(job.chunks()):
            value = (src[at, :] - mean) * rstd
            grad = dact[at, :]
            if active:
                z = value * gain + bias
                sig = sigmoid(z)
                grad = grad * (sig * (1.0 + z * (1.0 - sig)))
                dact[at, :] = grad
            sum_b = sum_b + fold(grad)
            sum_g = sum_g + fold(grad * value)
            if index % 3 == 2 and beside:
                beside.pop(0)()
        for more in beside:
            more()
        sum_b = over_rows(sum_b)
        sum_g = over_rows(sum_g)
        both = jnp.concatenate([sum_b * gain, sum_g * gain, jnp.zeros((6, CH), F32)], axis=0)
        means = group_mean(both, net.ones) * (1.0 / pixels)
        of_grad = rstd * gain
        of_value = rstd * rstd * means[1:2]
        constant = rstd * means[0:1]

        def final(at):
            return of_grad * dact[at, :] - (src[at, :] - mean) * of_value - constant

        return sum_b, sum_g, final

    sum_b, sum_g, final = act_sums("h", job.hid.at[3], vec(45), vec(46), True)
    add_vec(45, sum_g)
    add_vec(46, sum_b)
    yield
    total = jnp.zeros((8, CH), F32)
    for at in job.chunks():
        grad = final(at) * ROOT_HALF
        dhid[at, :] = grad
        total = total + fold(grad)
        gpat[at, 0:CH] = grad.astype(BF16)
        grad_t[0, :, at] = jnp.transpose(grad).astype(BF16)
    add_vec(44, over_rows(total))
    yield

    def wgrad(key, acc, at, value, last):
        if key in net.begun:
            value = value + acc[at]
        net.begun.add(key)
        if finish:
            last(value)
        else:
            acc[at] = value

    wgrad("proj", net.proj_g, (slice(None), slice(None)), mm(grad_t[0], job.mixed[...]), net.put_proj)
    total = jnp.zeros((8, CH), F32)
    query, key, value_of = (job.keep.at[part] for part in range(3))
    for at in job.blocks():
        out_t = mm_nt(net.proj_w[...], gpat[at, 0:CH])
        low_t = out_t.astype(BF16)
        inner = jnp.sum(low_t.astype(F32) * job.mixed_t[:, at], axis=0, keepdims=True)
        rinv = job.rinv[0:1, at]
        job.scaled[at, :] = jnp.transpose(out_t * rinv).astype(BF16)
        grad = mm(value_of[...], low_t)
        job.dscore[:, at] = (job.expo[:, at].astype(F32) * ((grad - inner) * rinv)).astype(BF16)
        dq_t = mm(job.key_t[...], job.dscore[:, at])
        dq = jnp.transpose(dq_t)
        total = total + fold(dq)
        job.dtri[0, at, :] = dq.astype(BF16)
        grad_t[0, :, at] = dq_t.astype(BF16)
        yield
    if finish:
        net.send("proj")
    add_vec(42, over_rows(total))
    total = jnp.zeros((8, CH), F32)
    for at in job.blocks():
        dk = mm(job.dscore[at, :], query[...])
        dv = mm(job.expo[at, :], job.scaled[...])
        total = total + fold(dv)
        job.dtri[1, at, :] = dk.astype(BF16)
        job.dtri[2, at, :] = dv.astype(BF16)
        grad_t[1, :, at] = jnp.transpose(dk).astype(BF16)
        grad_t[2, :, at] = jnp.transpose(dv).astype(BF16)
    add_vec(43, over_rows(total))
    yield
    for at in job.blocks():
        grad = None
        for part in range(3):
            more = mm_nt(job.dtri[part, at, :], net.triple_w[:, part * CH : (part + 1) * CH])
            grad = more if grad is None else grad + more
        dact[at, :] = grad
    for part in range(3):
        wgrad(
            ("triple", part),
            net.triple_g,
            (slice(part * CH, (part + 1) * CH), slice(None)),
            mm(grad_t[part], job.normed[...]),
            partial(net.put_triple, part),
        )
    if finish:
        net.send("triple")
    yield
    clear_ends(gpat, side)
    sum_b, sum_g, final = act_sums("n", job.hid.at[2], vec(40), vec(41), False)
    add_vec(40, sum_g)
    add_vec(41, sum_b)
    yield

    def conv_in(number, chunk_grad, slot):
        chunks = job.chunks()
        sums = [jnp.zeros((8, CH), F32)]

        def put(until):
            while chunks and chunks[0].start < until:
                at = chunks.pop(0)
                grad = chunk_grad(at)
                sums[0] = sums[0] + fold(grad)
                write_shifted(gpat, at.start, grad, side)
                grad_t[slot, :, at] = jnp.transpose(grad).astype(BF16)

        results = []
        for at in job.blocks():
            put(at.stop + side + job.rows)
            total = None
            for dy in range(3):
                for dx in range(3):
                    tap = dy * 3 + dx
                    start = (2 - dy) * side + at.start
                    part = mm_nt(
                        gpat[start : start + job.mrows, (2 - dx) * CH : (3 - dx) * CH],
                        net.conv_w[number, tap * CH : (tap + 1) * CH, :],
                    )
                    total = part if total is None else total + part
            job.dnext[at, :] = total
            yield
        sums_of[0] = over_rows(sums[0])

    sums_of = [None]

    def conv_matrix(number, slot):
        def one(dy):
            wgrad(
                (number, dy),
                net.conv_g,
                (number, slice(None), slice(dy * 768, (dy + 1) * 768)),
                mm(grad_t[slot], job.pat[number, dy * side : dy * side + pixels, :]),
                partial(net.put_conv, number, dy),
            )

        return [partial(one, dy) for dy in range(3)]

    for number in (1, 0):
        base = 28 + 6 * number

        def grad_second(at, final=final):
            grad = (dhid[at, :] + final(at)) * ROOT_HALF
            dhid[at, :] = grad
            return grad

        yield from conv_in(2 * number + 1, grad_second, 0)
        add_vec(base + 5, sums_of[0])
        dact, job.dnext = job.dnext, dact
        gain_t, bias_t = net.shifts(job, 1, number)
        sum_b, sum_g, final = act_sums(
            ("b", number),
            job.first.at[number],
            1.0 + gain_t + vec(base + 3),
            bias_t + vec(base + 4),
            True,
            conv_matrix(2 * number + 1, 0),
        )
        if finish:
            net.send(2 * number + 1)
        add_vec(base + 3, sum_g)
        add_vec(base + 4, sum_b)
        net.gtime[number, job.image : job.image + 1, 0:CH] = sum_g
        net.gtime[number, job.image : job.image + 1, CH:] = sum_b
        yield
        yield from conv_in(2 * number, final, 1)
        add_vec(base + 2, sums_of[0])
        dact, job.dnext = job.dnext, dact
        sum_b, sum_g, final = act_sums(
            ("a", number), job.hid.at[number], vec(base), vec(base + 1), True, conv_matrix(2 * number, 1)
        )
        if finish:
            net.send(2 * number)
        add_vec(base, sum_g)
        add_vec(base + 1, sum_b)
        yield

    total = jnp.zeros((80, CH), F32)
    for at in job.blocks():
        high, low = split(dhid[at, :] + final(at))
        wide = mm(job.x80[:, at], high)
        total = total + wide[0:80] + wide[80:160] + mm(job.x80[0:80, at], low)
    net.gin[...] += total
    yield


def together(passes):
    passes = list(passes)
    while passes:
        for one in list(passes):
            try:
                next(one)
            except StopIteration:
                passes.remove(one)


def later(one, steps):
    for _ in range(steps):
        yield
    yield from one


def net_kernel(
    owner_ref,
    number_ref,
    big_level_ref,
    small_level_ref,
    table_ref,
    big_ref,
    big_noise_ref,
    small_ref,
    small_noise_ref,
    mask_ref,
    vec_ref,
    whole_ref,
    grads_ref,
    conv_w,
    time_w,
    triple_w,
    proj_w,
    conv_g,
    triple_g,
    proj_g,
    tsh,
    gtime,
    gin_ref,
    ghead_ref,
    loss_ref,
    emb_ref,
    vin_ref,
    head_ref,
    gvec_ref,
    piece_ref,
    tile_ref,
    piece_low,
    load_sem,
    store_sem,
    piece_sem,
    *job_refs,
):
    bigs = big_ref.shape[1] // 2
    smalls = small_ref.shape[1] // 2
    count = bigs + smalls
    pair = lax.axis_index("pair")
    devices, shard_rows = grads_ref.shape[0], grads_ref.shape[1]
    per_device = shard_rows // BLOCK

    parts = {}
    for number in range(2):
        parts["time", number] = [
            (TIME_FIRST + TIME_COUNT * number + k, time_w.at[number], k // 4, k % 4) for k in range(TIME_COUNT)
        ]
    for m in range(4):
        parts[m] = [(m * CONV_BLOCKS + k, conv_w.at[m], k // 2, k % 2) for k in range(CONV_BLOCKS)]
    parts["triple"] = [(TRIPLE_FIRST + k, triple_w, k // 6, k % 6) for k in range(TRIPLE_COUNT)]
    parts["proj"] = [(PROJ_FIRST + k, proj_w, k // 2, k % 2) for k in range(PROJ_COUNT)]
    sem_of = {key: k for k, key in enumerate(parts)}

    def block(ref, i, j):
        return ref.at[i * BLOCK : (i + 1) * BLOCK, j * BLOCK : (j + 1) * BLOCK]

    def load(key):
        for index, ref, i, j in parts[key]:
            pltpu.make_async_copy(whole_ref.at[owner_ref[index]], block(ref, i, j), load_sem.at[sem_of[key]]).start()

    def wait_load(key):
        ref = parts[key][0][1]
        pltpu.make_async_copy(ref, ref, load_sem.at[sem_of[key]]).wait()

    def store(key):
        for index, ref, i, j in parts[key]:
            slot = owner_ref[index]
            home = slot // per_device
            row = pl.multiple_of((slot - home * per_device) * BLOCK, BLOCK)
            target = grads_ref.at[home, pl.ds(row, BLOCK), :]
            pltpu.make_async_copy(block(ref, i, j), target, store_sem.at[sem_of[key]]).start()

    def wait_store(key):
        ref = parts[key][0][1]
        pltpu.make_async_copy(ref, ref, store_sem.at[sem_of[key]]).wait()

    for key in parts:
        load(key)

    gvec_ref[...] = jnp.zeros_like(gvec_ref)
    gin_ref[...] = jnp.zeros_like(gin_ref)
    ghead_ref[...] = jnp.zeros_like(ghead_ref)
    loss_ref[...] = jnp.zeros_like(loss_ref)
    gtime[...] = jnp.zeros_like(gtime)

    vin_ref[...] = jnp.zeros_like(vin_ref)
    head_ref[...] = jnp.zeros_like(head_ref)
    for tap in range(9):
        vin_ref[8 * tap : 8 * tap + 3, :] = vec_ref[3 * tap : 3 * tap + 3, :]
        head_ref[8 * tap : 8 * tap + 3, :] = vec_ref[47 + 3 * tap : 50 + 3 * tap, :]
    vin_ref[72:73, :] = vec_ref[27:28, :]

    levels = [big_level_ref[pair * bigs + k] for k in range(bigs)]
    levels += [small_level_ref[pair * smalls + k] for k in range(smalls)]
    emb_ref[...] = jnp.zeros_like(emb_ref)
    for k in range(count):
        for which in range(2):
            emb_ref[2 * k + which : 2 * k + which + 1, :] = table_ref[pl.ds(levels[k] + which, 1), :]

    net = Shared()
    vin_hi, vin_lo = split(vin_ref[...])
    net.vin3 = jnp.concatenate([vin_hi, vin_lo, vin_hi], axis=0)
    head_hi, head_lo = split(head_ref[...])
    net.head_hi = head_hi
    net.head2 = jnp.concatenate([head_hi, head_lo], axis=0)
    net.head3 = jnp.concatenate([head_hi, head_lo, head_hi], axis=0)
    group_row = lax.broadcasted_iota(jnp.int32, (CH, CH), 0) >> 3
    group_col = lax.broadcasted_iota(jnp.int32, (CH, CH), 1) >> 3
    net.ones = jnp.where(group_row == group_col, 1.0, 0.0).astype(BF16)
    net.conv_w, net.triple_w, net.proj_w = conv_w, triple_w, proj_w
    net.conv_g, net.triple_g, net.proj_g = conv_g, triple_g, proj_g
    net.gvec, net.gin, net.ghead, net.loss, net.gtime = gvec_ref, gin_ref, ghead_ref, loss_ref, gtime
    net.vec = lambda row: vec_ref[row : row + 1, :]
    net.scal = lambda job, which, item: number_ref[(levels[job.image] + which) * 8 + item]

    def shifts(job, which, number):
        row = tsh[number, 2 * job.image + which : 2 * job.image + which + 1, :]
        return row[:, 0:CH], row[:, CH:]

    net.shifts = shifts
    loaded = set()

    def ready(what):
        if what == 0:
            keys = (("time", 0), ("time", 1), 0)
        else:
            keys = ("triple", "proj") if what == "attention" else (what,)
        for key in keys:
            if key not in loaded:
                loaded.add(key)
                wait_load(key)
                if isinstance(key, tuple):
                    tsh[key[1]] = mm(emb_ref[...].astype(BF16), time_w[key[1]])

    net.ready = ready

    def put_conv(number, dy, value):
        for i in range(6):
            row = (dy * 6 + i) * BLOCK
            for j in range(2):
                conv_w[number, row : row + BLOCK, j * BLOCK : (j + 1) * BLOCK] = value[
                    j * BLOCK : (j + 1) * BLOCK, i * BLOCK : (i + 1) * BLOCK
                ].astype(BF16)

    def put_triple(part, value):
        for j in range(2):
            for i in range(2):
                column = part * CH + j * BLOCK
                triple_w[i * BLOCK : (i + 1) * BLOCK, column : column + BLOCK] = value[
                    j * BLOCK : (j + 1) * BLOCK, i * BLOCK : (i + 1) * BLOCK
                ].astype(BF16)

    def put_proj(value):
        net.proj_value = value

    def send(key):
        if key == "proj":
            for i in range(2):
                for j in range(2):
                    proj_w[i * BLOCK : (i + 1) * BLOCK, j * BLOCK : (j + 1) * BLOCK] = net.proj_value[
                        j * BLOCK : (j + 1) * BLOCK, i * BLOCK : (i + 1) * BLOCK
                    ].astype(BF16)
        store(key)

    net.put_conv, net.put_triple, net.put_proj, net.send = put_conv, put_triple, put_proj, send

    big_jobs = [Job(k, pair * bigs + k, big_ref, big_noise_ref, None, SIDE, job_refs[:JOB_REFS]) for k in range(bigs)]
    small_jobs = [
        Job(bigs + k, pair * smalls + k, small_ref, small_noise_ref, mask_ref, SMALL_SIDE, job_refs[JOB_REFS:]) for k in range(smalls)
    ]
    net.begun = set()
    turns = [big_jobs[k : k + 1] + small_jobs[k : k + 1] for k in range(max(bigs, smalls))]
    if len(turns[-1]) > 1:
        turns[-1:] = [turns[-1][1:], turns[-1][:1]]
    for k, jobs in enumerate(turns):
        together(later(forward_pass(job, which, net), SKEW * which + k) for k, job in enumerate(jobs) for which in range(2))
        together(backward_pass(job, net, k == len(turns) - 1) for job in jobs)

    emb = emb_ref[...]
    mine = jnp.concatenate(
        [emb[2 * k + 1 : 2 * k + 2] for k in range(count)] + [jnp.zeros((gtime.shape[1] - count, CH), F32)], axis=0
    ).astype(BF16)
    for number in range(2):
        value = mm_tn(gtime[number].astype(BF16), mine)
        for k in range(TIME_COUNT):
            i, j = k // 4, k % 4
            time_w[number, i * BLOCK : (i + 1) * BLOCK, j * BLOCK : (j + 1) * BLOCK] = value[
                j * BLOCK : (j + 1) * BLOCK, i * BLOCK : (i + 1) * BLOCK
            ].astype(BF16)
        store(("time", number))

    for tap in range(9):
        gvec_ref[3 * tap : 3 * tap + 3, :] = gin_ref[8 * tap : 8 * tap + 3, :]
        gvec_ref[47 + 3 * tap : 50 + 3 * tap, :] = ghead_ref[8 * tap : 8 * tap + 3, :]
    gvec_ref[27:28, :] = gin_ref[72:73, :]
    gvec_ref[74:75, :] = loss_ref[0:1, :]
    piece_ref[...] = jnp.zeros_like(piece_ref)
    tile_ref[0:80, :] = gvec_ref[:, 0:BLOCK]
    tile_ref[80:160, :] = gvec_ref[:, BLOCK:]
    rows = piece_rows(devices)
    for k in range(-(-160 // rows)):
        end = min(160, (k + 1) * rows)
        piece_ref[k, 0 : end - k * rows, :] = tile_ref[k * rows : end, :]
    value = piece_ref[...]
    high = value.astype(BF16).astype(F32)
    piece_low[...] = jnp.concatenate([high, value - high], axis=1).astype(BF16)
    keep = pltpu.make_async_copy(piece_low, grads_ref.at[:, pl.ds(per_device * BLOCK, 16), :], piece_sem)
    keep.start()
    keep.wait()
    for key in parts:
        wait_store(key)


def network_grads(owner_map, numbers, table, big_level, small_level, big, big_noise, small, small_noise, mask, vectors, whole, devices):
    per_device = whole.shape[0] // devices
    images = -(-(big.shape[1] + small.shape[1]) // 16) * 16
    vmem = pl.BlockSpec(memory_space=pltpu.VMEM)
    smem = pl.BlockSpec(memory_space=pltpu.SMEM)
    hbm = pl.BlockSpec(memory_space=ANY)
    return pl.pallas_call(
        net_kernel,
        out_shape=jax.ShapeDtypeStruct((devices, per_device * BLOCK + 16, BLOCK), BF16),
        in_specs=[smem] * 4 + [vmem] * 7 + [hbm],
        out_specs=hbm,
        scratch_shapes=[
            pltpu.VMEM((4, 9 * CH, CH), BF16),
            pltpu.VMEM((2, CH, 2 * CH), BF16),
            pltpu.VMEM((CH, 3 * CH), BF16),
            pltpu.VMEM((CH, CH), BF16),
            pltpu.VMEM((4, CH, 9 * CH), F32),
            pltpu.VMEM((3 * CH, CH), F32),
            pltpu.VMEM((CH, CH), F32),
            pltpu.VMEM((2, images, 2 * CH), F32),
            pltpu.VMEM((2, images, 2 * CH), F32),
            pltpu.VMEM((80, CH), F32),
            pltpu.VMEM((80, CH), F32),
            pltpu.VMEM((8, CH), F32),
            pltpu.VMEM((images, CH), F32),
            pltpu.VMEM((80, CH), F32),
            pltpu.VMEM((80, CH), F32),
            pltpu.VMEM((80, CH), F32),
            pltpu.VMEM((devices, 8, BLOCK), F32),
            pltpu.VMEM((160, BLOCK), F32),
            pltpu.VMEM((devices, 16, BLOCK), BF16),
            pltpu.SemaphoreType.DMA((8,)),
            pltpu.SemaphoreType.DMA((8,)),
            pltpu.SemaphoreType.DMA,
        ]
        + job_scratch(SIDE)
        + job_scratch(SMALL_SIDE),
        compiler_params=pltpu.CompilerParams(vmem_limit_bytes=62 * 1024 * 1024),
        cost_estimate=pl.CostEstimate(flops=57 * 10**9, bytes_accessed=20 * 10**6, transcendentals=10**7),
    )(owner_map, numbers, big_level, small_level, table, big, big_noise, small, small_noise, mask, vectors, whole)


MESH_ID = pl.DeviceIdType.MESH


def where_am_i():
    dp = lax.axis_index("dp")
    return lax.axis_index("pair"), dp // 4, (dp // 2) % 2, dp % 2


def device(pair, line, mid, core):
    return (pair, (line * 2 + mid) * 2 + core)


def neighbours():
    pair, line, mid, core = where_am_i()
    flip_pair, flip_mid = 1 - 2 * pair, 1 - 2 * mid
    second = device(pair + (1 - core) * flip_pair, line, mid + core * flip_mid, core)
    third = device(pair + core * flip_pair, line, mid + (1 - core) * flip_mid, core)
    sibling = device(pair, line, mid, 1 - core)
    at_second = (1 - core) * pair + core * mid
    at_third = core * pair + (1 - core) * mid
    return pair, line, mid, core, at_second, at_third, second, third, sibling


def greet(lines, devices, lower, upper, line):
    barrier = pltpu.get_barrier_semaphore()
    for other in devices:
        pl.semaphore_signal(barrier, inc=1, device_id=other, device_id_type=MESH_ID)
    for there, other in ((lower >= 0, lower), (upper < lines, upper)):

        @pl.when(there)
        def _(other=other):
            pl.semaphore_signal(barrier, inc=1, device_id=line(other), device_id_type=MESH_ID)

    beside = jnp.where(lower >= 0, 1, 0) + jnp.where(upper < lines, 1, 0)
    pl.semaphore_wait(barrier, len(devices) + beside)


def gather_kernel(
    lines, blocks_ref, whole_ref, own, up_send, down_send, second_send, third_send, sib_send, line_recv, second_recv, third_recv, sib_recv, own_sem
):
    pair, line, mid, core, at_second, at_third, second, third, sibling = neighbours()
    count = blocks_ref.shape[0]
    group = 4 * lines
    upper = device(pair, (line + 1) % lines, mid, core)
    lower = device(pair, (line + lines - 1) % lines, mid, core)

    def place(l, s, t, c):
        p = (1 - c) * s + c * t
        m = c * s + (1 - c) * t
        return whole_ref.at[pl.ds((p * group + (l * 2 + m) * 2 + c) * count, count)]

    def copy(source, target, send, recv, to):
        return pltpu.make_async_remote_copy(
            src_ref=source, dst_ref=target, send_sem=send, recv_sem=recv, device_id=to, device_id_type=MESH_ID
        )

    def to_sibling(l, s, t, source=None):
        where = place(l, s, t, core)
        p = (1 - core) * s + core * t
        m = core * s + (1 - core) * t
        index = l * 4 + p * 2 + m
        return copy(where if source is None else source, where, sib_send.at[index], sib_recv.at[index], sibling)

    def to_second(l, source=None):
        where = place(l, at_second, at_third, core)
        return copy(where if source is None else source, where, second_send.at[l], second_recv.at[l], second)

    def to_third(l, s, source=None):
        where = place(l, s, at_third, core)
        index = l * 2 + s
        return copy(where if source is None else source, where, third_send.at[index], third_recv.at[index], third)

    def to_upper(l, source=None):
        where = place(l, at_second, at_third, core)
        return copy(where if source is None else source, where, up_send.at[l], line_recv.at[l], upper)

    def to_lower(l, source=None):
        where = place(l, at_second, at_third, core)
        return copy(where if source is None else source, where, down_send.at[l], line_recv.at[l], lower)

    own[...] = blocks_ref[...].astype(BF16)
    greet(lines, (second, third, sibling), line - 1, line + 1, lambda l: device(pair, l, mid, core))

    @pl.when(line < lines - 1)
    def _():
        to_upper(line, own).start()

    @pl.when(line > 0)
    def _():
        to_lower(line, own).start()

    to_third(line, at_second, own).start()
    to_second(line, own).start()
    to_sibling(line, at_second, at_third, own).start()
    keep = pltpu.make_async_copy(own, place(line, at_second, at_third, core), own_sem)
    keep.start()

    def from_second(l):
        to_second(l).wait_recv()
        to_third(l, 1 - at_second).start()
        to_sibling(l, 1 - at_second, at_third).start()

    def from_line(l):
        to_upper(l).wait_recv()

        @pl.when((l < line) & (line < lines - 1))
        def _():
            to_upper(l).start()

        @pl.when((l > line) & (line > 0))
        def _():
            to_lower(l).start()

        to_second(l).start()
        to_third(l, at_second).start()
        to_sibling(l, at_second, at_third).start()

    def both(distance, carry):
        @pl.when(line - distance >= 0)
        def _():
            from_line(line - distance)

        @pl.when(line + distance < lines)
        def _():
            from_line(line + distance)

        @pl.when(line - distance + 1 >= 0)
        def _():
            from_second(line - distance + 1)

        @pl.when((line + distance - 1 < lines) & (distance > 1))
        def _():
            from_second(line + distance - 1)

        return carry

    lax.fori_loop(1, lines + 1, both, 0)

    def from_third(l, carry):
        for s in range(2):
            to_third(l, s).wait_recv()
            to_sibling(l, s, 1 - at_third).start()
        return carry

    lax.fori_loop(0, lines, from_third, 0)

    def finish(l, carry):
        @pl.when((l <= line) & (line < lines - 1))
        def _():
            to_upper(l).wait_send()

        @pl.when((l >= line) & (line > 0))
        def _():
            to_lower(l).wait_send()

        to_second(l).wait_send()
        for s in range(2):
            to_third(l, s).wait_send()
            for t in range(2):
                done = to_sibling(l, s, t)
                done.wait_send()
                done.wait_recv()
        return carry

    lax.fori_loop(0, lines, finish, 0)
    keep.wait()


def gather_blocks(blocks):
    lines = lax.axis_size("dp") // 4
    count = blocks.shape[0]
    total = count * lines * 8
    dma = pltpu.SemaphoreType.DMA
    return pl.pallas_call(
        partial(gather_kernel, lines),
        out_shape=jax.ShapeDtypeStruct((total, BLOCK, BLOCK), BF16),
        in_specs=[pl.BlockSpec(memory_space=pltpu.VMEM)],
        out_specs=pl.BlockSpec(memory_space=ANY),
        scratch_shapes=[
            pltpu.VMEM((count, BLOCK, BLOCK), BF16),
            dma((lines,)),
            dma((lines,)),
            dma((lines,)),
            dma((2 * lines,)),
            dma((4 * lines,)),
            dma((lines,)),
            dma((lines,)),
            dma((2 * lines,)),
            dma((4 * lines,)),
            dma,
        ],
        compiler_params=pltpu.CompilerParams(collective_id=0, has_side_effects=True),
        cost_estimate=pl.CostEstimate(flops=0, bytes_accessed=2 * total * BLOCK * BLOCK * 2, transcendentals=0),
    )(blocks)


def sum_kernel(
    lines,
    grads_ref,
    owner_ref,
    sum_ref,
    tiles_ref,
    mine,
    from_sib,
    from_third,
    from_second,
    from_lower,
    from_upper,
    tiles,
    load_sem,
    sib_send,
    third_send,
    second_send,
    up_send,
    down_send,
    sib_recv,
    third_recv,
    second_recv,
    up_recv,
    down_recv,
    near_send,
    near_recv,
    far_send,
    far_recv,
):
    pair, line, mid, core, at_second, at_third, second, third, sibling = neighbours()
    count = sum_ref.shape[0]
    main = count * BLOCK
    group = 4 * lines
    upper = device(pair, (line + 1) % lines, mid, core)
    lower = device(pair, (line + lines - 1) % lines, mid, core)
    here = pair * 4 + mid * 2 + core

    def peer(k):
        return device(k // 4, line, (k // 2) % 2, k % 2)

    def on_line(l):
        return device(pair, l, mid, core)

    def copy(source, target, send, recv, to):
        return pltpu.make_async_remote_copy(
            src_ref=source, dst_ref=target, send_sem=send, recv_sem=recv, device_id=to, device_id_type=MESH_ID
        )

    def spot(l, s, t):
        return l * 4 + s * 2 + t

    def shard(l, s, t, c):
        p = (1 - c) * s + c * t
        m = c * s + (1 - c) * t
        return p * group + (l * 2 + m) * 2 + c

    def to_sibling(l, s, t):
        index = spot(l, s, t)
        return copy(grads_ref.at[shard(l, s, t, 1 - core)], from_sib.at[index], sib_send.at[index], sib_recv.at[index], sibling)

    def load(l, s, t):
        index = spot(l, s, t)
        return pltpu.make_async_copy(grads_ref.at[shard(l, s, t, core)], mine.at[index], load_sem.at[index])

    def to_third(l, s):
        index = l * 2 + s
        return copy(mine.at[spot(l, s, 1 - at_third)], from_third.at[index], third_send.at[index], third_recv.at[index], third)

    def to_second(l):
        return copy(mine.at[spot(l, 1 - at_second, at_third)], from_second.at[l], second_send.at[l], second_recv.at[l], second)

    def to_upper(l):
        return copy(mine.at[spot(l, at_second, at_third)], from_lower.at[l], up_send.at[l], up_recv.at[l], upper)

    def to_lower(l):
        return copy(mine.at[spot(l, at_second, at_third)], from_upper.at[l], down_send.at[l], down_recv.at[l], lower)

    barrier = pltpu.get_barrier_semaphore()
    for k in range(8):

        @pl.when(here != k)
        def _(k=k):
            pl.semaphore_signal(barrier, inc=1, device_id=peer(k), device_id_type=MESH_ID)

    def greet_line(l, carry):
        @pl.when(l != line)
        def _():
            pl.semaphore_signal(barrier, inc=1, device_id=on_line(l), device_id_type=MESH_ID)

        return carry

    lax.fori_loop(0, lines, greet_line, 0)
    pl.semaphore_wait(barrier, 7 + lines - 1)

    def far_first(function):
        def step(k, carry):
            distance = lines - 1 - k

            @pl.when(line + distance < lines)
            def _():
                function(line + distance)

            @pl.when((line - distance >= 0) & (distance > 0))
            def _():
                function(line - distance)

            return carry

        lax.fori_loop(0, lines, step, 0)

    def start_both(l, places):
        s_at, t_at, s_own, t_own = places
        to_sibling(l, s_at, t_at).start()
        load(l, s_own, t_own).start()

    sib_second, sib_third = at_third, at_second
    for s, t in ((1, 1), (0, 1), (1, 0), (0, 0)):
        places = (
            sib_second + s * (1 - 2 * sib_second),
            sib_third + t * (1 - 2 * sib_third),
            at_second + s * (1 - 2 * at_second),
            at_third + t * (1 - 2 * at_third),
        )
        far_first(partial(start_both, places=places))

    def read(ref, index):
        tile = ref[index, main:, :].astype(F32)
        return ref[index, 0:main, :].astype(F32), tile[0:8] + tile[8:16]

    def add(value, ref, index):
        other = read(ref, index)
        return value[0] + other[0], value[1] + other[1]

    def write(index, value):
        high = value[1].astype(BF16).astype(F32)
        mine[index, 0:main, :] = value[0].astype(BF16)
        mine[index, main:, :] = jnp.concatenate([high, value[1] - high], axis=0).astype(BF16)

    def both_cores(l, s, t):
        load(l, s, t).wait()
        to_sibling(l, s, t).wait_recv()
        index = spot(l, s, t)
        return add(read(mine, index), from_sib, index)

    def send_third(l, s):
        write(spot(l, s, 1 - at_third), both_cores(l, s, 1 - at_third))
        to_third(l, s).start()

    far_first(lambda l: send_third(l, 1 - at_second))
    far_first(lambda l: send_third(l, at_second))

    def with_third(l, s):
        total = both_cores(l, s, at_third)
        to_third(l, s).wait_recv()
        return add(total, from_third, l * 2 + s)

    def send_second(l):
        write(spot(l, 1 - at_second, at_third), with_third(l, 1 - at_second))
        to_second(l).start()

    far_first(send_second)

    def with_second(l):
        total = with_third(l, at_second)
        to_second(l).wait_recv()
        return add(total, from_second, l)

    def send_line(k, carry):
        distance = lines - 1 - k
        above = line + distance
        below = line - distance

        @pl.when(above < lines)
        def _():
            index = spot(above, at_second, at_third)
            write(index, with_second(above))

            @pl.when(line > 0)
            def _():
                to_upper(above).wait_recv()
                write(index, add(read(mine, index), from_lower, above))

            to_upper(above).start()

        @pl.when(below >= 0)
        def _():
            index = spot(below, at_second, at_third)
            write(index, with_second(below))

            @pl.when(line < lines - 1)
            def _():
                to_lower(below).wait_recv()
                write(index, add(read(mine, index), from_upper, below))

            to_lower(below).start()

        return carry

    lax.fori_loop(0, lines - 1, send_line, 0)
    blocks, piece = with_second(line)
    sum_ref[...] = blocks.reshape(count, BLOCK, BLOCK)
    tiles[line, here] = piece

    def last(ref):
        more, piece = read(ref, line)
        sum_ref[...] += more.reshape(count, BLOCK, BLOCK)
        tiles[line, here] += piece

    @pl.when(line > 0)
    def _():
        to_upper(line).wait_recv()
        last(from_lower)

    @pl.when(line < lines - 1)
    def _():
        to_lower(line).wait_recv()
        last(from_upper)

    square = jnp.zeros((8, BLOCK), F32)
    for k in range(count):
        slot = (pair * group + (line * 2 + mid) * 2 + core) * count + k
        held = jnp.max(jnp.where(owner_ref[...] == slot, 1.0, 0.0), axis=1, keepdims=True)
        value = jnp.where(held > 0.0, sum_ref[k], 0.0)
        sum_ref[k] = value
        square = square + fold(value * value)
    at_last = lax.broadcasted_iota(jnp.int32, (8, BLOCK), 0) == 7
    tiles[line, here] = jnp.where(at_last, over_rows(square), tiles[line, here])

    def near(k):
        tile = tiles.at[line, here]
        return copy(tile, tile, near_send.at[k], near_recv.at[here], peer(k))

    def near_from(k):
        tile = tiles.at[line, k]
        return copy(tile, tile, near_send.at[k], near_recv.at[k], peer(k))

    def far(l):
        return copy(tiles.at[line], tiles.at[line], far_send.at[l], far_recv.at[line], on_line(l))

    def far_from(l):
        return copy(tiles.at[l], tiles.at[l], far_send.at[l], far_recv.at[l], on_line(l))

    def others(function):
        for k in range(8):

            @pl.when(here != k)
            def _(k=k):
                function(k)

    def other_lines(function):
        def step(l, carry):
            @pl.when(l != line)
            def _():
                function(l)

            return carry

        lax.fori_loop(0, lines, step, 0)

    others(lambda k: near(k).start())
    others(lambda k: near_from(k).wait_recv())
    other_lines(lambda l: far(l).start())

    def finish(l, carry):
        for s in range(2):
            for t in range(2):
                to_sibling(l, s, t).wait_send()
            to_third(l, s).wait_send()
        to_second(l).wait_send()

        @pl.when((l > line) & (line < lines - 1))
        def _():
            to_upper(l).wait_send()

        @pl.when((l < line) & (line > 0))
        def _():
            to_lower(l).wait_send()

        return carry

    lax.fori_loop(0, lines, finish, 0)
    others(lambda k: near(k).wait_send())
    other_lines(lambda l: far_from(l).wait_recv())
    other_lines(lambda l: far(l).wait_send())
    tiles_ref[...] = tiles[...]


def sum_by_slot(grads, owner_map):
    lines = lax.axis_size("dp") // 4
    rows = grads.shape[1]
    count = rows // BLOCK
    dma = pltpu.SemaphoreType.DMA
    vmem = pl.BlockSpec(memory_space=pltpu.VMEM)
    shard = (rows, BLOCK)
    return pl.pallas_call(
        partial(sum_kernel, lines),
        out_shape=(
            jax.ShapeDtypeStruct((count, BLOCK, BLOCK), F32),
            jax.ShapeDtypeStruct((lines, 8, 8, BLOCK), F32),
        ),
        in_specs=[pl.BlockSpec(memory_space=ANY), vmem],
        out_specs=(vmem, vmem),
        scratch_shapes=[
            pltpu.VMEM((4 * lines,) + shard, BF16),
            pltpu.VMEM((4 * lines,) + shard, BF16),
            pltpu.VMEM((2 * lines,) + shard, BF16),
            pltpu.VMEM((lines,) + shard, BF16),
            pltpu.VMEM((lines,) + shard, BF16),
            pltpu.VMEM((lines,) + shard, BF16),
            pltpu.VMEM((lines, 8, 8, BLOCK), F32),
            dma((4 * lines,)),
            dma((4 * lines,)),
            dma((2 * lines,)),
            dma((lines,)),
            dma((lines,)),
            dma((lines,)),
            dma((4 * lines,)),
            dma((2 * lines,)),
            dma((lines,)),
            dma((lines,)),
            dma((lines,)),
            dma((8,)),
            dma((8,)),
            dma((lines,)),
            dma((lines,)),
        ],
        compiler_params=pltpu.CompilerParams(collective_id=1, has_side_effects=True, vmem_limit_bytes=48 * 1024 * 1024),
        cost_estimate=pl.CostEstimate(flops=0, bytes_accessed=2 * grads.size * 2, transcendentals=0),
    )(grads, owner_map.reshape(1, -1))


def mm_split(left, right, over):
    high, low = split(left)
    other_high, other_low = split(right)

    def one(first, second):
        return lax.dot_general(first, second, (over, ((), ())), preferred_element_type=F32)

    return one(high, other_high) + (one(high, other_low) + one(low, other_high))


def update_kernel(
    sum_ref,
    tiles_ref,
    blocks_ref,
    moments_ref,
    left_ref,
    right_ref,
    left_root_ref,
    right_root_ref,
    vec_ref,
    vec_first_ref,
    vec_second_ref,
    scalars_ref,
    new_blocks_ref,
    new_moments_ref,
    new_left_ref,
    new_right_ref,
    new_vec_ref,
    new_first_ref,
    new_second_ref,
    rows_ref,
):
    lines = tiles_ref.shape[0]
    piece = piece_rows(8 * lines)
    for line in range(lines):
        for k in range(8):
            shard = (k // 4) * 4 * lines + (line * 2 + (k // 2) % 2) * 2 + k % 2
            rows_ref[shard * piece : (shard + 1) * piece, :] = tiles_ref[line, k, 0:piece, :]
    count = vec_ref.shape[0]
    grads = jnp.concatenate([rows_ref[0:80, :], rows_ref[80:160, :]], axis=1)
    vec_grad = grads[0:count]
    square = jnp.sum(tiles_ref[...].reshape(64 * lines, BLOCK).reshape(8 * lines, 8, BLOCK)[:, 7, :])
    total = jnp.full((1, 1), square + jnp.sum(vec_grad * vec_grad), F32)
    norm = jnp.sqrt(total)
    lane = lax.broadcasted_iota(jnp.int32, (8, BLOCK), 1)
    scalars_ref[...] = jnp.where(lane == 0, grads[74:75, 0:BLOCK], norm)
    factor = jnp.minimum(1.0, CLIP / (norm + 1e-06))

    for k in range(sum_ref.shape[0]):
        turned_grad = sum_ref[k] * factor
        first = BETA_ONE * moments_ref[k] + (1 - BETA_ONE) * jnp.transpose(turned_grad)
        new_moments_ref[k] = first
        new_left_ref[k] = BETA_TWO * left_ref[k] + (1 - BETA_TWO) * mm_split(turned_grad, turned_grad, ((0,), (0,)))
        new_right_ref[k] = BETA_TWO * right_ref[k] + (1 - BETA_TWO) * mm_split(turned_grad, turned_grad, ((1,), (1,)))
        turned = mm_split(left_root_ref[k], first, ((1,), (0,)))
        turned = mm_split(turned, right_root_ref[k], ((1,), (0,)))
        mean = jnp.sum(over_rows(fold(turned * turned)), axis=1, keepdims=True) * (1.0 / BLOCK**2)
        master = blocks_ref[k]
        new_blocks_ref[k] = master - RATE_MATRIX * (turned * (1.0 / jnp.sqrt(mean + 1e-20)) + DECAY * master)

    grad = vec_grad * factor
    params = vec_ref[...]
    first = BETA_ONE * vec_first_ref[...] + (1 - BETA_ONE) * grad
    second = BETA_TWO * vec_second_ref[...] + (1 - BETA_TWO) * grad * grad
    fixed_first = first * (1.0 / (1 - BETA_ONE**STEP))
    fixed_second = second * (1.0 / (1 - BETA_TWO**STEP))
    new_vec_ref[...] = params - RATE_VECTOR * (fixed_first / (jnp.sqrt(fixed_second) + 1e-08) + DECAY * params)
    new_first_ref[...] = first
    new_second_ref[...] = second


def piece_rows(devices):
    return -(-160 // devices)


def update(summed, tiles, blocks, moments, left_stats, right_stats, left_roots, right_roots, vectors, vec_first, vec_second):
    vmem = pl.BlockSpec(memory_space=pltpu.VMEM)
    devices = 8 * tiles.shape[0]
    like = lambda value: jax.ShapeDtypeStruct(value.shape, F32)
    scalars = jax.ShapeDtypeStruct((8, BLOCK), F32)
    return pl.pallas_call(
        update_kernel,
        out_shape=(scalars,) + (like(blocks),) * 4 + (like(vectors),) * 3,
        in_specs=[vmem] * 11,
        out_specs=(vmem,) * 8,
        scratch_shapes=[pltpu.VMEM((max(160, devices * piece_rows(devices)), BLOCK), F32)],
        compiler_params=pltpu.CompilerParams(vmem_limit_bytes=48 * 1024 * 1024),
        cost_estimate=pl.CostEstimate(flops=10**9, bytes_accessed=6 * 10**6, transcendentals=10**5),
    )(summed, tiles, blocks, moments, left_stats, right_stats, left_roots, right_roots, vectors, vec_first, vec_second)


def sigma_of(level):
    lowest = SIGMA_MIN ** (1.0 / RHO)
    highest = SIGMA_MAX ** (1.0 / RHO)
    return (lowest + level / (NSTEPS - 1) * (highest - lowest)) ** RHO


def level_tables():
    level = np.arange(NSTEPS, dtype=np.float64)
    sigma = sigma_of(level)
    inner = 1.0 / np.sqrt(sigma**2 + SIGMA_DATA**2)
    skip = SIGMA_DATA**2 / ((sigma - SIGMA_MIN) ** 2 + SIGMA_DATA**2)
    outer = (sigma - SIGMA_MIN) * SIGMA_DATA * inner
    rate = 1.0 / (sigma_of(level + 1) - sigma)
    numbers = np.stack([sigma, inner, skip, outer, rate] + [np.zeros_like(sigma)] * 3, axis=1).reshape(-1)
    half = CH // 2
    phase = np.log(sigma)[:, None] / 4.0 * np.exp(np.arange(half) * (math.log(100.0) / (half - 1)))
    embed = np.zeros((16, CH))
    embed[:NSTEPS] = np.concatenate([np.sin(phase), np.cos(phase)], axis=1)
    return numbers.astype(np.float32), embed.astype(np.float32)


def image_rows(big_images, big_noise, small_images, small_noise):
    return tuple(jnp.swapaxes(value, 0, 1) for value in (big_images, big_noise, small_images, small_noise))


def local(
    big_images,
    big_noise,
    small_images,
    small_noise,
    big_level,
    small_level,
    small_mask,
    owner_map,
    blocks,
    moments,
    left_stats,
    right_stats,
    left_roots,
    right_roots,
    vectors,
    vec_first,
    vec_second,
):
    whole = gather_blocks(blocks)
    numbers, table = level_tables()
    grads = network_grads(
        owner_map,
        jnp.asarray(numbers),
        jnp.asarray(table),
        big_level,
        small_level,
        *image_rows(big_images, big_noise, small_images, small_noise),
        small_mask,
        vectors,
        whole,
        lax.axis_size("pair") * lax.axis_size("dp"),
    )
    summed, tiles = sum_by_slot(grads, owner_map)
    scalars, *rest = update(
        summed, tiles, blocks, moments, left_stats, right_stats, left_roots, right_roots, vectors, vec_first, vec_second
    )
    return (scalars[0, 0], scalars[0, 1], *rest)


def solution(mesh):
    by_slot = P(("pair", "dp"), None, None)
    by_image = P("dp", None, None)
    placed = (by_image,) * 4 + (P("dp"), P("dp"), P("dp", None), P()) + (by_slot,) * 6 + (P(),) * 3
    return jax.shard_map(
        local,
        mesh=mesh,
        in_specs=placed,
        out_specs=(P(), P()) + (by_slot,) * 4 + (P(),) * 3,
        check_vma=False,
    )
```
